128 devices in a mesh: fsdp: 32 (over x, y_lo, z), seq: 4 (over y_hi, core).
Axes of the slice: x: 4, y: 4 (y_hi: 2, y_lo: 2; y = y_hi * 2 + y_lo), z: 4, core: 2. Of those that a mesh axis runs over, the one named last changes fastest.
Arguments:
- tokens: bfloat16 [1024, 6144], P('seq'), may hold values from -6 to 6
- target: bfloat16 [1024, 6144], P('seq'), may hold values from -6 to 6
- norm_gain: float32 [6144], replicated, may hold values from 0.1 to 1.9
- qkv_weight: bfloat16 [6144, 9216], P(None, 'fsdp'), may hold values from -1 to 1
- out_weight: bfloat16 [3072, 6144], P('fsdp'), may hold values from -0.109375 to 0.109375
- probe_seed: int32 [1], replicated, may hold values from 0 to 1073741823
- block_order: int32 [4], P('seq'), may hold values from 0 to 3, each once
Outputs:
- qkv_curv: float32 [6144, 9216], P('seq', 'fsdp')
- out_curv: float32 [3072, 6144], P('fsdp', 'seq')
The draws below stay inside these ranges and needn't reach their ends.
Inputs may be any that keep to these rules, and one draw needn't show every extreme that they name: block_order is a permutation: each block of 256 tokens has its own place in the sequence.
All inputs are finite; a program needn't handle non-finite values.
Results may differ from the reference program's by a relative error of at most 0.02.
Values may be sent and summed in bfloat16 or wider, within the bound.
A program may use at most 128 MiB of HBM per device.

```python
import math
import jax
import jax.numpy as jnp
from jax import lax

D = 6144
HS = 96
ROT = 24
SEQ_DEV = 256
HEADS = 32
SEQ = 1024
N_SEQ = 4


def draw_tokens(key, part):
    key = jax.random.fold_in(key, 11)
    noise = jax.random.truncated_normal(key, -6.0, 6.0, (SEQ, D), jnp.float32)
    return noise.astype(jnp.bfloat16)


def draw_qkv_weight(key, part):
    key = jax.random.fold_in(key, 12)
    weights = jax.random.truncated_normal(key, -6.0, 6.0, (D, 3 * HEADS * HS), jnp.float32) / math.sqrt(D)
    return weights.astype(jnp.bfloat16)


def steps_of(own_key, dims, shards, low, largest):
    level = 1.0
    for axis_at, shards_of in shards:
        steps = jax.random.uniform(jax.random.fold_in(jax.random.fold_in(own_key, 6), axis_at), (shards_of,), jnp.float32, low / len(shards), largest / len(shards))
        level = level * jnp.repeat(jnp.exp(steps), dims[axis_at] // shards_of).reshape((-1,) + (1,) * (len(dims) - 1 - axis_at))
    return level


def scatter_about(key, shape, scale, most, split=(), held_as=jnp.bfloat16):
    entries = scale * jax.random.normal(key, shape, jnp.float32)
    if split:
        entries = entries * steps_of(key, shape, split, -0.22, 0.18)
    return jnp.clip(entries, -most, most).astype(held_as)


def setup_inputs(seed: int = 0) -> dict:
    streams_of = jax.random.split(jax.random.key(seed), 8)
    tokens = draw_tokens(jax.random.fold_in(streams_of[7], 71), 0)
    target = scatter_about(streams_of[1], (SEQ, D), 1.0, 6.0, ((0, 4),))
    norm_gain = jnp.clip(1.0 + 0.18 * jax.random.normal(streams_of[2], (D,), jnp.float32), 0.1, 1.9)
    qkv_weight = draw_qkv_weight(jax.random.fold_in(streams_of[7], 71), 0)
    out_weight = scatter_about(streams_of[4], (HEADS * HS, D), (HEADS * HS) ** -0.5, 0.109375, ((0, 32),))
    probe_seed = jax.random.randint(streams_of[5], (1,), 0, 1073741824).astype(jnp.int32)
    block_order = jax.random.permutation(streams_of[6], N_SEQ).astype(jnp.int32)
    return dict(tokens=tokens, target=target, norm_gain=norm_gain, qkv_weight=qkv_weight, out_weight=out_weight, probe_seed=probe_seed, block_order=block_order)


mix_one = -1640531535
mix_two = -2048144789
mix_three = -1028477387

def probe_signs(probe_seed, flat_index):
    state = flat_index * jnp.int32(mix_one) + probe_seed[0]
    state = state ^ lax.shift_right_logical(state, jnp.int32(16))
    state = state * jnp.int32(mix_two)
    state = state ^ lax.shift_right_logical(state, jnp.int32(13))
    state = state * jnp.int32(mix_three)
    state = state ^ lax.shift_right_logical(state, jnp.int32(16))
    chosen = lax.shift_right_logical(state, jnp.int32(7)) & jnp.int32(1)
    return (1 - 2 * chosen).astype(jnp.float32)

def layer_norm(tokens, norm_gain):
    values = tokens.astype(jnp.float32)
    average = lax.optimization_barrier(jnp.mean(values, axis=-1, keepdims=True))
    centred = values - average
    spread = lax.optimization_barrier(jnp.mean(centred * centred, axis=-1, keepdims=True))
    return (centred * lax.rsqrt(spread + 1e-05) * norm_gain).astype(jnp.bfloat16)

def rotate(field, positions):
    half_rot = ROT // 2
    inverse = 10000.0 ** (-2.0 * jnp.arange(half_rot, dtype=jnp.float32) / ROT)
    angles = positions.astype(jnp.float32)[:, None] * inverse[None, :]
    cosine = jnp.cos(angles)[:, None, :]
    sine = jnp.sin(angles)[:, None, :]
    lower_half = field[..., :half_rot]
    upper_half = field[..., half_rot:ROT]
    remainder = field[..., ROT:]
    return jnp.concatenate([lower_half * cosine - upper_half * sine, upper_half * cosine + lower_half * sine, remainder], axis=-1)

def prepare(qkv, positions):
    grid = qkv.reshape(qkv.shape[0], qkv.shape[1] // (3 * HS), 3, HS)
    query = rotate(grid[:, :, 0], positions).astype(jnp.bfloat16)
    keys = rotate(grid[:, :, 1], positions).astype(jnp.bfloat16)
    values = grid[:, :, 2].astype(jnp.bfloat16)
    return (query, keys, values)

def widened(qkv, positions):
    return tuple((part.astype(jnp.float32) for part in prepare(qkv, positions)))

def attend(query, keys, values, query_pos, key_pos):
    scores = jnp.einsum('qhd,khd->hqk', query, keys) / math.sqrt(query.shape[-1])
    allowed = key_pos[None, None, :] <= query_pos[None, :, None]
    scores = jnp.where(allowed, scores, -1e+30)
    highest = lax.stop_gradient(lax.optimization_barrier(jnp.max(scores, axis=-1, keepdims=True)))
    weights = jnp.exp(scores - highest)
    weights = weights / lax.optimization_barrier(jnp.sum(weights, axis=-1, keepdims=True))
    rounded = weights.astype(jnp.bfloat16).astype(jnp.float32)
    result = jnp.einsum('hqk,khd->qhd', rounded, values)
    return result.reshape(query.shape[0], -1).astype(jnp.bfloat16)

def by_head(field):
    return jnp.moveaxis(field, 1, 0)[:, :, None, :]

def from_head(field):
    return jnp.moveaxis(field, 0, 1).reshape(field.shape[1], -1)

def reference(tokens, target, norm_gain, qkv_weight, out_weight, probe_seed, block_order):
    offsets = jnp.arange(SEQ_DEV, dtype=jnp.int32)
    positions = (block_order[:, None] * SEQ_DEV + offsets[None, :]).reshape(-1).astype(jnp.int32)
    normed = layer_norm(tokens, norm_gain)
    col_count = 3 * HEADS * HS
    inner = HEADS * HS
    row_ids = lax.broadcasted_iota(jnp.int32, (D, col_count), 0)
    col_ids = lax.broadcasted_iota(jnp.int32, (D, col_count), 1)
    qkv_signs = probe_signs(probe_seed, row_ids * col_count + col_ids)
    out_rows = lax.broadcasted_iota(jnp.int32, (inner, D), 0)
    out_cols = lax.broadcasted_iota(jnp.int32, (inner, D), 1)
    out_signs = probe_signs(probe_seed, D * col_count + out_rows * D + out_cols)
    qkv_probe = (qkv_signs / math.sqrt(D)).astype(jnp.bfloat16)
    out_probe = (out_signs / math.sqrt(inner)).astype(jnp.bfloat16)
    qkv = jnp.dot(normed, qkv_weight, preferred_element_type=jnp.float32)
    qkv_tan = jnp.dot(normed, qkv_probe, preferred_element_type=jnp.float32)
    primals, tangents = jax.jvp(lambda field: widened(field, positions), (qkv,), (qkv_tan,))

    def forward_head(parts):
        return jax.jvp(lambda one, two, three: attend(one, two, three, positions, positions), parts[:3], parts[3:])
    heads_in = tuple((by_head(part) for part in primals + tangents))
    attn_heads, tan_heads = lax.map(forward_head, heads_in)
    attn = from_head(attn_heads)
    attn_tan = from_head(tan_heads)
    mixed = jnp.dot(attn, out_weight, preferred_element_type=jnp.float32)
    mixed_tan = jnp.dot(attn_tan, out_weight, preferred_element_type=jnp.float32) + jnp.dot(attn, out_probe, preferred_element_type=jnp.float32)
    resid = tokens.astype(jnp.float32) + mixed - target.astype(jnp.float32)
    grad_out = (resid / SEQ).astype(jnp.bfloat16)
    grad_tan = (mixed_tan / SEQ).astype(jnp.bfloat16)
    back = jnp.dot(grad_out, out_weight.T, preferred_element_type=jnp.float32).astype(jnp.bfloat16)
    back_tan = (jnp.dot(grad_tan, out_weight.T, preferred_element_type=jnp.float32) + jnp.dot(grad_out, out_probe.T, preferred_element_type=jnp.float32)).astype(jnp.bfloat16)
    out_hv = jnp.dot(attn_tan.T, grad_out, preferred_element_type=jnp.float32) + jnp.dot(attn.T, grad_tan, preferred_element_type=jnp.float32)

    def backward_head(parts):

        def pull_back(one, two, three, cotangent):
            return jax.vjp(lambda aa, bb, cc: attend(aa, bb, cc, positions, positions), one, two, three)[1](cotangent)
        return jax.jvp(pull_back, parts[:3] + (parts[6],), parts[3:6] + (parts[7],))[1]
    back_heads = jnp.moveaxis(back.reshape(SEQ, HEADS, HS), 1, 0)
    back_tan_heads = jnp.moveaxis(back_tan.reshape(SEQ, HEADS, HS), 1, 0)
    cot_parts = lax.map(backward_head, heads_in + (back_heads, back_tan_heads))
    cot_tans = tuple((jnp.moveaxis(part[:, :, 0, :], 0, 1) for part in cot_parts))
    qkv_cot = jax.vjp(lambda field: widened(field, positions), qkv)[1](cot_tans)[0]
    qkv_hv = jnp.dot(normed.T, qkv_cot.astype(jnp.bfloat16), preferred_element_type=jnp.float32)
    return (qkv_hv * qkv_signs * math.sqrt(D), out_hv * out_signs * math.sqrt(inner))
```

```python
import functools
import math

import jax
import jax.numpy as jnp
import numpy as np
from jax import lax
from jax.experimental import pallas as pl
from jax.experimental.pallas import tpu as pltpu
from jax.sharding import PartitionSpec as P

MESH = pl.DeviceIdType.MESH
BF = jnp.bfloat16
F32 = jnp.float32
D = 6144
HS = 96
ROT = 24
TOK = 256
COLS = 288
WIDE = 9216
INNER = 3072
SHARE = 1536
PART = 384
HALF = 48
MIX = (-1640531535, -2048144789, -1028477387)
N_REMOTE = 136
N_LOCAL = 16


def wrap(value):
    return ((value + 2**31) % 2**32) - 2**31


def shifted(state, places):
    return lax.shift_right_logical(state, jnp.full(state.shape, places, jnp.int32))


def sign_bit(state):
    state = state ^ shifted(state, 16)
    state = state * jnp.int32(MIX[1])
    state = state ^ shifted(state, 13)
    state = state * jnp.int32(MIX[2])
    return (state ^ shifted(state, 16)) & jnp.int32(128)


def dot(a, b, contract):
    return lax.dot_general(a, b, (contract, ((), ())), preferred_element_type=F32)


NN = ((1,), (0,))
NT = ((1,), (1,))
TN = ((0,), (0,))


def kernel(
    tok_in, tgt_in, gain, wq_in, wo_in, seed, block, tab_t, tab_b,
    oq, oo,
    tok, tgt, wq, nrm, acc,
    nb, nt, gkv, ta, tb, wa, wb, pa, pb, ga, gb,
    score, score_tan, prob, prob_tan, rnd, rnd_tan,
    mix_acc, mix_out, mix_in, grads, back_acc,
    sa, sb, ra1, rb1, sa2, sb2, ra2, rb2,
    ha, hb, ca, cb, xa, xb, ya, yb, fa, fb, oa, ob,
    ck, cr, cx, cy, cot, sgn,
    send, recv, local,
):
    fs = lax.axis_index("fsdp")
    s = lax.axis_index("seq")
    x = fs // 8
    yl = (fs // 4) % 2
    z = fs % 4
    yh = s // 2
    c = s % 2
    s_sib = yh * 2 + (1 - c)
    s_crs = (1 - yh) * 2 + c
    s_crd = (1 - yh) * 2 + (1 - c)
    own_cols = (x * 4 + z) * PART

    def device(px, py, pz, ps):
        return ((px * 2 + py) * 4 + pz, ps)

    def xp(d):
        return device((x + d) % 4, yl, z, s)

    def zp(d):
        return device(x, yl, (z + d) % 4, s)

    def fin(d):
        return device(s, yl, (z + d) % 4, x)

    partner = device(x, 1 - yl, z, s)
    sib = device(x, yl, z, s_sib)
    crs = device(x, yl, z, s_crs)
    crd = device(x, yl, z, s_crd)

    count = [0]
    sent = []

    def remote(src, dst, to, begin=True):
        i = count[0]
        count[0] += 1
        copy = pltpu.make_async_remote_copy(
            src_ref=src, dst_ref=dst, send_sem=send.at[i], recv_sem=recv.at[i],
            device_id=to, device_id_type=MESH,
        )
        if begin:
            copy.start()
            sent.append(copy)
        return copy

    local_count = [0]

    def stay(src, dst):
        i = local_count[0]
        local_count[0] += 1
        copy = pltpu.make_async_copy(src, dst, local.at[i])
        copy.start()
        return copy

    def arrived(copies):
        for copy in copies:
            copy.wait_recv()

    def lanes(start, size):
        return pl.ds(pl.multiple_of(start, 128), size)

    def rows(start, size):
        return pl.ds(pl.multiple_of(start, 16), size)

    tok_load = stay(tok_in, tok)
    wq_load = stay(wq_in, wq)
    tgt_load = stay(tgt_in.at[:, lanes(own_cols, PART)], tgt)
    own_ta = stay(wo_in.at[pl.ds(0, HALF), lanes(x * SHARE, SHARE)], ta.at[x])
    own_tb = [
        stay(wo_in.at[pl.ds(HALF, HALF), lanes((k * 4 + z) * PART, PART)], tb.at[z, k])
        for k in range(4)
    ]

    barrier = pltpu.get_barrier_semaphore()

    def greet(to):
        pl.semaphore_signal(barrier, inc=1, device_id=to, device_id_type=MESH)

    for d in (1, 2, 3):
        greet(xp(d))
        greet(zp(d))
    for to in (partner, sib, crs, crd):
        greet(to)

    @pl.when(x != s)
    def _():
        for d in range(4):
            greet(fin(d))

    pl.semaphore_wait(barrier, jnp.where(x != s, 14, 10))

    w_one = []
    for d in (1, 2, 3):
        other = (x + d) % 4
        w_one.append(
            remote(wo_in.at[pl.ds(0, HALF), lanes(other * SHARE, SHARE)], ta.at[x], xp(d))
        )
        other = (z + d) % 4
        for k in range(4):
            w_one.append(
                remote(
                    wo_in.at[pl.ds(HALF, HALF), lanes((k * 4 + other) * PART, PART)],
                    tb.at[z, k], zp(d),
                )
            )

    tok_load.wait()

    def norm_rows(i, carry):
        at = rows(i * 16, 16)
        values = tok[at, :].astype(F32)
        centred = values - jnp.mean(values, axis=-1, keepdims=True)
        spread = jnp.mean(centred * centred, axis=-1, keepdims=True)
        nrm[at, :] = (centred * lax.rsqrt(spread + 1e-05) * gain[...]).astype(BF)
        return carry

    lax.fori_loop(0, TOK // 16, norm_rows, 0)

    piece = jnp.where(c == 0, z * 4 + x, x * 4 + z) * 16
    n_sib = remote(nrm.at[:, lanes(s_sib * SHARE, SHARE)], nb.at[s], sib)
    n_crs = remote(
        nrm.at[rows(piece, 16), lanes(s_crs * SHARE, SHARE)], nb.at[s, rows(piece, 16)], crs
    )
    n_crd = remote(
        nrm.at[rows(piece, 16), lanes(s_crd * SHARE, SHARE)], nb.at[s, rows(piece, 16)], crd
    )

    wq_load.wait()
    acc[...] = jnp.zeros_like(acc)
    seeded = seed[0]
    q_probe = float(np.float32(1 / math.sqrt(D)).astype(jnp.bfloat16))
    o_probe = float(np.float32(1 / math.sqrt(INNER)).astype(jnp.bfloat16))
    q_rows = lax.broadcasted_iota(jnp.int32, (TOK, COLS), 0)
    q_cols = lax.broadcasted_iota(jnp.int32, (TOK, COLS), 1)
    q_base = (q_rows * WIDE + q_cols + fs * COLS) * jnp.int32(MIX[0]) + seeded

    def project(i, carry):
        at = pl.ds(pl.multiple_of(i * TOK, TOK), TOK)
        bit = sign_bit(q_base + i * jnp.int32(wrap(TOK * WIDE * MIX[0])))
        probe = jnp.where(bit == 0, F32(q_probe), F32(-q_probe)).astype(BF)
        left = nrm[:, pl.ds(pl.multiple_of(i * TOK, TOK), TOK)]
        acc[0, :, pl.ds(0, COLS)] += dot(left, wq[at, :], NN)
        acc[1, :, pl.ds(0, COLS)] += dot(left, probe, NN)
        return carry

    lax.fori_loop(0, D // TOK, project, 0)

    number = block[0]
    cos_b = jnp.zeros((ROT, TOK), F32)
    sin_b = jnp.zeros((ROT, TOK), F32)
    for k in range(4):
        here = jnp.full((ROT, TOK), number, jnp.int32) == k
        cos_b = jnp.where(here, tab_b[k, 0], cos_b)
        sin_b = jnp.where(here, tab_b[k, 1], sin_b)
    cos = cos_b * tab_t[0] - sin_b * tab_t[1]
    sin = sin_b * tab_t[0] + cos_b * tab_t[1]
    low = lax.broadcasted_iota(jnp.int32, (ROT, TOK), 0) < ROT // 2
    sin = jnp.where(low, -sin, sin)

    def rotate(field, turn):
        head = field[:ROT]
        swapped = pltpu.roll(head, ROT // 2, 0)
        return jnp.concatenate([head * cos + swapped * turn, field[ROT:]], axis=0)

    fields = []
    for k in range(2):
        turned = acc[k].T
        fields.append(
            (
                rotate(turned[0:HS], sin).astype(BF),
                rotate(turned[HS : 2 * HS], sin).astype(BF),
                turned[2 * HS : 3 * HS].astype(BF),
            )
        )
    q, q_tan = fields[0][0], fields[1][0]
    q_both = jnp.concatenate([q_tan, q], axis=0)
    gkv[s, 0:HS] = fields[0][1]
    gkv[s, HS : 2 * HS] = fields[1][1]
    gkv[s, 2 * HS : 3 * HS] = fields[0][2]
    gkv[s, 3 * HS : 4 * HS] = fields[1][2]
    gkv[s, 4 * HS : 4 * HS + 16] = jnp.full((16, TOK), number, jnp.int32).astype(F32).astype(BF)
    kv_crs = remote(gkv.at[s], gkv.at[s], crs)
    kv_sib = remote(gkv.at[s], gkv.at[s], sib)

    b0 = (1 - yh) * 2
    b1 = b0 + 1
    arrived([n_crs, n_crd])
    n_one = []
    for d in (1, 2, 3):
        at0 = nb.at[b0, rows((z * 4 + x) * 16, 16)]
        at1 = nb.at[b1, rows((x * 4 + z) * 16, 16)]
        n_one.append(remote(at0, at0, xp(d)))
        n_one.append(remote(at1, at1, zp(d)))

    for copy in [own_ta] + own_tb:
        copy.wait()
    arrived(w_one)
    w_two = []
    for d in (1, 2, 3):
        other = (z + d) % 4
        w_two.append(remote(ta.at[:, :, lanes(other * PART, PART)], wa.at[z], zp(d)))
        other = (x + d) % 4
        w_two.append(remote(tb.at[:, other], wb.at[x], xp(d)))
    own_wa = stay(ta.at[:, :, lanes(z * PART, PART)], wa.at[z])
    own_wb = stay(tb.at[:, x], wb.at[x])

    o_rows = lax.broadcasted_iota(jnp.int32, (HALF, PART), 0)
    o_lanes = lax.broadcasted_iota(jnp.int32, (HALF, PART), 1)
    o_base = (o_rows * D + o_lanes + (D * WIDE + own_cols)) * jnp.int32(MIX[0]) + seeded

    def probe_piece(i, carry):
        for k in range(4):
            first = ((k * 2 + yl) * 4 + i) * HS
            second = ((i * 2 + yl) * 4 + k) * HS + HALF
            bit = sign_bit(o_base + first * jnp.int32(wrap(D * MIX[0])))
            pa[i, k] = jnp.where(bit == 0, F32(o_probe), F32(-o_probe)).astype(BF)
            bit = sign_bit(o_base + second * jnp.int32(wrap(D * MIX[0])))
            pb[i, k] = jnp.where(bit == 0, F32(o_probe), F32(-o_probe)).astype(BF)
        return carry

    lax.fori_loop(0, 4, probe_piece, 0)

    arrived([kv_crs])
    kv_rel = remote(gkv.at[s_crs], gkv.at[s_crs], sib)

    arrived(n_one)
    n_two = []
    for d in (1, 2, 3):
        at0 = nb.at[b0, rows(z * 64, 64)]
        at1 = nb.at[b1, rows(x * 64, 64)]
        n_two.append(remote(at0, at0, zp(d)))
        n_two.append(remote(at1, at1, xp(d)))

    arrived([kv_sib, kv_rel])
    root = 1 / math.sqrt(HS)

    def keys_of(b):
        return lanes(b * TOK, TOK)

    def score_block(b, carry):
        score[:, keys_of(b)] = dot(q, gkv[b, 0:HS], TN) * root
        score_tan[:, keys_of(b)] = dot(q_both, gkv[b, 0 : 2 * HS], TN) * root
        return carry

    lax.fori_loop(0, 4, score_block, 0)
    along = lax.broadcasted_iota(jnp.int32, (1, TOK), 1).astype(F32)
    key_pos = jnp.concatenate(
        [gkv[b, 4 * HS : 4 * HS + 16].astype(F32)[0:1] * float(TOK) + along for b in range(4)], axis=1
    )
    number_f = jnp.full((32, 1), number, jnp.int32).astype(F32)
    down = lax.broadcasted_iota(jnp.int32, (32, 1), 0)

    def soft_rows(i, carry):
        at = pl.ds(pl.multiple_of(i * 32, 32), 32)
        query_pos = number_f * float(TOK) + (down + i * 32).astype(F32)
        allowed = key_pos <= query_pos
        values = jnp.where(allowed, score[at, :], -1e30)
        highest = jnp.max(values, axis=-1, keepdims=True)
        weights = jnp.exp(values - highest)
        weights = weights * (1.0 / jnp.sum(weights, axis=-1, keepdims=True))
        tans = score_tan[at, :]
        moved = weights * tans
        moved = moved - weights * jnp.sum(moved, axis=-1, keepdims=True)
        prob[at, :] = weights
        prob_tan[at, :] = moved
        rnd[at, :] = weights.astype(BF)
        rnd_tan[at, :] = moved.astype(BF)
        return carry

    lax.fori_loop(0, TOK // 32, soft_rows, 0)

    def sum_blocks(term, shape):
        total = jnp.zeros(shape, F32)
        return lax.fori_loop(0, 4, lambda b, held: held + term(b), total)

    def gather_one(t):
        copies = []
        for d in (1, 2, 3):
            copies.append(remote(ga.at[t, z, x], ga.at[t, z, x], xp(d)))
            copies.append(remote(gb.at[t, x, z], gb.at[t, x, z], zp(d)))
        return copies

    def gather_two(t):
        copies = []
        for d in (1, 2, 3):
            copies.append(remote(ga.at[t, z], ga.at[t, z], zp(d)))
            copies.append(remote(gb.at[t, x], gb.at[t, x], xp(d)))
        return copies

    value_terms = sum_blocks(
        lambda b: dot(gkv[b, 2 * HS : 4 * HS], rnd[:, keys_of(b)], NT), (2 * HS, TOK)
    )
    attn = value_terms[:HS].astype(BF)
    ga[0, z, x] = attn[:HALF]
    gb[0, x, z] = attn[HALF:]
    g_one = gather_one(0)
    attn_tan = (
        sum_blocks(lambda b: dot(gkv[b, 2 * HS : 3 * HS], rnd_tan[:, keys_of(b)], NT), (HS, TOK))
        + value_terms[HS:]
    ).astype(BF)
    ga[1, z, x] = attn_tan[:HALF]
    gb[1, x, z] = attn_tan[HALF:]
    g_one_tan = gather_one(1)
    arrived(g_one)
    g_two = gather_two(0)
    arrived(g_one_tan)
    g_two_tan = gather_two(1)


    arrived([n_sib] + n_two)

    def turn_own(i, carry):
        nt[s, pl.ds(pl.multiple_of(i * TOK, TOK), TOK), :] = nrm[:, lanes(s * SHARE + i * TOK, TOK)].T
        return carry

    lax.fori_loop(0, SHARE // TOK, turn_own, 0)

    def turn_other(i, carry):
        b = (s + 1 + i // 6) % 4
        k = i % 6
        nt[b, pl.ds(pl.multiple_of(k * TOK, TOK), TOK), :] = nb[b, :, lanes(k * TOK, TOK)].T
        return carry

    lax.fori_loop(0, 18, turn_other, 0)

    own_wa.wait()
    own_wb.wait()
    arrived(w_two)
    arrived(g_two)

    def whole(ref, *at):
        value = ref[at]
        return value.reshape(4 * HALF, value.shape[-1])

    mix_acc[...] = jnp.zeros_like(mix_acc)

    def mix_one(i, carry):
        left, right = whole(ga, 0, i), whole(gb, 0, i)
        mix_acc[0] += dot(left, whole(wa, i), TN) + dot(right, whole(wb, i), TN)
        mix_acc[1] += dot(left, whole(pa, i), TN) + dot(right, whole(pb, i), TN)
        return carry

    lax.fori_loop(0, 4, mix_one, 0)
    mix_out[0] = mix_acc[0].astype(BF)
    m_one = remote(mix_out.at[0], mix_in.at[0], partner)
    arrived(g_two_tan)

    def mix_two(i, carry):
        mix_acc[1] += dot(whole(ga, 1, i), whole(wa, i), TN) + dot(whole(gb, 1, i), whole(wb, i), TN)
        return carry

    lax.fori_loop(0, 4, mix_two, 0)
    mix_out[1] = mix_acc[1].astype(BF)
    m_two = remote(mix_out.at[1], mix_in.at[1], partner)

    s_base = (
        (lax.broadcasted_iota(jnp.int32, (128, COLS), 0) + s * SHARE) * WIDE
        + lax.broadcasted_iota(jnp.int32, (128, COLS), 1)
        + fs * COLS
    ) * jnp.int32(MIX[0]) + seeded

    def sign_rows(i, carry):
        bit = sign_bit(s_base + i * jnp.int32(wrap(128 * WIDE * MIX[0])))
        sgn[pl.ds(pl.multiple_of(i * 128, 128), 128), :] = jnp.where(
            bit == 0, F32(math.sqrt(D)), F32(-math.sqrt(D))
        )
        return carry

    lax.fori_loop(0, SHARE // 128, sign_rows, 0)

    tgt_load.wait()
    arrived([m_one])
    resid = tok[:, lanes(own_cols, PART)].astype(F32) - tgt[...].astype(F32)
    resid = resid + (mix_acc[0] + mix_in[0].astype(F32))
    grads[0] = (resid * (1 / 1024)).astype(BF)

    def back_one(i, carry):
        grad = grads[0]
        sa[0, i] = dot(whole(wa, i), grad, NT).astype(BF).reshape(4, HALF, TOK)
        sb[0, i] = dot(whole(wb, i), grad, NT).astype(BF).reshape(4, HALF, TOK)
        back_acc[0, i] = dot(whole(pa, i), grad, NT)
        back_acc[1, i] = dot(whole(pb, i), grad, NT)
        return carry

    lax.fori_loop(0, 4, back_one, 0)

    def scatter_one(t):
        copies = []
        for d in (1, 2, 3):
            copies.append(remote(sa.at[t, (z + d) % 4], ra1.at[t, d - 1], zp(d)))
            copies.append(remote(sb.at[t, (x + d) % 4], rb1.at[t, d - 1], xp(d)))
        return copies

    def total_of(own, others):
        total = own.astype(F32)
        for other in others:
            total = total + other.astype(F32)
        return total

    def scatter_two(t):
        sa2[t] = total_of(sa[t, z], [ra1[t, k] for k in range(3)]).astype(BF)
        sb2[t] = total_of(sb[t, x], [rb1[t, k] for k in range(3)]).astype(BF)
        copies = []
        for d in (1, 2, 3):
            copies.append(remote(sa2.at[t, (x + d) % 4], ra2.at[t, d - 1], xp(d)))
            copies.append(remote(sb2.at[t, (z + d) % 4], rb2.at[t, d - 1], zp(d)))
        return copies

    def scattered(t):
        first = total_of(sa2[t, x], [ra2[t, k] for k in range(3)])
        second = total_of(sb2[t, z], [rb2[t, k] for k in range(3)])
        return jnp.concatenate([first.astype(BF), second.astype(BF)], axis=0)

    r_one = scatter_one(0)
    arrived([m_two])
    grads[1] = ((mix_acc[1] + mix_in[1].astype(F32)) * (1 / 1024)).astype(BF)

    def back_two(i, carry):
        grad = grads[1]
        sa[1, i] = (dot(whole(wa, i), grad, NT) + back_acc[0, i]).astype(BF).reshape(4, HALF, TOK)
        sb[1, i] = (dot(whole(wb, i), grad, NT) + back_acc[1, i]).astype(BF).reshape(4, HALF, TOK)
        return carry

    lax.fori_loop(0, 4, back_two, 0)
    r_one_tan = scatter_one(1)

    def out_terms(i, carry):
        one, two = grads[0], grads[1]
        ha[i] = (
            (dot(whole(ga, 1, i), one, NN) + dot(whole(ga, 0, i), two, NN))
            .astype(BF).reshape(4, HALF, PART)
        )
        hb[i] = (
            (dot(whole(gb, 1, i), one, NN) + dot(whole(gb, 0, i), two, NN))
            .astype(BF).reshape(4, HALF, PART)
        )
        return carry

    lax.fori_loop(0, 4, out_terms, 0)
    o_core = []
    for k in range(2):
        o_core.append(remote(ha.at[:, 2 * k + 1 - c], ca.at[k], sib))
        o_core.append(remote(hb.at[2 * k + 1 - c], cb.at[k], sib))
    arrived(r_one)
    r_two = scatter_two(0)

    arrived(o_core)
    far = 1 - yh
    xa[...] = total_of(ha[:, 2 * far + c], [ca[far]]).astype(BF)
    xb[...] = total_of(hb[2 * far + c], [cb[far]]).astype(BF)
    o_crs = [remote(xa, ya, crs), remote(xb, yb, crs)]

    arrived(r_one_tan)
    r_two_tan = scatter_two(1)

    arrived(r_two)
    g = scattered(0)

    def pull_block(b, carry):
        score[:, keys_of(b)] = dot(g, gkv[b, 2 * HS : 3 * HS], TN)
        return carry

    lax.fori_loop(0, 4, pull_block, 0)
    arrived(o_crs)
    fa[...] = total_of(ha[:, s], [ca[yh], ya[...]]).astype(BF)
    fb[...] = total_of(hb[s], [cb[yh], yb[...]]).astype(BF)
    o_fin = []
    for d in (1, 2, 3):
        other = (z + d) % 4
        o_fin.append(remote(fa.at[other], oa.at[z], fin(d)))
        o_fin.append(remote(fb.at[other], ob.at[z], fin(d)))
    o_far = [
        remote(fa.at[z], oa.at[z], fin(0), begin=False),
        remote(fb.at[z], ob.at[z], fin(0), begin=False),
    ]
    near = local_count[0]
    o_near = [
        pltpu.make_async_copy(fa.at[z], oa.at[z], local.at[near]),
        pltpu.make_async_copy(fb.at[z], ob.at[z], local.at[near + 1]),
    ]

    @pl.when(x != s)
    def _():
        for copy in o_far:
            copy.start()

    @pl.when(x == s)
    def _():
        for copy in o_near:
            copy.start()

    arrived(r_two_tan)
    g_tan = scattered(1)
    g_both = jnp.concatenate([g_tan, g], axis=0)

    def pull_block_tan(b, carry):
        score_tan[:, keys_of(b)] = dot(g_both, gkv[b, 2 * HS : 4 * HS], TN)
        return carry

    lax.fori_loop(0, 4, pull_block_tan, 0)
    rnd_q, rnd_q_tan = prob, prob_tan

    def soft_back(i, carry):
        at = pl.ds(pl.multiple_of(i * 32, 32), 32)
        weights, moved = prob[at, :], prob_tan[at, :]
        pulled, pulled_tan = score[at, :], score_tan[at, :]
        base = jnp.sum(weights * pulled, axis=-1, keepdims=True)
        base_tan = jnp.sum(moved * pulled + weights * pulled_tan, axis=-1, keepdims=True)
        less = pulled - base
        score[at, :] = weights * less
        score_tan[at, :] = moved * less + weights * (pulled_tan - base_tan)
        return carry

    lax.fori_loop(0, TOK // 32, soft_back, 0)

    def cot_block(b, held):
        at = keys_of(b)
        slope, slope_tan = score[:, at].astype(BF), score_tan[:, at].astype(BF)
        ck[b, 0:HS] = ((dot(q, slope_tan, NN) + dot(q_tan, slope, NN)) * root).astype(BF)
        ck[b, HS : 2 * HS] = (dot(g, rnd_tan[:, at], NN) + dot(g_tan, rnd[:, at], NN)).astype(BF)
        return held + dot(gkv[b, 0:HS], slope_tan, NT) + dot(gkv[b, HS : 2 * HS], slope, NT)

    cot_query = lax.fori_loop(0, 4, cot_block, jnp.zeros((HS, TOK), F32)) * root
    c_core = [remote(ck.at[2 * k + 1 - c], cr.at[k], sib) for k in range(2)]
    cot[s, 0:HS] = rotate(cot_query.astype(BF).astype(F32), -sin).astype(BF)
    arrived(c_core)
    cx[...] = total_of(ck[2 * far + c], [cr[far]]).astype(BF)
    c_crs = remote(cx, cy, crs)

    arrived(o_fin)

    @pl.when(x != s)
    def _():
        for copy in o_far:
            copy.wait_recv()
            copy.wait_send()

    @pl.when(x == s)
    def _():
        for copy in o_near:
            copy.wait()

    e_base = (
        lax.broadcasted_iota(jnp.int32, (HALF, PART), 0) * D
        + lax.broadcasted_iota(jnp.int32, (HALF, PART), 1)
        + (D * WIDE + fs * HS * D + s * SHARE)
    ) * jnp.int32(MIX[0]) + seeded
    scale = math.sqrt(INNER)
    for half, ref in enumerate((oa, ob)):
        for k in range(4):
            bit = sign_bit(e_base + jnp.int32(wrap((half * HALF * D + k * PART) * MIX[0])))
            oo[half * HALF : (half + 1) * HALF, k * PART : (k + 1) * PART] = ref[k].astype(
                F32
            ) * jnp.where(bit == 0, F32(scale), F32(-scale))

    arrived([c_crs])
    both = total_of(ck[s], [cr[yh], cy[...]])
    cot[s, HS : 2 * HS] = rotate(both[:HS].astype(BF).astype(F32), -sin).astype(BF)
    cot[s, 2 * HS : 3 * HS] = both[HS:].astype(BF)
    t_crs = remote(cot.at[s], cot.at[s], crs)
    t_sib = remote(cot.at[s], cot.at[s], sib)

    def share_rows(i):
        return pl.ds(pl.multiple_of(i * TOK, TOK), TOK)

    def first_term(i, carry):
        oq[share_rows(i), :] = dot(nt[s, share_rows(i), :], cot[s], NT)
        return carry

    lax.fori_loop(0, SHARE // TOK, first_term, 0)
    arrived([t_sib])

    def second_term(i, carry):
        oq[share_rows(i), :] += dot(nt[s_sib, share_rows(i), :], cot[s_sib], NT)
        return carry

    lax.fori_loop(0, SHARE // TOK, second_term, 0)
    arrived([t_crs])
    t_rel = remote(cot.at[s_crs], cot.at[s_crs], sib)

    def third_term(i, carry):
        oq[share_rows(i), :] += dot(nt[s_crs, share_rows(i), :], cot[s_crs], NT)
        return carry

    lax.fori_loop(0, SHARE // TOK, third_term, 0)
    arrived([t_rel])

    def last_term(i, carry):
        at = share_rows(i)
        oq[at, :] = (oq[at, :] + dot(nt[s_crd, at, :], cot[s_crd], NT)) * sgn[at, :]
        return carry

    lax.fori_loop(0, SHARE // TOK, last_term, 0)
    for copy in sent:
        copy.wait_send()


def tables():
    rate = 10000.0 ** (-2.0 * np.arange(ROT // 2) / ROT)
    rate = np.concatenate([rate, rate])[:, None]
    within = np.arange(TOK)[None, :] * rate
    blocks = np.arange(4)[:, None, None] * float(TOK) * rate[None] + np.zeros((1, 1, TOK))
    tab_t = np.stack([np.cos(within), np.sin(within)]).astype(np.float32)
    tab_b = np.stack([np.cos(blocks), np.sin(blocks)], axis=1).astype(np.float32)
    return tab_t, tab_b


def per_device(tokens, target, norm_gain, qkv_weight, out_weight, probe_seed, block_order):
    tab_t, tab_b = tables()
    anywhere = pl.BlockSpec(memory_space=pl.ANY)
    vmem = pl.BlockSpec(memory_space=pltpu.VMEM)
    smem = pl.BlockSpec(memory_space=pltpu.SMEM)
    v = pltpu.VMEM
    scratch = [
        v((TOK, D), BF), v((TOK, PART), BF), v((D, COLS), BF), v((TOK, D), BF), v((2, TOK, 384), F32),
        v((4, TOK, SHARE), BF), v((4, SHARE, TOK), BF), v((4, 4 * HS + 16, TOK), BF),
        v((4, HALF, SHARE), BF), v((4, 4, HALF, PART), BF),
        v((4, 4, HALF, PART), BF), v((4, 4, HALF, PART), BF),
        v((4, 4, HALF, PART), BF), v((4, 4, HALF, PART), BF),
        v((2, 4, 4, HALF, TOK), BF), v((2, 4, 4, HALF, TOK), BF),
        v((TOK, 1024), F32), v((TOK, 1024), F32), v((TOK, 1024), F32), v((TOK, 1024), F32),
        v((TOK, 1024), BF), v((TOK, 1024), BF),
        v((2, TOK, PART), F32), v((2, TOK, PART), BF), v((2, TOK, PART), BF), v((2, TOK, PART), BF),
        v((2, 4, 4 * HALF, TOK), F32),
        v((2, 4, 4, HALF, TOK), BF), v((2, 4, 4, HALF, TOK), BF),
        v((2, 3, 4, HALF, TOK), BF), v((2, 3, 4, HALF, TOK), BF),
        v((2, 4, HALF, TOK), BF), v((2, 4, HALF, TOK), BF),
        v((2, 3, HALF, TOK), BF), v((2, 3, HALF, TOK), BF),
        v((4, 4, HALF, PART), BF), v((4, 4, HALF, PART), BF),
        v((2, 4, HALF, PART), BF), v((2, 4, HALF, PART), BF),
        v((4, HALF, PART), BF), v((4, HALF, PART), BF), v((4, HALF, PART), BF), v((4, HALF, PART), BF),
        v((4, HALF, PART), BF), v((4, HALF, PART), BF), v((4, HALF, PART), BF), v((4, HALF, PART), BF),
        v((4, 2 * HS, TOK), BF), v((2, 2 * HS, TOK), BF), v((2 * HS, TOK), BF), v((2 * HS, TOK), BF),
        v((4, 3 * HS, TOK), BF), v((SHARE, COLS), F32),
        pltpu.SemaphoreType.DMA((N_REMOTE,)), pltpu.SemaphoreType.DMA((N_REMOTE,)),
        pltpu.SemaphoreType.DMA((N_LOCAL,)),
    ]
    return pl.pallas_call(
        kernel,
        out_shape=(
            jax.ShapeDtypeStruct((SHARE, COLS), F32),
            jax.ShapeDtypeStruct((HS, SHARE), F32),
        ),
        in_specs=[anywhere, anywhere, vmem, anywhere, anywhere, smem, smem, vmem, vmem],
        out_specs=(vmem, vmem),
        scratch_shapes=scratch,
        compiler_params=pltpu.CompilerParams(
            collective_id=0, has_side_effects=True, vmem_limit_bytes=60 * 2**20
        ),
    )(
        tokens, target, norm_gain.reshape(1, D), qkv_weight, out_weight, probe_seed, block_order,
        jnp.asarray(tab_t), jnp.asarray(tab_b),
    )


def solution(mesh):
    placed = (P("seq", None), P("seq", None), P(), P(None, "fsdp"), P("fsdp", None), P(), P("seq"))
    return jax.shard_map(
        per_device,
        mesh=mesh,
        in_specs=placed,
        out_specs=(P("seq", "fsdp"), P("fsdp", "seq")),
        check_vma=False,
    )
```

```python
import functools
import math

import jax
import jax.numpy as jnp
import numpy as np
from jax import lax
from jax.experimental import pallas as pl
from jax.experimental.pallas import tpu as pltpu
from jax.sharding import PartitionSpec as P

MESH = pl.DeviceIdType.MESH
BF = jnp.bfloat16
F32 = jnp.float32
D = 6144
HS = 96
ROT = 24
TOK = 256
COLS = 288
WIDE = 9216
INNER = 3072
SHARE = 1536
PART = 384
HALF = 48
STEP = 768
MIX = (-1640531535, -2048144789, -1028477387)
N_REMOTE = 136
N_LOCAL = 16


def wrap(value):
    return ((value + 2**31) % 2**32) - 2**31


def shifted(state, places):
    return lax.shift_right_logical(state, jnp.full(state.shape, places, jnp.int32))


def sign_bit(state):
    state = state ^ shifted(state, 16)
    state = state * jnp.int32(MIX[1])
    state = state ^ shifted(state, 13)
    state = state * jnp.int32(MIX[2])
    return (state ^ shifted(state, 16)) & jnp.int32(128)


def dot(a, b, contract):
    return lax.dot_general(a, b, (contract, ((), ())), preferred_element_type=F32)


NN = ((1,), (0,))
NT = ((1,), (1,))
TN = ((0,), (0,))


def kernel(
    tok_in, tgt_in, gain, wq_in, wo_in, seed, block, tab_t, tab_b,
    oq, oo,
    tok, tgt, wq, nrm, acc,
    nb, gkv, ta, tb, wa, wb, pa, pb, ga, gb,
    score, score_tan, prob, prob_tan, rnd, rnd_tan,
    mix_acc, mix_out, mix_in, grads, back_acc,
    sa, sb, ra1, rb1, sa2, sb2, ra2, rb2,
    ha, hb, ca, cb, xa, xb, ya, yb, fa, fb, oa, ob,
    ck, cr, cx, cy, cot, sgn,
    send, recv, local,
):
    fs = lax.axis_index("fsdp")
    s = lax.axis_index("seq")
    x = fs // 8
    yl = (fs // 4) % 2
    z = fs % 4
    yh = s // 2
    c = s % 2
    s_sib = yh * 2 + (1 - c)
    s_crs = (1 - yh) * 2 + c
    s_crd = (1 - yh) * 2 + (1 - c)
    own_cols = (x * 4 + z) * PART

    def device(px, py, pz, ps):
        return ((px * 2 + py) * 4 + pz, ps)

    def xp(d):
        return device((x + d) % 4, yl, z, s)

    def zp(d):
        return device(x, yl, (z + d) % 4, s)

    def fin(d):
        return device(s, yl, (z + d) % 4, x)

    partner = device(x, 1 - yl, z, s)
    sib = device(x, yl, z, s_sib)
    crs = device(x, yl, z, s_crs)
    crd = device(x, yl, z, s_crd)

    count = [0]
    sent = []

    def remote(src, dst, to, begin=True):
        i = count[0]
        count[0] += 1
        copy = pltpu.make_async_remote_copy(
            src_ref=src, dst_ref=dst, send_sem=send.at[i], recv_sem=recv.at[i],
            device_id=to, device_id_type=MESH,
        )
        if begin:
            copy.start()
            sent.append(copy)
        return copy

    local_count = [0]

    def stay(src, dst):
        i = local_count[0]
        local_count[0] += 1
        copy = pltpu.make_async_copy(src, dst, local.at[i])
        copy.start()
        return copy

    def arrived(copies):
        for copy in copies:
            copy.wait_recv()

    def lanes(start, size):
        return pl.ds(pl.multiple_of(start, 128), size)

    def rows(start, size):
        return pl.ds(pl.multiple_of(start, 16), size)

    tok_load = stay(tok_in, tok)
    wq_load = stay(wq_in, wq)
    tgt_load = stay(tgt_in.at[:, lanes(own_cols, PART)], tgt)
    own_ta = stay(wo_in.at[pl.ds(0, HALF), lanes(x * SHARE, SHARE)], ta.at[x])
    own_tb = [
        stay(wo_in.at[pl.ds(HALF, HALF), lanes((k * 4 + z) * PART, PART)], tb.at[z, k])
        for k in range(4)
    ]

    barrier = pltpu.get_barrier_semaphore()

    def greet(to):
        pl.semaphore_signal(barrier, inc=1, device_id=to, device_id_type=MESH)

    for d in (1, 2, 3):
        greet(xp(d))
        greet(zp(d))
    for to in (partner, sib, crs, crd):
        greet(to)

    @pl.when(x != s)
    def _():
        for d in range(4):
            greet(fin(d))

    pl.semaphore_wait(barrier, jnp.where(x != s, 14, 10))

    w_one = []
    for d in (1, 2, 3):
        other = (x + d) % 4
        w_one.append(
            remote(wo_in.at[pl.ds(0, HALF), lanes(other * SHARE, SHARE)], ta.at[x], xp(d))
        )
        other = (z + d) % 4
        for k in range(4):
            w_one.append(
                remote(
                    wo_in.at[pl.ds(HALF, HALF), lanes((k * 4 + other) * PART, PART)],
                    tb.at[z, k], zp(d),
                )
            )

    tok_load.wait()

    def norm_rows(i, carry):
        at = rows(i * 16, 16)
        values = tok[at, :].astype(F32)
        centred = values - jnp.mean(values, axis=-1, keepdims=True)
        spread = jnp.mean(centred * centred, axis=-1, keepdims=True)
        nrm[at, :] = (centred * lax.rsqrt(spread + 1e-05) * gain[...]).astype(BF)
        return carry

    lax.fori_loop(0, TOK // 16, norm_rows, 0)

    piece = jnp.where(c == 0, z * 4 + x, x * 4 + z) * 16
    n_sib = remote(nrm.at[:, lanes(s_sib * SHARE, SHARE)], nb.at[s], sib)
    n_crs = remote(
        nrm.at[rows(piece, 16), lanes(s_crs * SHARE, SHARE)], nb.at[s, rows(piece, 16)], crs
    )
    n_crd = remote(
        nrm.at[rows(piece, 16), lanes(s_crd * SHARE, SHARE)], nb.at[s, rows(piece, 16)], crd
    )

    wq_load.wait()
    acc[...] = jnp.zeros_like(acc)
    seeded = seed[0]
    q_probe = float(np.float32(1 / math.sqrt(D)).astype(jnp.bfloat16))
    o_probe = float(np.float32(1 / math.sqrt(INNER)).astype(jnp.bfloat16))
    q_rows = lax.broadcasted_iota(jnp.int32, (COLS, STEP), 1)
    q_cols = lax.broadcasted_iota(jnp.int32, (COLS, STEP), 0)
    q_base = (q_rows * WIDE + q_cols + fs * COLS) * jnp.int32(MIX[0]) + seeded

    def project(i, carry):
        at = pl.ds(pl.multiple_of(i * STEP, STEP), STEP)
        bit = sign_bit(q_base + i * jnp.int32(wrap(STEP * WIDE * MIX[0])))
        probe = jnp.where(bit == 0, F32(q_probe), F32(-q_probe)).astype(BF)
        right = nrm[:, at]
        acc[0] += dot(wq[:, at], right, NT)
        acc[1] += dot(probe, right, NT)
        return carry

    lax.fori_loop(0, D // STEP, project, 0)

    number = block[0]
    cos_b = jnp.zeros((ROT, TOK), F32)
    sin_b = jnp.zeros((ROT, TOK), F32)
    for k in range(4):
        here = jnp.full((ROT, TOK), number, jnp.int32) == k
        cos_b = jnp.where(here, tab_b[k, 0], cos_b)
        sin_b = jnp.where(here, tab_b[k, 1], sin_b)
    cos = cos_b * tab_t[0] - sin_b * tab_t[1]
    sin = sin_b * tab_t[0] + cos_b * tab_t[1]
    low = lax.broadcasted_iota(jnp.int32, (ROT, TOK), 0) < ROT // 2
    sin = jnp.where(low, -sin, sin)

    def rotate(field, turn):
        head = field[:ROT]
        swapped = pltpu.roll(head, ROT // 2, 0)
        return jnp.concatenate([head * cos + swapped * turn, field[ROT:]], axis=0)

    fields = []
    for k in range(2):
        turned = acc[k]
        fields.append(
            (
                rotate(turned[0:HS], sin).astype(BF),
                rotate(turned[HS : 2 * HS], sin).astype(BF),
                turned[2 * HS : 3 * HS].astype(BF),
            )
        )
    q, q_tan = fields[0][0], fields[1][0]
    q_both = jnp.concatenate([q_tan, q], axis=0)
    gkv[s, 0:HS] = fields[0][1]
    gkv[s, HS : 2 * HS] = fields[1][1]
    gkv[s, 2 * HS : 3 * HS] = fields[0][2]
    gkv[s, 3 * HS : 4 * HS] = fields[1][2]
    gkv[s, 4 * HS : 4 * HS + 16] = jnp.full((16, TOK), number, jnp.int32).astype(F32).astype(BF)
    kv_crs = remote(gkv.at[s], gkv.at[s], crs)
    kv_sib = remote(gkv.at[s], gkv.at[s], sib)

    b0 = (1 - yh) * 2
    b1 = b0 + 1
    arrived([n_crs, n_crd])
    n_one = []
    for d in (1, 2, 3):
        at0 = nb.at[b0, rows((z * 4 + x) * 16, 16)]
        at1 = nb.at[b1, rows((x * 4 + z) * 16, 16)]
        n_one.append(remote(at0, at0, xp(d)))
        n_one.append(remote(at1, at1, zp(d)))

    for copy in [own_ta] + own_tb:
        copy.wait()
    arrived(w_one)
    w_two = []
    for d in (1, 2, 3):
        other = (z + d) % 4
        w_two.append(remote(ta.at[:, :, lanes(other * PART, PART)], wa.at[z], zp(d)))
        other = (x + d) % 4
        w_two.append(remote(tb.at[:, other], wb.at[x], xp(d)))
    own_wa = stay(ta.at[:, :, lanes(z * PART, PART)], wa.at[z])
    own_wb = stay(tb.at[:, x], wb.at[x])

    o_rows = lax.broadcasted_iota(jnp.int32, (HALF, PART), 0)
    o_lanes = lax.broadcasted_iota(jnp.int32, (HALF, PART), 1)
    o_base = (o_rows * D + o_lanes + (D * WIDE + own_cols)) * jnp.int32(MIX[0]) + seeded

    def probe_piece(i, carry):
        for k in range(4):
            first = ((k * 2 + yl) * 4 + i) * HS
            second = ((i * 2 + yl) * 4 + k) * HS + HALF
            bit = sign_bit(o_base + first * jnp.int32(wrap(D * MIX[0])))
            pa[i, k] = jnp.where(bit == 0, F32(o_probe), F32(-o_probe)).astype(BF)
            bit = sign_bit(o_base + second * jnp.int32(wrap(D * MIX[0])))
            pb[i, k] = jnp.where(bit == 0, F32(o_probe), F32(-o_probe)).astype(BF)
        return carry

    lax.fori_loop(0, 4, probe_piece, 0)

    arrived([kv_crs])
    kv_rel = remote(gkv.at[s_crs], gkv.at[s_crs], sib)

    arrived(n_one)
    n_two = []
    for d in (1, 2, 3):
        at0 = nb.at[b0, rows(z * 64, 64)]
        at1 = nb.at[b1, rows(x * 64, 64)]
        n_two.append(remote(at0, at0, zp(d)))
        n_two.append(remote(at1, at1, xp(d)))

    arrived([kv_sib, kv_rel])
    root = 1 / math.sqrt(HS)

    def keys_of(b):
        return lanes(b * TOK, TOK)

    def score_block(b, carry):
        score[:, keys_of(b)] = dot(q, gkv[b, 0:HS], TN) * root
        score_tan[:, keys_of(b)] = dot(q_both, gkv[b, 0 : 2 * HS], TN) * root
        return carry

    lax.fori_loop(0, 4, score_block, 0)
    along = lax.broadcasted_iota(jnp.int32, (1, TOK), 1).astype(F32)
    key_pos = jnp.concatenate(
        [gkv[b, 4 * HS : 4 * HS + 16].astype(F32)[0:1] * float(TOK) + along for b in range(4)], axis=1
    )
    number_f = jnp.full((32, 1), number, jnp.int32).astype(F32)
    down = lax.broadcasted_iota(jnp.int32, (32, 1), 0)

    def soft_rows(i, carry):
        at = pl.ds(pl.multiple_of(i * 32, 32), 32)
        query_pos = number_f * float(TOK) + (down + i * 32).astype(F32)
        allowed = key_pos <= query_pos
        values = jnp.where(allowed, score[at, :], -1e30)
        highest = jnp.max(values, axis=-1, keepdims=True)
        weights = jnp.exp(values - highest)
        weights = weights * (1.0 / jnp.sum(weights, axis=-1, keepdims=True))
        tans = score_tan[at, :]
        moved = weights * tans
        moved = moved - weights * jnp.sum(moved, axis=-1, keepdims=True)
        prob[at, :] = weights
        prob_tan[at, :] = moved
        rnd[at, :] = weights.astype(BF)
        rnd_tan[at, :] = moved.astype(BF)
        return carry

    lax.fori_loop(0, TOK // 32, soft_rows, 0)

    def sum_blocks(term, shape):
        total = jnp.zeros(shape, F32)
        return lax.fori_loop(0, 4, lambda b, held: held + term(b), total)

    def gather_one(t):
        copies = []
        for d in (1, 2, 3):
            copies.append(remote(ga.at[t, z, x], ga.at[t, z, x], xp(d)))
            copies.append(remote(gb.at[t, x, z], gb.at[t, x, z], zp(d)))
        return copies

    def gather_two(t):
        copies = []
        for d in (1, 2, 3):
            copies.append(remote(ga.at[t, z], ga.at[t, z], zp(d)))
            copies.append(remote(gb.at[t, x], gb.at[t, x], xp(d)))
        return copies

    value_terms = sum_blocks(
        lambda b: dot(gkv[b, 2 * HS : 4 * HS], rnd[:, keys_of(b)], NT), (2 * HS, TOK)
    )
    attn = value_terms[:HS].astype(BF)
    ga[0, z, x] = attn[:HALF]
    gb[0, x, z] = attn[HALF:]
    g_one = gather_one(0)
    attn_tan = (
        sum_blocks(lambda b: dot(gkv[b, 2 * HS : 3 * HS], rnd_tan[:, keys_of(b)], NT), (HS, TOK))
        + value_terms[HS:]
    ).astype(BF)
    ga[1, z, x] = attn_tan[:HALF]
    gb[1, x, z] = attn_tan[HALF:]
    g_one_tan = gather_one(1)
    arrived(g_one)
    g_two = gather_two(0)
    arrived(g_one_tan)
    g_two_tan = gather_two(1)

    own_wa.wait()
    own_wb.wait()
    arrived(w_two)
    arrived(g_two)

    def whole(ref, *at):
        value = ref[at]
        return value.reshape(4 * HALF, value.shape[-1])

    mix_acc[...] = jnp.zeros_like(mix_acc)

    def mix_one(i, carry):
        left, right = whole(ga, 0, i), whole(gb, 0, i)
        mix_acc[0] += dot(left, whole(wa, i), TN) + dot(right, whole(wb, i), TN)
        mix_acc[1] += dot(left, whole(pa, i), TN) + dot(right, whole(pb, i), TN)
        return carry

    lax.fori_loop(0, 4, mix_one, 0)
    mix_out[0] = mix_acc[0].astype(BF)
    m_one = remote(mix_out.at[0], mix_in.at[0], partner)
    arrived(g_two_tan)

    def mix_two(i, carry):
        mix_acc[1] += dot(whole(ga, 1, i), whole(wa, i), TN) + dot(whole(gb, 1, i), whole(wb, i), TN)
        return carry

    lax.fori_loop(0, 4, mix_two, 0)
    mix_out[1] = mix_acc[1].astype(BF)
    m_two = remote(mix_out.at[1], mix_in.at[1], partner)

    s_base = (
        (lax.broadcasted_iota(jnp.int32, (COLS, TOK), 1) + s * SHARE) * WIDE
        + lax.broadcasted_iota(jnp.int32, (COLS, TOK), 0)
        + fs * COLS
    ) * jnp.int32(MIX[0]) + seeded

    def sign_cols(i, carry):
        bit = sign_bit(s_base + i * jnp.int32(wrap(TOK * WIDE * MIX[0])))
        sgn[:, lanes(i * TOK, TOK)] = jnp.where(bit == 0, F32(math.sqrt(D)), F32(-math.sqrt(D)))
        return carry

    lax.fori_loop(0, SHARE // TOK, sign_cols, 0)

    tgt_load.wait()
    arrived([m_one])
    resid = tok[:, lanes(own_cols, PART)].astype(F32) - tgt[...].astype(F32)
    resid = resid + (mix_acc[0] + mix_in[0].astype(F32))
    grads[0] = (resid * (1 / 1024)).astype(BF)

    def back_one(i, carry):
        grad = grads[0]
        sa[0, i] = dot(whole(wa, i), grad, NT).astype(BF).reshape(4, HALF, TOK)
        sb[0, i] = dot(whole(wb, i), grad, NT).astype(BF).reshape(4, HALF, TOK)
        back_acc[0, i] = dot(whole(pa, i), grad, NT)
        back_acc[1, i] = dot(whole(pb, i), grad, NT)
        return carry

    lax.fori_loop(0, 4, back_one, 0)

    def scatter_one(t):
        copies = []
        for d in (1, 2, 3):
            copies.append(remote(sa.at[t, (z + d) % 4], ra1.at[t, d - 1], zp(d)))
            copies.append(remote(sb.at[t, (x + d) % 4], rb1.at[t, d - 1], xp(d)))
        return copies

    def total_of(own, others):
        total = own.astype(F32)
        for other in others:
            total = total + other.astype(F32)
        return total

    def scatter_two(t):
        sa2[t] = total_of(sa[t, z], [ra1[t, k] for k in range(3)]).astype(BF)
        sb2[t] = total_of(sb[t, x], [rb1[t, k] for k in range(3)]).astype(BF)
        copies = []
        for d in (1, 2, 3):
            copies.append(remote(sa2.at[t, (x + d) % 4], ra2.at[t, d - 1], xp(d)))
            copies.append(remote(sb2.at[t, (z + d) % 4], rb2.at[t, d - 1], zp(d)))
        return copies

    def scattered(t):
        first = total_of(sa2[t, x], [ra2[t, k] for k in range(3)])
        second = total_of(sb2[t, z], [rb2[t, k] for k in range(3)])
        return jnp.concatenate([first.astype(BF), second.astype(BF)], axis=0)

    r_one = scatter_one(0)
    arrived([m_two])
    grads[1] = ((mix_acc[1] + mix_in[1].astype(F32)) * (1 / 1024)).astype(BF)

    def back_two(i, carry):
        grad = grads[1]
        sa[1, i] = (dot(whole(wa, i), grad, NT) + back_acc[0, i]).astype(BF).reshape(4, HALF, TOK)
        sb[1, i] = (dot(whole(wb, i), grad, NT) + back_acc[1, i]).astype(BF).reshape(4, HALF, TOK)
        return carry

    lax.fori_loop(0, 4, back_two, 0)
    r_one_tan = scatter_one(1)

    def out_terms(i, carry):
        one, two = grads[0], grads[1]
        ha[i] = (
            (dot(whole(ga, 1, i), one, NN) + dot(whole(ga, 0, i), two, NN))
            .astype(BF).reshape(4, HALF, PART)
        )
        hb[i] = (
            (dot(whole(gb, 1, i), one, NN) + dot(whole(gb, 0, i), two, NN))
            .astype(BF).reshape(4, HALF, PART)
        )
        return carry

    lax.fori_loop(0, 4, out_terms, 0)
    o_core = []
    for k in range(2):
        o_core.append(remote(ha.at[:, 2 * k + 1 - c], ca.at[k], sib))
        o_core.append(remote(hb.at[2 * k + 1 - c], cb.at[k], sib))
    arrived(r_one)
    r_two = scatter_two(0)

    arrived(o_core)
    far = 1 - yh
    xa[...] = total_of(ha[:, 2 * far + c], [ca[far]]).astype(BF)
    xb[...] = total_of(hb[2 * far + c], [cb[far]]).astype(BF)
    o_crs = [remote(xa, ya, crs), remote(xb, yb, crs)]

    arrived(r_one_tan)
    r_two_tan = scatter_two(1)

    arrived(r_two)
    g = scattered(0)

    def pull_block(b, carry):
        score[:, keys_of(b)] = dot(g, gkv[b, 2 * HS : 3 * HS], TN)
        return carry

    lax.fori_loop(0, 4, pull_block, 0)
    arrived(o_crs)
    fa[...] = total_of(ha[:, s], [ca[yh], ya[...]]).astype(BF)
    fb[...] = total_of(hb[s], [cb[yh], yb[...]]).astype(BF)
    o_fin = []
    for d in (1, 2, 3):
        other = (z + d) % 4
        o_fin.append(remote(fa.at[other], oa.at[z], fin(d)))
        o_fin.append(remote(fb.at[other], ob.at[z], fin(d)))
    o_far = [
        remote(fa.at[z], oa.at[z], fin(0), begin=False),
        remote(fb.at[z], ob.at[z], fin(0), begin=False),
    ]
    near = local_count[0]
    o_near = [
        pltpu.make_async_copy(fa.at[z], oa.at[z], local.at[near]),
        pltpu.make_async_copy(fb.at[z], ob.at[z], local.at[near + 1]),
    ]

    @pl.when(x != s)
    def _():
        for copy in o_far:
            copy.start()

    @pl.when(x == s)
    def _():
        for copy in o_near:
            copy.start()

    arrived(r_two_tan)
    g_tan = scattered(1)
    g_both = jnp.concatenate([g_tan, g], axis=0)

    def pull_block_tan(b, carry):
        score_tan[:, keys_of(b)] = dot(g_both, gkv[b, 2 * HS : 4 * HS], TN)
        return carry

    lax.fori_loop(0, 4, pull_block_tan, 0)

    def soft_back(i, carry):
        at = pl.ds(pl.multiple_of(i * 32, 32), 32)
        weights, moved = prob[at, :], prob_tan[at, :]
        pulled, pulled_tan = score[at, :], score_tan[at, :]
        base = jnp.sum(weights * pulled, axis=-1, keepdims=True)
        base_tan = jnp.sum(moved * pulled + weights * pulled_tan, axis=-1, keepdims=True)
        less = pulled - base
        score[at, :] = weights * less
        score_tan[at, :] = moved * less + weights * (pulled_tan - base_tan)
        return carry

    lax.fori_loop(0, TOK // 32, soft_back, 0)

    def cot_block(b, held):
        at = keys_of(b)
        slope, slope_tan = score[:, at].astype(BF), score_tan[:, at].astype(BF)
        ck[b, 0:HS] = ((dot(q, slope_tan, NN) + dot(q_tan, slope, NN)) * root).astype(BF)
        ck[b, HS : 2 * HS] = (dot(g, rnd_tan[:, at], NN) + dot(g_tan, rnd[:, at], NN)).astype(BF)
        return held + dot(gkv[b, 0:HS], slope_tan, NT) + dot(gkv[b, HS : 2 * HS], slope, NT)

    cot_query = lax.fori_loop(0, 4, cot_block, jnp.zeros((HS, TOK), F32)) * root
    c_core = [remote(ck.at[2 * k + 1 - c], cr.at[k], sib) for k in range(2)]
    cot[s, 0:HS] = rotate(cot_query.astype(BF).astype(F32), -sin).astype(BF)
    arrived(c_core)
    cx[...] = total_of(ck[2 * far + c], [cr[far]]).astype(BF)
    c_crs = remote(cx, cy, crs)

    arrived(o_fin)

    @pl.when(x != s)
    def _():
        for copy in o_far:
            copy.wait_recv()
            copy.wait_send()

    @pl.when(x == s)
    def _():
        for copy in o_near:
            copy.wait()

    e_base = (
        lax.broadcasted_iota(jnp.int32, (HALF, PART), 0) * D
        + lax.broadcasted_iota(jnp.int32, (HALF, PART), 1)
        + (D * WIDE + fs * HS * D + s * SHARE)
    ) * jnp.int32(MIX[0]) + seeded
    scale = math.sqrt(INNER)
    for half, ref in enumerate((oa, ob)):
        for k in range(4):
            bit = sign_bit(e_base + jnp.int32(wrap((half * HALF * D + k * PART) * MIX[0])))
            oo[half * HALF : (half + 1) * HALF, k * PART : (k + 1) * PART] = ref[k].astype(
                F32
            ) * jnp.where(bit == 0, F32(scale), F32(-scale))

    arrived([c_crs])
    both = total_of(ck[s], [cr[yh], cy[...]])
    cot[s, HS : 2 * HS] = rotate(both[:HS].astype(BF).astype(F32), -sin).astype(BF)
    cot[s, 2 * HS : 3 * HS] = both[HS:].astype(BF)
    t_crs = remote(cot.at[s], cot.at[s], crs)
    t_sib = remote(cot.at[s], cot.at[s], sib)

    arrived([n_sib] + n_two)

    def first_term(i, carry):
        oq[:, lanes(i * TOK, TOK)] = dot(cot[s], nrm[:, lanes(s * SHARE + i * TOK, TOK)], NN)
        return carry

    lax.fori_loop(0, SHARE // TOK, first_term, 0)
    arrived([t_sib])

    def next_term(b):
        def term(i, carry):
            at = lanes(i * TOK, TOK)
            oq[:, at] += dot(cot[b], nb[b, :, at], NN)
            return carry

        lax.fori_loop(0, SHARE // TOK, term, 0)

    next_term(s_sib)
    arrived([t_crs])
    t_rel = remote(cot.at[s_crs], cot.at[s_crs], sib)
    next_term(s_crs)
    arrived([t_rel])

    def last_term(i, carry):
        at = lanes(i * TOK, TOK)
        oq[:, at] = (oq[:, at] + dot(cot[s_crd], nb[s_crd, :, at], NN)) * sgn[:, at]
        return carry

    lax.fori_loop(0, SHARE // TOK, last_term, 0)
    for copy in sent:
        copy.wait_send()


def tables():
    rate = 10000.0 ** (-2.0 * np.arange(ROT // 2) / ROT)
    rate = np.concatenate([rate, rate])[:, None]
    within = np.arange(TOK)[None, :] * rate
    blocks = np.arange(4)[:, None, None] * float(TOK) * rate[None] + np.zeros((1, 1, TOK))
    tab_t = np.stack([np.cos(within), np.sin(within)]).astype(np.float32)
    tab_b = np.stack([np.cos(blocks), np.sin(blocks)], axis=1).astype(np.float32)
    return tab_t, tab_b


def per_device(tokens, target, norm_gain, qkv_weight, out_weight, probe_seed, block_order):
    tab_t, tab_b = tables()
    anywhere = pl.BlockSpec(memory_space=pl.ANY)
    vmem = pl.BlockSpec(memory_space=pltpu.VMEM)
    smem = pl.BlockSpec(memory_space=pltpu.SMEM)
    v = pltpu.VMEM
    scratch = [
        v((TOK, D), BF), v((TOK, PART), BF), v((COLS, D), BF), v((TOK, D), BF), v((2, COLS, TOK), F32),
        v((4, TOK, SHARE), BF), v((4, 4 * HS + 16, TOK), BF),
        v((4, HALF, SHARE), BF), v((4, 4, HALF, PART), BF),
        v((4, 4, HALF, PART), BF), v((4, 4, HALF, PART), BF),
        v((4, 4, HALF, PART), BF), v((4, 4, HALF, PART), BF),
        v((2, 4, 4, HALF, TOK), BF), v((2, 4, 4, HALF, TOK), BF),
        v((TOK, 1024), F32), v((TOK, 1024), F32), v((TOK, 1024), F32), v((TOK, 1024), F32),
        v((TOK, 1024), BF), v((TOK, 1024), BF),
        v((2, TOK, PART), F32), v((2, TOK, PART), BF), v((2, TOK, PART), BF), v((2, TOK, PART), BF),
        v((2, 4, 4 * HALF, TOK), F32),
        v((2, 4, 4, HALF, TOK), BF), v((2, 4, 4, HALF, TOK), BF),
        v((2, 3, 4, HALF, TOK), BF), v((2, 3, 4, HALF, TOK), BF),
        v((2, 4, HALF, TOK), BF), v((2, 4, HALF, TOK), BF),
        v((2, 3, HALF, TOK), BF), v((2, 3, HALF, TOK), BF),
        v((4, 4, HALF, PART), BF), v((4, 4, HALF, PART), BF),
        v((2, 4, HALF, PART), BF), v((2, 4, HALF, PART), BF),
        v((4, HALF, PART), BF), v((4, HALF, PART), BF), v((4, HALF, PART), BF), v((4, HALF, PART), BF),
        v((4, HALF, PART), BF), v((4, HALF, PART), BF), v((4, HALF, PART), BF), v((4, HALF, PART), BF),
        v((4, 2 * HS, TOK), BF), v((2, 2 * HS, TOK), BF), v((2 * HS, TOK), BF), v((2 * HS, TOK), BF),
        v((4, 3 * HS, TOK), BF), v((COLS, SHARE), F32),
        pltpu.SemaphoreType.DMA((N_REMOTE,)), pltpu.SemaphoreType.DMA((N_REMOTE,)),
        pltpu.SemaphoreType.DMA((N_LOCAL,)),
    ]
    product, out_curv = pl.pallas_call(
        kernel,
        out_shape=(
            jax.ShapeDtypeStruct((COLS, SHARE), F32),
            jax.ShapeDtypeStruct((HS, SHARE), F32),
        ),
        in_specs=[anywhere, anywhere, vmem, anywhere, anywhere, smem, smem, vmem, vmem],
        out_specs=(vmem, vmem),
        scratch_shapes=scratch,
        compiler_params=pltpu.CompilerParams(
            collective_id=0, has_side_effects=True, vmem_limit_bytes=60 * 2**20
        ),
    )(
        tokens, target, norm_gain.reshape(1, D), qkv_weight.T, out_weight, probe_seed, block_order,
        jnp.asarray(tab_t), jnp.asarray(tab_b),
    )
    return product.T, out_curv


def solution(mesh):
    placed = (P("seq", None), P("seq", None), P(), P(None, "fsdp"), P("fsdp", None), P(), P("seq"))
    return jax.shard_map(
        per_device,
        mesh=mesh,
        in_specs=placed,
        out_specs=(P("seq", "fsdp"), P("fsdp", "seq")),
        check_vma=False,
    )
```

```python
import functools
import math

import jax
import jax.numpy as jnp
import numpy as np
from jax import lax
from jax.experimental import pallas as pl
from jax.experimental.pallas import tpu as pltpu
from jax.sharding import PartitionSpec as P

MESH = pl.DeviceIdType.MESH
BF = jnp.bfloat16
F32 = jnp.float32
D = 6144
HS = 96
ROT = 24
TOK = 256
COLS = 288
WIDE = 9216
INNER = 3072
SHARE = 1536
PART = 384
HALF = 48
KEYS = 2 * HS + 16
STEP = 768
MIX = (-1640531535, -2048144789, -1028477387)
N_REMOTE = 136
N_LOCAL = 16


def wrap(value):
    return ((value + 2**31) % 2**32) - 2**31


def shifted(state, places):
    return lax.shift_right_logical(state, jnp.full(state.shape, places, jnp.int32))


def sign_bit(state):
    state = state ^ shifted(state, 16)
    state = state * jnp.int32(MIX[1])
    state = state ^ shifted(state, 13)
    state = state * jnp.int32(MIX[2])
    return (state ^ shifted(state, 16)) & jnp.int32(128)


def dot(a, b, contract):
    return lax.dot_general(a, b, (contract, ((), ())), preferred_element_type=F32)


NN = ((1,), (0,))
NT = ((1,), (1,))
TN = ((0,), (0,))


def kernel(
    tok_in, tgt_in, gain, wq_in, wo_in, seed, block, tab_t, tab_b,
    oq, oo,
    tok, tgt, wq, nrm, acc,
    stat, nb, gkv,
    wt, ww, pa, pb, ga, gb,
    score, score_tan, prob, prob_tan, rnd, rnd_tan,
    mix_acc, mix_out, mix_in, grads, back_acc,
    sa, sb, ra1, rb1, sa2, sb2, ra2, rb2,
    ha, hb, ca, cb, xa, xb, ya, yb, fa, fb, oa, ob,
    cv, cvr, cvs, cvf, ck, ckr, cks, ckf, cot, sgn, part,
    send, recv, local,
):
    fs = lax.axis_index("fsdp")
    s = lax.axis_index("seq")
    x = fs // 8
    yl = (fs // 4) % 2
    z = fs % 4
    yh = s // 2
    c = s % 2
    s_sib = yh * 2 + (1 - c)
    s_crs = (1 - yh) * 2 + c
    s_crd = (1 - yh) * 2 + (1 - c)
    own_cols = (x * 4 + z) * PART

    def device(px, py, pz, ps):
        return ((px * 2 + py) * 4 + pz, ps)

    def xp(d):
        return device((x + d) % 4, yl, z, s)

    def zp(d):
        return device(x, yl, (z + d) % 4, s)

    def fin(d):
        return device(s, yl, (z + d) % 4, x)

    partner = device(x, 1 - yl, z, s)
    sib = device(x, yl, z, s_sib)
    crs = device(x, yl, z, s_crs)
    crd = device(x, yl, z, s_crd)

    count = [0]
    sent = []

    def remote(src, dst, to, begin=True):
        i = count[0]
        count[0] += 1
        copy = pltpu.make_async_remote_copy(
            src_ref=src, dst_ref=dst, send_sem=send.at[i], recv_sem=recv.at[i],
            device_id=to, device_id_type=MESH,
        )
        if begin:
            copy.start()
            sent.append(copy)
        return copy

    local_count = [0]

    def stay(src, dst):
        i = local_count[0]
        local_count[0] += 1
        copy = pltpu.make_async_copy(src, dst, local.at[i])
        copy.start()
        return copy

    def arrived(copies):
        for copy in copies:
            copy.wait_recv()

    def lanes(start, size):
        return pl.ds(pl.multiple_of(start, 128), size)

    def rows(start, size):
        return pl.ds(pl.multiple_of(start, 16), size)

    tok_load = stay(tok_in, tok)
    wq_load = stay(wq_in, wq)
    tgt_load = stay(tgt_in.at[:, lanes(own_cols, PART)], tgt)
    first, second = jnp.where(c == 0, x, z), jnp.where(c == 0, z, x)

    def column(a, k):
        return jnp.where(c == 0, a * 4 + k, k * 4 + a) * PART

    own_w = [
        stay(wo_in.at[rows(c * HALF, HALF), lanes(column(first, k), PART)], wt.at[first, k])
        for k in range(4)
    ]

    barrier = pltpu.get_barrier_semaphore()

    def greet(to):
        pl.semaphore_signal(barrier, inc=1, device_id=to, device_id_type=MESH)

    for d in (1, 2, 3):
        greet(xp(d))
        greet(zp(d))
    for to in (partner, sib, crs, crd):
        greet(to)

    @pl.when(x != s)
    def _():
        for d in range(4):
            greet(fin(d))

    tok_load.wait()

    def norm_sums(i, carry):
        at = rows(i * 16, 16)
        totals = [jnp.zeros((16, 128), F32) for _ in range(2)]
        for k in range(D // 128):
            totals[k % 2] += tok[at, k * 128 : (k + 1) * 128].astype(F32)
        stat[0, at, :] = totals[0] + totals[1]
        return carry

    lax.fori_loop(0, TOK // 16, norm_sums, 0)
    average = jnp.sum(stat[0], axis=-1, keepdims=True) * (1 / D)
    stat[0] = jnp.broadcast_to(average, (TOK, 128))

    def norm_squares(i, carry):
        at = rows(i * 16, 16)
        middle = stat[0, at, :]
        totals = [jnp.zeros((16, 128), F32) for _ in range(2)]
        for k in range(D // 128):
            centred = tok[at, k * 128 : (k + 1) * 128].astype(F32) - middle
            totals[k % 2] += centred * centred
        stat[1, at, :] = totals[0] + totals[1]
        return carry

    lax.fori_loop(0, TOK // 16, norm_squares, 0)
    spread = jnp.sum(stat[1], axis=-1, keepdims=True) * (1 / D)
    stat[1] = jnp.broadcast_to(lax.rsqrt(spread + 1e-05), (TOK, 128))

    pl.semaphore_wait(barrier, jnp.where(x != s, 14, 10))

    def along_first(d):
        return device(
            jnp.where(c == 0, (x + d) % 4, x), yl, jnp.where(c == 0, z, (z + d) % 4), s
        )

    def along_second(d):
        return device(
            jnp.where(c == 0, x, (x + d) % 4), yl, jnp.where(c == 0, (z + d) % 4, z), s
        )

    w_one = []
    for d in (1, 2, 3):
        for k in range(4):
            w_one.append(
                remote(
                    wo_in.at[rows(c * HALF, HALF), lanes(column((first + d) % 4, k), PART)],
                    wt.at[first, k], along_first(d),
                )
            )

    def norm_rows(i, carry):
        at = rows(i * 16, 16)
        middle, factor = stat[0, at, :], stat[1, at, :]
        for k in range(D // 128):
            cols = slice(k * 128, (k + 1) * 128)
            nrm[at, cols] = ((tok[at, cols].astype(F32) - middle) * factor * gain[:, cols]).astype(BF)
        return carry

    lax.fori_loop(0, TOK // 16, norm_rows, 0)

    piece = jnp.where(c == 0, z * 4 + x, x * 4 + z) * 16
    n_crs = remote(
        nrm.at[rows(piece, 16), lanes(s_crs * SHARE, SHARE)], nb.at[s, rows(piece, 16)], crs
    )
    n_crd = remote(
        nrm.at[rows(piece, 16), lanes(s_crd * SHARE, SHARE)], nb.at[s, rows(piece, 16)], crd
    )
    n_sib = remote(nrm.at[:, lanes(s_sib * SHARE, SHARE)], nb.at[s], sib)

    wq_load.wait()
    acc[...] = jnp.zeros_like(acc)
    seeded = seed[0]
    q_probe = float(np.float32(1 / math.sqrt(D)).astype(jnp.bfloat16))
    o_probe = float(np.float32(1 / math.sqrt(INNER)).astype(jnp.bfloat16))

    def project(start, size):
        q_rows = lax.broadcasted_iota(jnp.int32, (size, STEP), 1)
        q_cols = lax.broadcasted_iota(jnp.int32, (size, STEP), 0)
        q_base = (q_rows * WIDE + q_cols + (fs * COLS + start)) * jnp.int32(MIX[0]) + seeded
        to = pl.ds(start, size)

        def step(i, carry):
            at = pl.ds(pl.multiple_of(i * STEP, STEP), STEP)
            bit = sign_bit(q_base + i * jnp.int32(wrap(STEP * WIDE * MIX[0])))
            probe = jnp.where(bit == 0, F32(q_probe), F32(-q_probe)).astype(BF)
            both = dot(jnp.concatenate([wq[to, at], probe], axis=0), nrm[:, at], NT)
            acc[0, to] += both[:size]
            acc[1, to] += both[size:]
            return carry

        lax.fori_loop(0, D // STEP, step, 0)

    project(HS, 2 * HS)

    number = block[0]
    low = lax.broadcasted_iota(jnp.int32, (ROT, TOK), 0) < ROT // 2

    def trig(here):
        cos_b = jnp.zeros((ROT, TOK), F32)
        sin_b = jnp.zeros((ROT, TOK), F32)
        for k in range(4):
            cos_b = jnp.where(here == k, tab_b[k, 0], cos_b)
            sin_b = jnp.where(here == k, tab_b[k, 1], sin_b)
        cos = cos_b * tab_t[0] - sin_b * tab_t[1]
        sin = sin_b * tab_t[0] + cos_b * tab_t[1]
        return cos, jnp.where(low, -sin, sin)

    own_trig = trig(jnp.full((ROT, TOK), number, jnp.int32))

    def rotate(field, turns, sign=1.0):
        cos, sin = turns
        head = field[:ROT]
        swapped = pltpu.roll(head, ROT // 2, 0)
        return jnp.concatenate([head * cos + swapped * (sin * sign), field[ROT:]], axis=0)

    for k in range(2):
        gkv[s, k * HS : (k + 1) * HS] = rotate(acc[k, HS : 2 * HS], own_trig).astype(BF)
    gkv[s, KEYS - 16 : KEYS] = jnp.full((16, TOK), number, jnp.int32).astype(F32).astype(BF)
    k_part, v_part = pl.ds(0, KEYS), pl.ds(KEYS, 2 * HS)

    def spread_kv(slot, part, to):
        return remote(gkv.at[slot, part], gkv.at[slot, part], to)

    k_crs = spread_kv(s, k_part, crs)
    k_sib = spread_kv(s, k_part, sib)
    for k in range(2):
        gkv[s, KEYS + k * HS : KEYS + (k + 1) * HS] = acc[k, 2 * HS : 3 * HS].astype(BF)
    v_crs = spread_kv(s, v_part, crs)
    v_sib = spread_kv(s, v_part, sib)

    project(0, HS)
    q = rotate(acc[0, :HS], own_trig).astype(BF)
    q_tan = rotate(acc[1, :HS], own_trig).astype(BF)
    q_both = jnp.concatenate([q_tan, q], axis=0)

    b0 = (1 - yh) * 2
    b1 = b0 + 1
    arrived([n_crs, n_crd])
    n_one = []
    for d in (1, 2, 3):
        at0 = nb.at[b0, rows((z * 4 + x) * 16, 16)]
        at1 = nb.at[b1, rows((x * 4 + z) * 16, 16)]
        n_one.append(remote(at0, at0, xp(d)))
        n_one.append(remote(at1, at1, zp(d)))

    for copy in own_w:
        copy.wait()
    arrived(w_one)
    w_two = []
    for d in (1, 2, 3):
        w_two.append(remote(wt.at[:, (second + d) % 4], ww.at[c, second], along_second(d)))
    own_ww = stay(wt.at[:, second], ww.at[c, second])

    o_rows = lax.broadcasted_iota(jnp.int32, (HALF, PART), 0)
    o_lanes = lax.broadcasted_iota(jnp.int32, (HALF, PART), 1)
    o_base = (o_rows * D + o_lanes + (D * WIDE + own_cols)) * jnp.int32(MIX[0]) + seeded

    def probe_piece(i, carry):
        for k in range(4):
            first = ((k * 2 + yl) * 4 + i) * HS
            second = ((i * 2 + yl) * 4 + k) * HS + HALF
            bit = sign_bit(o_base + first * jnp.int32(wrap(D * MIX[0])))
            pa[i, k] = jnp.where(bit == 0, F32(o_probe), F32(-o_probe)).astype(BF)
            bit = sign_bit(o_base + second * jnp.int32(wrap(D * MIX[0])))
            pb[i, k] = jnp.where(bit == 0, F32(o_probe), F32(-o_probe)).astype(BF)
        return carry

    lax.fori_loop(0, 4, probe_piece, 0)

    arrived([k_crs])
    k_rel = spread_kv(s_crs, k_part, sib)
    arrived([v_crs])
    v_rel = spread_kv(s_crs, v_part, sib)
    own_ww.wait()
    arrived(w_two)
    w_sib = remote(ww.at[c], ww.at[c], sib)

    arrived([k_sib, k_rel])
    root = 1 / math.sqrt(HS)

    def keys_of(b):
        return lanes(b * TOK, TOK)

    def score_block(b, carry):
        score[:, keys_of(b)] = dot(q, gkv[b, 0:HS], TN) * root
        score_tan[:, keys_of(b)] = dot(q_both, gkv[b, 0 : 2 * HS], TN) * root
        return carry

    lax.fori_loop(0, 4, score_block, 0)
    along = lax.broadcasted_iota(jnp.int32, (1, TOK), 1).astype(F32)
    key_pos = jnp.concatenate(
        [gkv[b, KEYS - 16 : KEYS].astype(F32)[0:1] * float(TOK) + along for b in range(4)], axis=1
    )
    number_f = jnp.full((32, 1), number, jnp.int32).astype(F32)
    down = lax.broadcasted_iota(jnp.int32, (32, 1), 0)

    def soft_rows(i, carry):
        at = pl.ds(pl.multiple_of(i * 32, 32), 32)
        query_pos = number_f * float(TOK) + (down + i * 32).astype(F32)
        allowed = key_pos <= query_pos
        values = jnp.where(allowed, score[at, :], -1e30)
        highest = jnp.max(values, axis=-1, keepdims=True)
        weights = jnp.exp(values - highest)
        weights = weights * (1.0 / jnp.sum(weights, axis=-1, keepdims=True))
        tans = score_tan[at, :]
        moved = weights * tans
        moved = moved - weights * jnp.sum(moved, axis=-1, keepdims=True)
        prob[at, :] = weights
        prob_tan[at, :] = moved
        rnd[at, :] = weights.astype(BF)
        rnd_tan[at, :] = moved.astype(BF)
        return carry

    lax.fori_loop(0, TOK // 32, soft_rows, 0)

    def sum_blocks(term, shape):
        total = jnp.zeros(shape, F32)
        return lax.fori_loop(0, 4, lambda b, held: held + term(b), total)

    def gather_one(t):
        copies = []
        for d in (1, 2, 3):
            copies.append(remote(ga.at[t, z, x], ga.at[t, z, x], xp(d)))
            copies.append(remote(gb.at[t, x, z], gb.at[t, x, z], zp(d)))
        return copies

    def gather_two(t):
        copies = []
        for d in (1, 2, 3):
            copies.append(remote(ga.at[t, z], ga.at[t, z], zp(d)))
            copies.append(remote(gb.at[t, x], gb.at[t, x], xp(d)))
        return copies

    arrived([v_sib, v_rel])
    value_terms = sum_blocks(
        lambda b: dot(gkv[b, KEYS : KEYS + 2 * HS], rnd[:, keys_of(b)], NT), (2 * HS, TOK)
    )
    attn = value_terms[:HS].astype(BF)
    ga[0, z, x] = attn[:HALF]
    gb[0, x, z] = attn[HALF:]
    g_one = gather_one(0)
    attn_tan = (
        sum_blocks(lambda b: dot(gkv[b, KEYS : KEYS + HS], rnd_tan[:, keys_of(b)], NT), (HS, TOK))
        + value_terms[HS:]
    ).astype(BF)
    ga[1, z, x] = attn_tan[:HALF]
    gb[1, x, z] = attn_tan[HALF:]
    g_one_tan = gather_one(1)
    arrived(g_one)
    g_two = gather_two(0)
    arrived(g_one_tan)
    g_two_tan = gather_two(1)

    arrived([w_sib])
    wa, wb = ww.at[0], ww.at[1]
    arrived(g_two)

    def whole(ref, *at):
        value = ref[at]
        return value.reshape(4 * HALF, value.shape[-1])

    mix_acc[...] = jnp.zeros_like(mix_acc)

    def mix_one(i, carry):
        left, right = whole(ga, 0, i), whole(gb, 0, i)
        mix_acc[0] += dot(left, whole(wa, i), TN) + dot(right, whole(wb, i), TN)
        mix_acc[1] += dot(left, whole(pa, i), TN) + dot(right, whole(pb, i), TN)
        return carry

    lax.fori_loop(0, 4, mix_one, 0)
    mix_out[0] = mix_acc[0].astype(BF)
    m_one = remote(mix_out.at[0], mix_in.at[0], partner)
    arrived(g_two_tan)

    def mix_two(i, carry):
        mix_acc[1] += dot(whole(ga, 1, i), whole(wa, i), TN) + dot(whole(gb, 1, i), whole(wb, i), TN)
        return carry

    lax.fori_loop(0, 4, mix_two, 0)
    mix_out[1] = mix_acc[1].astype(BF)
    m_two = remote(mix_out.at[1], mix_in.at[1], partner)

    s_base = (
        (lax.broadcasted_iota(jnp.int32, (COLS, TOK), 1) + s * SHARE) * WIDE
        + lax.broadcasted_iota(jnp.int32, (COLS, TOK), 0)
        + fs * COLS
    ) * jnp.int32(MIX[0]) + seeded

    def sign_cols(i, carry):
        bit = sign_bit(s_base + i * jnp.int32(wrap(TOK * WIDE * MIX[0])))
        sgn[:, lanes(i * TOK, TOK)] = jnp.where(bit == 0, F32(math.sqrt(D)), F32(-math.sqrt(D)))
        return carry

    lax.fori_loop(0, SHARE // TOK, sign_cols, 0)

    tgt_load.wait()
    arrived([m_one])
    resid = tok[:, lanes(own_cols, PART)].astype(F32) - tgt[...].astype(F32)
    resid = resid + (mix_acc[0] + mix_in[0].astype(F32))
    grads[0] = (resid * (1 / 1024)).astype(BF)

    def back_one(i, carry):
        grad = grads[0]
        sa[0, i] = dot(whole(wa, i), grad, NT).astype(BF).reshape(4, HALF, TOK)
        sb[0, i] = dot(whole(wb, i), grad, NT).astype(BF).reshape(4, HALF, TOK)
        back_acc[0, i] = dot(whole(pa, i), grad, NT)
        back_acc[1, i] = dot(whole(pb, i), grad, NT)
        return carry

    lax.fori_loop(0, 4, back_one, 0)

    def scatter_one(t):
        copies = []
        for d in (1, 2, 3):
            copies.append(remote(sa.at[t, (z + d) % 4], ra1.at[t, d - 1], zp(d)))
            copies.append(remote(sb.at[t, (x + d) % 4], rb1.at[t, d - 1], xp(d)))
        return copies

    def total_of(own, others):
        total = own.astype(F32)
        for other in others:
            total = total + other.astype(F32)
        return total

    def scatter_two(t):
        sa2[t] = total_of(sa[t, z], [ra1[t, k] for k in range(3)]).astype(BF)
        sb2[t] = total_of(sb[t, x], [rb1[t, k] for k in range(3)]).astype(BF)
        copies = []
        for d in (1, 2, 3):
            copies.append(remote(sa2.at[t, (x + d) % 4], ra2.at[t, d - 1], xp(d)))
            copies.append(remote(sb2.at[t, (z + d) % 4], rb2.at[t, d - 1], zp(d)))
        return copies

    def scattered(t):
        first = total_of(sa2[t, x], [ra2[t, k] for k in range(3)])
        second = total_of(sb2[t, z], [rb2[t, k] for k in range(3)])
        return jnp.concatenate([first.astype(BF), second.astype(BF)], axis=0)

    r_one = scatter_one(0)
    arrived([m_two])
    grads[1] = ((mix_acc[1] + mix_in[1].astype(F32)) * (1 / 1024)).astype(BF)

    def back_two(i, carry):
        grad = grads[1]
        sa[1, i] = (dot(whole(wa, i), grad, NT) + back_acc[0, i]).astype(BF).reshape(4, HALF, TOK)
        sb[1, i] = (dot(whole(wb, i), grad, NT) + back_acc[1, i]).astype(BF).reshape(4, HALF, TOK)
        return carry

    lax.fori_loop(0, 4, back_two, 0)
    r_one_tan = scatter_one(1)

    def out_terms(i, carry):
        one, two = grads[0], grads[1]
        ha[i] = (
            (dot(whole(ga, 1, i), one, NN) + dot(whole(ga, 0, i), two, NN))
            .astype(BF).reshape(4, HALF, PART)
        )
        hb[i] = (
            (dot(whole(gb, 1, i), one, NN) + dot(whole(gb, 0, i), two, NN))
            .astype(BF).reshape(4, HALF, PART)
        )
        return carry

    lax.fori_loop(0, 4, out_terms, 0)
    o_core = []
    for k in range(2):
        o_core.append(remote(ha.at[:, 2 * k + 1 - c], ca.at[k], sib))
        o_core.append(remote(hb.at[2 * k + 1 - c], cb.at[k], sib))
    arrived(r_one)
    r_two = scatter_two(0)

    arrived(o_core)
    far = 1 - yh
    xa[...] = total_of(ha[:, 2 * far + c], [ca[far]]).astype(BF)
    xb[...] = total_of(hb[2 * far + c], [cb[far]]).astype(BF)
    o_crs = [remote(xa, ya, crs), remote(xb, yb, crs)]

    arrived(r_one_tan)
    r_two_tan = scatter_two(1)

    arrived(r_two)
    g = scattered(0)

    def pull_block(b, carry):
        score[:, keys_of(b)] = dot(g, gkv[b, KEYS : KEYS + HS], TN)
        return carry

    lax.fori_loop(0, 4, pull_block, 0)
    arrived(r_two_tan)
    arrived(n_one)
    n_two = []
    for d in (1, 2, 3):
        at0 = nb.at[b0, rows(z * 64, 64)]
        at1 = nb.at[b1, rows(x * 64, 64)]
        n_two.append(remote(at0, at0, zp(d)))
        n_two.append(remote(at1, at1, xp(d)))
    g_tan = scattered(1)
    g_both = jnp.concatenate([g_tan, g], axis=0)

    def value_block(b, carry):
        at = keys_of(b)
        cv[b] = (dot(g, rnd_tan[:, at], NN) + dot(g_tan, rnd[:, at], NN)).astype(BF)
        return carry

    lax.fori_loop(0, 4, value_block, 0)
    v_core = [remote(cv.at[2 * k + 1 - c], cvr.at[k], sib) for k in range(2)]

    def pull_block_tan(b, carry):
        score_tan[:, keys_of(b)] = dot(g_both, gkv[b, KEYS : KEYS + 2 * HS], TN)
        return carry

    lax.fori_loop(0, 4, pull_block_tan, 0)

    def chip_sums(own, other, kept):
        for k in range(2):
            kept[k] = total_of(own[2 * k + c], [other[k]]).astype(BF)

    arrived(v_core)
    chip_sums(cv, cvr, cvs)
    v_far = remote(cvs, cvf, crs)

    def soft_back(i, carry):
        at = pl.ds(pl.multiple_of(i * 32, 32), 32)
        weights, moved = prob[at, :], prob_tan[at, :]
        pulled, pulled_tan = score[at, :], score_tan[at, :]
        base = jnp.sum(weights * pulled, axis=-1, keepdims=True)
        base_tan = jnp.sum(moved * pulled + weights * pulled_tan, axis=-1, keepdims=True)
        less = pulled - base
        score[at, :] = weights * less
        score_tan[at, :] = moved * less + weights * (pulled_tan - base_tan)
        return carry

    lax.fori_loop(0, TOK // 32, soft_back, 0)

    def key_block(b, carry):
        at = keys_of(b)
        slope, slope_tan = score[:, at].astype(BF), score_tan[:, at].astype(BF)
        ck[b] = ((dot(q, slope_tan, NN) + dot(q_tan, slope, NN)) * root).astype(BF)
        return carry

    lax.fori_loop(0, 4, key_block, 0)

    k_core = [remote(ck.at[2 * k + 1 - c], ckr.at[k], sib) for k in range(2)]

    def query_block(b, held):
        at = keys_of(b)
        slope, slope_tan = score[:, at].astype(BF), score_tan[:, at].astype(BF)
        return held + dot(gkv[b, 0:HS], slope_tan, NT) + dot(gkv[b, HS : 2 * HS], slope, NT)

    cot_query = lax.fori_loop(0, 4, query_block, jnp.zeros((HS, TOK), F32)) * root
    cot[s, 0:HS] = rotate(cot_query.astype(BF).astype(F32), own_trig, -1.0).astype(BF)
    q_far = remote(cot.at[s, pl.ds(0, HS)], cot.at[s, pl.ds(0, HS)], crs)
    arrived(k_core)
    chip_sums(ck, ckr, cks)
    k_far = remote(cks, ckf, crs)

    arrived(o_crs)
    fa[...] = total_of(ha[:, s], [ca[yh], ya[...]]).astype(BF)
    fb[...] = total_of(hb[s], [cb[yh], yb[...]]).astype(BF)
    o_fin = []
    for d in (1, 2, 3):
        other = (z + d) % 4
        o_fin.append(remote(fa.at[other], oa.at[z], fin(d)))
        o_fin.append(remote(fb.at[other], ob.at[z], fin(d)))
    o_far = [
        remote(fa.at[z], oa.at[z], fin(0), begin=False),
        remote(fb.at[z], ob.at[z], fin(0), begin=False),
    ]
    near = local_count[0]
    o_near = [
        pltpu.make_async_copy(fa.at[z], oa.at[z], local.at[near]),
        pltpu.make_async_copy(fb.at[z], ob.at[z], local.at[near + 1]),
    ]

    @pl.when(x != s)
    def _():
        for copy in o_far:
            copy.start()

    @pl.when(x == s)
    def _():
        for copy in o_near:
            copy.start()

    arrived([v_far])
    for k in range(2):
        cot[2 * k + c, 2 * HS : 3 * HS] = total_of(cvs[k], [cvf[k]]).astype(BF)
    turns = [
        trig(jnp.broadcast_to(gkv[2 * k + c, KEYS - 16 : KEYS].astype(F32)[0:1], (ROT, TOK)))
        for k in range(2)
    ]
    arrived([k_far])
    for k in range(2):
        both = total_of(cks[k], [ckf[k]]).astype(BF).astype(F32)
        cot[2 * k + c, HS : 2 * HS] = rotate(both, turns[k], -1.0).astype(BF)
    arrived([q_far])
    t_sib = [remote(cot.at[2 * k + c], cot.at[2 * k + c], sib) for k in range(2)]
    arrived([n_sib] + n_two)

    def first_terms(i, carry):
        at = lanes(i * TOK, TOK)
        part[:, at] = dot(cot[s], nrm[:, lanes(s * SHARE + i * TOK, TOK)], NN) + dot(
            cot[s_crs], nb[s_crs, :, at], NN
        )
        return carry

    lax.fori_loop(0, SHARE // TOK, first_terms, 0)
    arrived(o_fin)

    @pl.when(x != s)
    def _():
        for copy in o_far:
            copy.wait_recv()
            copy.wait_send()

    @pl.when(x == s)
    def _():
        for copy in o_near:
            copy.wait()

    e_base = (
        lax.broadcasted_iota(jnp.int32, (HALF, PART), 0) * D
        + lax.broadcasted_iota(jnp.int32, (HALF, PART), 1)
        + (D * WIDE + fs * HS * D + s * SHARE)
    ) * jnp.int32(MIX[0]) + seeded
    scale = math.sqrt(INNER)
    for half, ref in enumerate((oa, ob)):
        for k in range(4):
            bit = sign_bit(e_base + jnp.int32(wrap((half * HALF * D + k * PART) * MIX[0])))
            oo[half * HALF : (half + 1) * HALF, k * PART : (k + 1) * PART] = (
                ref[k].astype(F32) * jnp.where(bit == 0, F32(scale), F32(-scale))
            ).astype(BF)


    arrived(t_sib)

    def last_terms(i, carry):
        at = lanes(i * TOK, TOK)
        total = part[:, at] + (dot(cot[s_sib], nb[s_sib, :, at], NN) + dot(cot[s_crd], nb[s_crd, :, at], NN))
        oq[:, at] = (total * sgn[:, at]).astype(BF)
        return carry

    lax.fori_loop(0, SHARE // TOK, last_terms, 0)

    for copy in sent:
        copy.wait_send()


def tables():
    rate = 10000.0 ** (-2.0 * np.arange(ROT // 2) / ROT)
    rate = np.concatenate([rate, rate])[:, None]
    within = np.arange(TOK)[None, :] * rate
    blocks = np.arange(4)[:, None, None] * float(TOK) * rate[None] + np.zeros((1, 1, TOK))
    tab_t = np.stack([np.cos(within), np.sin(within)]).astype(np.float32)
    tab_b = np.stack([np.cos(blocks), np.sin(blocks)], axis=1).astype(np.float32)
    return tab_t, tab_b


def per_device(tokens, target, norm_gain, qkv_weight, out_weight, probe_seed, block_order):
    tab_t, tab_b = tables()
    anywhere = pl.BlockSpec(memory_space=pl.ANY)
    vmem = pl.BlockSpec(memory_space=pltpu.VMEM)
    smem = pl.BlockSpec(memory_space=pltpu.SMEM)
    v = pltpu.VMEM
    scratch = [
        v((TOK, D), BF), v((TOK, PART), BF), v((COLS, D), BF), v((TOK, D), BF), v((2, COLS, TOK), F32),
        v((2, TOK, 128), F32), v((4, TOK, SHARE), BF), v((4, 4 * HS + 16, TOK), BF),
        v((4, 4, HALF, PART), BF), v((2, 4, 4, HALF, PART), BF),
        v((4, 4, HALF, PART), BF), v((4, 4, HALF, PART), BF),
        v((2, 4, 4, HALF, TOK), BF), v((2, 4, 4, HALF, TOK), BF),
        v((TOK, 1024), F32), v((TOK, 1024), F32), v((TOK, 1024), F32), v((TOK, 1024), F32),
        v((TOK, 1024), BF), v((TOK, 1024), BF),
        v((2, TOK, PART), F32), v((2, TOK, PART), BF), v((2, TOK, PART), BF), v((2, TOK, PART), BF),
        v((2, 4, 4 * HALF, TOK), F32),
        v((2, 4, 4, HALF, TOK), BF), v((2, 4, 4, HALF, TOK), BF),
        v((2, 3, 4, HALF, TOK), BF), v((2, 3, 4, HALF, TOK), BF),
        v((2, 4, HALF, TOK), BF), v((2, 4, HALF, TOK), BF),
        v((2, 3, HALF, TOK), BF), v((2, 3, HALF, TOK), BF),
        v((4, 4, HALF, PART), BF), v((4, 4, HALF, PART), BF),
        v((2, 4, HALF, PART), BF), v((2, 4, HALF, PART), BF),
        v((4, HALF, PART), BF), v((4, HALF, PART), BF), v((4, HALF, PART), BF), v((4, HALF, PART), BF),
        v((4, HALF, PART), BF), v((4, HALF, PART), BF), v((4, HALF, PART), BF), v((4, HALF, PART), BF),
        v((4, HS, TOK), BF), v((2, HS, TOK), BF), v((2, HS, TOK), BF), v((2, HS, TOK), BF),
        v((4, HS, TOK), BF), v((2, HS, TOK), BF), v((2, HS, TOK), BF), v((2, HS, TOK), BF),
        v((4, 3 * HS, TOK), BF), v((COLS, SHARE), F32), v((COLS, SHARE), F32),
        pltpu.SemaphoreType.DMA((N_REMOTE,)), pltpu.SemaphoreType.DMA((N_REMOTE,)),
        pltpu.SemaphoreType.DMA((N_LOCAL,)),
    ]
    product, out_curv = pl.pallas_call(
        kernel,
        out_shape=(
            jax.ShapeDtypeStruct((COLS, SHARE), BF),
            jax.ShapeDtypeStruct((HS, SHARE), BF),
        ),
        in_specs=[anywhere, anywhere, vmem, anywhere, anywhere, smem, smem, vmem, vmem],
        out_specs=(vmem, vmem),
        scratch_shapes=scratch,
        compiler_params=pltpu.CompilerParams(
            collective_id=0, has_side_effects=True, vmem_limit_bytes=60 * 2**20
        ),
    )(
        tokens, target, norm_gain.reshape(1, D), qkv_weight.T, out_weight, probe_seed, block_order,
        jnp.asarray(tab_t), jnp.asarray(tab_b),
    )
    return product.astype(F32).T, out_curv.astype(F32)


def solution(mesh):
    placed = (P("seq", None), P("seq", None), P(), P(None, "fsdp"), P("fsdp", None), P(), P("seq"))
    return jax.shard_map(
        per_device,
        mesh=mesh,
        in_specs=placed,
        out_specs=(P("seq", "fsdp"), P("fsdp", "seq")),
        check_vma=False,
    )
```

```python
import functools
import math

import jax
import jax.numpy as jnp
import numpy as np
from jax import lax
from jax.experimental import pallas as pl
from jax.experimental.pallas import tpu as pltpu
from jax.sharding import PartitionSpec as P

MESH = pl.DeviceIdType.MESH
BF = jnp.bfloat16
F32 = jnp.float32
D = 6144
HS = 96
ROT = 24
TOK = 256
COLS = 288
WIDE = 9216
INNER = 3072
SHARE = 1536
PART = 384
HALF = 48
SPAN = 128
KEYS = 2 * HS + 16
STEP = 768
MIX = (-1640531535, -2048144789, -1028477387)
N_REMOTE = 168
N_LOCAL = 16


def wrap(value):
    return ((value + 2**31) % 2**32) - 2**31


def shifted(state, places):
    return lax.shift_right_logical(state, jnp.full(state.shape, places, jnp.int32))


def sign_bit(state):
    state = state ^ shifted(state, 16)
    state = state * jnp.int32(MIX[1])
    state = state ^ shifted(state, 13)
    state = state * jnp.int32(MIX[2])
    return (state ^ shifted(state, 16)) & jnp.int32(128)


def dot(a, b, contract):
    return lax.dot_general(a, b, (contract, ((), ())), preferred_element_type=F32)


NN = ((1,), (0,))
NT = ((1,), (1,))
TN = ((0,), (0,))


def kernel(
    tok_in, tgt_in, gain, wq_in, wo_in, seed, block, tab_t, tab_b,
    oq, oo,
    tok, tgt, wq, nrm, acc,
    stat, nb, gkv,
    wt, ww, pa, pb, ga, gb,
    score, score_tan, prob, prob_tan, rnd, rnd_tan, slope, slope_tan, cv_acc, ck_acc,
    mix_acc, mix_out, mix_in, grads, back_acc,
    sa, sb, ra1, rb1, sa2, sb2, ra2, rb2,
    ha, hb, ca, cb, xa, xb, ya, yb, fa, fb, oa, ob,
    cv, cvr, cvs, cvf, ck, ckr, cks, ckf, cot, sgn, part,
    send, recv, local,
):
    fs = lax.axis_index("fsdp")
    s = lax.axis_index("seq")
    x = fs // 8
    yl = (fs // 4) % 2
    z = fs % 4
    yh = s // 2
    c = s % 2
    s_sib = yh * 2 + (1 - c)
    s_crs = (1 - yh) * 2 + c
    s_crd = (1 - yh) * 2 + (1 - c)
    own_cols = (x * 4 + z) * PART

    def device(px, py, pz, ps):
        return ((px * 2 + py) * 4 + pz, ps)

    def xp(d):
        return device((x + d) % 4, yl, z, s)

    def zp(d):
        return device(x, yl, (z + d) % 4, s)

    def fin(d):
        return device(s, yl, (z + d) % 4, x)

    partner = device(x, 1 - yl, z, s)
    sib = device(x, yl, z, s_sib)
    crs = device(x, yl, z, s_crs)
    crd = device(x, yl, z, s_crd)

    count = [0]
    sent = []

    def remote(src, dst, to, begin=True):
        i = count[0]
        count[0] += 1
        copy = pltpu.make_async_remote_copy(
            src_ref=src, dst_ref=dst, send_sem=send.at[i], recv_sem=recv.at[i],
            device_id=to, device_id_type=MESH,
        )
        if begin:
            copy.start()
            sent.append(copy)
        return copy

    local_count = [0]

    def stay(src, dst):
        i = local_count[0]
        local_count[0] += 1
        copy = pltpu.make_async_copy(src, dst, local.at[i])
        copy.start()
        return copy

    def arrived(copies):
        for copy in copies:
            copy.wait_recv()

    def lanes(start, size):
        return pl.ds(pl.multiple_of(start, 128), size)

    def rows(start, size):
        return pl.ds(pl.multiple_of(start, 16), size)

    tok_load = stay(tok_in, tok)
    wq_load = stay(wq_in, wq)
    tgt_load = stay(tgt_in.at[:, lanes(own_cols, PART)], tgt)
    first, second = jnp.where(c == 0, x, z), jnp.where(c == 0, z, x)

    def column(a, k):
        return jnp.where(c == 0, a * 4 + k, k * 4 + a) * PART

    own_w = [
        stay(wo_in.at[rows(c * HALF, HALF), lanes(column(first, k), PART)], wt.at[first, k])
        for k in range(4)
    ]

    barrier = pltpu.get_barrier_semaphore()

    def greet(to):
        pl.semaphore_signal(barrier, inc=1, device_id=to, device_id_type=MESH)

    for d in (1, 2, 3):
        greet(xp(d))
        greet(zp(d))
    for to in (partner, sib, crs, crd):
        greet(to)

    @pl.when(x != s)
    def _():
        for d in range(4):
            greet(fin(d))

    tok_load.wait()

    def norm_sums(i, carry):
        at = rows(i * 16, 16)
        totals = [jnp.zeros((16, 128), F32) for _ in range(2)]
        for k in range(D // 128):
            totals[k % 2] += tok[at, k * 128 : (k + 1) * 128].astype(F32)
        stat[0, at, :] = totals[0] + totals[1]
        return carry

    lax.fori_loop(0, TOK // 16, norm_sums, 0)
    average = jnp.sum(stat[0], axis=-1, keepdims=True) * (1 / D)
    stat[0] = jnp.broadcast_to(average, (TOK, 128))

    def norm_squares(i, carry):
        at = rows(i * 16, 16)
        middle = stat[0, at, :]
        totals = [jnp.zeros((16, 128), F32) for _ in range(2)]
        for k in range(D // 128):
            centred = tok[at, k * 128 : (k + 1) * 128].astype(F32) - middle
            totals[k % 2] += centred * centred
        stat[1, at, :] = totals[0] + totals[1]
        return carry

    lax.fori_loop(0, TOK // 16, norm_squares, 0)
    spread = jnp.sum(stat[1], axis=-1, keepdims=True) * (1 / D)
    stat[1] = jnp.broadcast_to(lax.rsqrt(spread + 1e-05), (TOK, 128))

    pl.semaphore_wait(barrier, jnp.where(x != s, 14, 10))

    def along_first(d):
        return device(
            jnp.where(c == 0, (x + d) % 4, x), yl, jnp.where(c == 0, z, (z + d) % 4), s
        )

    def along_second(d):
        return device(
            jnp.where(c == 0, x, (x + d) % 4), yl, jnp.where(c == 0, (z + d) % 4, z), s
        )

    w_one = []
    for d in (1, 2, 3):
        for k in range(4):
            w_one.append(
                remote(
                    wo_in.at[rows(c * HALF, HALF), lanes(column((first + d) % 4, k), PART)],
                    wt.at[first, k], along_first(d),
                )
            )

    def norm_rows(i, carry):
        at = rows(i * 16, 16)
        middle, factor = stat[0, at, :], stat[1, at, :]
        for k in range(D // 128):
            cols = slice(k * 128, (k + 1) * 128)
            nrm[at, cols] = ((tok[at, cols].astype(F32) - middle) * factor * gain[:, cols]).astype(BF)
        return carry

    lax.fori_loop(0, TOK // 16, norm_rows, 0)

    piece = jnp.where(c == 0, z * 4 + x, x * 4 + z) * 16
    n_crs = remote(
        nrm.at[rows(piece, 16), lanes(s_crs * SHARE, SHARE)], nb.at[s, rows(piece, 16)], crs
    )
    n_crd = remote(
        nrm.at[rows(piece, 16), lanes(s_crd * SHARE, SHARE)], nb.at[s, rows(piece, 16)], crd
    )
    n_sib = remote(nrm.at[:, lanes(s_sib * SHARE, SHARE)], nb.at[s], sib)

    wq_load.wait()
    acc[...] = jnp.zeros_like(acc)
    seeded = seed[0]
    q_probe = float(np.float32(1 / math.sqrt(D)).astype(jnp.bfloat16))
    o_probe = float(np.float32(1 / math.sqrt(INNER)).astype(jnp.bfloat16))

    def project(start, size):
        q_rows = lax.broadcasted_iota(jnp.int32, (size, STEP), 1)
        q_cols = lax.broadcasted_iota(jnp.int32, (size, STEP), 0)
        q_base = (q_rows * WIDE + q_cols + (fs * COLS + start)) * jnp.int32(MIX[0]) + seeded
        to = pl.ds(start, size)

        def step(i, carry):
            at = pl.ds(pl.multiple_of(i * STEP, STEP), STEP)
            bit = sign_bit(q_base + i * jnp.int32(wrap(STEP * WIDE * MIX[0])))
            probe = jnp.where(bit == 0, F32(q_probe), F32(-q_probe)).astype(BF)
            both = dot(jnp.concatenate([wq[to, at], probe], axis=0), nrm[:, at], NT)
            acc[0, to] += both[:size]
            acc[1, to] += both[size:]
            return carry

        lax.fori_loop(0, D // STEP, step, 0)

    project(HS, 2 * HS)

    number = block[0]
    low = lax.broadcasted_iota(jnp.int32, (ROT, TOK), 0) < ROT // 2

    def trig(here):
        cos_b = jnp.zeros((ROT, TOK), F32)
        sin_b = jnp.zeros((ROT, TOK), F32)
        for k in range(4):
            cos_b = jnp.where(here == k, tab_b[k, 0], cos_b)
            sin_b = jnp.where(here == k, tab_b[k, 1], sin_b)
        cos = cos_b * tab_t[0] - sin_b * tab_t[1]
        sin = sin_b * tab_t[0] + cos_b * tab_t[1]
        return cos, jnp.where(low, -sin, sin)

    own_trig = trig(jnp.full((ROT, TOK), number, jnp.int32))

    def rotate(field, turns, sign=1.0):
        cos, sin = turns
        head = field[:ROT]
        swapped = pltpu.roll(head, ROT // 2, 0)
        return jnp.concatenate([head * cos + swapped * (sin * sign), field[ROT:]], axis=0)

    for k in range(2):
        gkv[s, k * HS : (k + 1) * HS] = rotate(acc[k, HS : 2 * HS], own_trig).astype(BF)
    gkv[s, KEYS - 16 : KEYS] = jnp.full((16, TOK), number, jnp.int32).astype(F32).astype(BF)
    k_part, v_part = pl.ds(0, KEYS), pl.ds(KEYS, 2 * HS)

    def spread_kv(slot, part, to):
        return remote(gkv.at[slot, part], gkv.at[slot, part], to)

    k_crs = spread_kv(s, k_part, crs)
    k_sib = spread_kv(s, k_part, sib)
    for k in range(2):
        gkv[s, KEYS + k * HS : KEYS + (k + 1) * HS] = acc[k, 2 * HS : 3 * HS].astype(BF)
    v_crs = spread_kv(s, v_part, crs)
    v_sib = spread_kv(s, v_part, sib)

    project(0, HS)
    q = rotate(acc[0, :HS], own_trig).astype(BF)
    q_tan = rotate(acc[1, :HS], own_trig).astype(BF)
    q_both = jnp.concatenate([q_tan, q], axis=0)

    b0 = (1 - yh) * 2
    b1 = b0 + 1
    arrived([n_crs, n_crd])
    n_one = []
    for d in (1, 2, 3):
        at0 = nb.at[b0, rows((z * 4 + x) * 16, 16)]
        at1 = nb.at[b1, rows((x * 4 + z) * 16, 16)]
        n_one.append(remote(at0, at0, xp(d)))
        n_one.append(remote(at1, at1, zp(d)))

    for copy in own_w:
        copy.wait()
    arrived(w_one)
    w_two = []
    for d in (1, 2, 3):
        w_two.append(remote(wt.at[:, (second + d) % 4], ww.at[c, second], along_second(d)))
    own_ww = stay(wt.at[:, second], ww.at[c, second])

    o_rows = lax.broadcasted_iota(jnp.int32, (HALF, PART), 0)
    o_lanes = lax.broadcasted_iota(jnp.int32, (HALF, PART), 1)
    o_base = (o_rows * D + o_lanes + (D * WIDE + own_cols)) * jnp.int32(MIX[0]) + seeded

    def probe_piece(i, carry):
        for k in range(4):
            first = ((k * 2 + yl) * 4 + i) * HS
            second = ((i * 2 + yl) * 4 + k) * HS + HALF
            bit = sign_bit(o_base + first * jnp.int32(wrap(D * MIX[0])))
            pa[i, k] = jnp.where(bit == 0, F32(o_probe), F32(-o_probe)).astype(BF)
            bit = sign_bit(o_base + second * jnp.int32(wrap(D * MIX[0])))
            pb[i, k] = jnp.where(bit == 0, F32(o_probe), F32(-o_probe)).astype(BF)
        return carry

    lax.fori_loop(0, 4, probe_piece, 0)

    arrived([k_crs])
    k_rel = spread_kv(s_crs, k_part, sib)
    arrived([v_crs])
    v_rel = spread_kv(s_crs, v_part, sib)
    own_ww.wait()
    arrived(w_two)
    w_sib = remote(ww.at[c], ww.at[c], sib)

    arrived([k_sib, k_rel])
    root = 1 / math.sqrt(HS)

    def keys_of(b):
        return lanes(b * TOK, TOK)

    def span(h):
        return slice(h * SPAN, (h + 1) * SPAN)

    def score_blocks(h):
        left, left_both = q[:, span(h)], q_both[:, span(h)]

        def score_block(b, carry):
            score[span(h), keys_of(b)] = dot(left, gkv[b, 0:HS], TN) * root
            score_tan[span(h), keys_of(b)] = dot(left_both, gkv[b, 0 : 2 * HS], TN) * root
            return carry

        lax.fori_loop(0, 4, score_block, 0)

    along = lax.broadcasted_iota(jnp.int32, (1, TOK), 1).astype(F32)
    key_pos = jnp.concatenate(
        [gkv[b, KEYS - 16 : KEYS].astype(F32)[0:1] * float(TOK) + along for b in range(4)], axis=1
    )
    number_f = jnp.full((32, 1), number, jnp.int32).astype(F32)
    down = lax.broadcasted_iota(jnp.int32, (32, 1), 0)

    def soft_rows(i, carry):
        at = pl.ds(pl.multiple_of(i * 32, 32), 32)
        query_pos = number_f * float(TOK) + (down + i * 32).astype(F32)
        allowed = key_pos <= query_pos
        values = jnp.where(allowed, score[at, :], -1e30)
        highest = jnp.max(values, axis=-1, keepdims=True)
        weights = jnp.exp(values - highest)
        weights = weights * (1.0 / jnp.sum(weights, axis=-1, keepdims=True))
        tans = score_tan[at, :]
        moved = weights * tans
        moved = moved - weights * jnp.sum(moved, axis=-1, keepdims=True)
        prob[at, :] = weights
        prob_tan[at, :] = moved
        rnd[at, :] = weights.astype(BF)
        rnd_tan[at, :] = moved.astype(BF)
        return carry

    def soft(h):
        lax.fori_loop(h * SPAN // 32, (h + 1) * SPAN // 32, soft_rows, 0)


    def sum_blocks(term, shape):
        total = jnp.zeros(shape, F32)
        return lax.fori_loop(0, 4, lambda b, held: held + term(b), total)

    def gather_one(h, t):
        copies = []
        for d in (1, 2, 3):
            copies.append(remote(ga.at[h, t, z, x], ga.at[h, t, z, x], xp(d)))
            copies.append(remote(gb.at[h, t, x, z], gb.at[h, t, x, z], zp(d)))
        return copies

    def gather_two(h, t):
        copies = []
        for d in (1, 2, 3):
            copies.append(remote(ga.at[h, t, z], ga.at[h, t, z], zp(d)))
            copies.append(remote(gb.at[h, t, x], gb.at[h, t, x], xp(d)))
        return copies

    def attn_products(h):
        terms = sum_blocks(
            lambda b: dot(gkv[b, KEYS : KEYS + 2 * HS], rnd[span(h), keys_of(b)], NT), (2 * HS, SPAN)
        )
        attn = terms[:HS].astype(BF)
        ga[h, 0, z, x] = attn[:HALF]
        gb[h, 0, x, z] = attn[HALF:]
        one = gather_one(h, 0)
        attn_tan = (
            sum_blocks(
                lambda b: dot(gkv[b, KEYS : KEYS + HS], rnd_tan[span(h), keys_of(b)], NT), (HS, SPAN)
            )
            + terms[HS:]
        ).astype(BF)
        ga[h, 1, z, x] = attn_tan[:HALF]
        gb[h, 1, x, z] = attn_tan[HALF:]
        return one, gather_one(h, 1)

    score_blocks(0)
    soft(0)
    arrived([v_sib, v_rel])
    g_one = [attn_products(0)]
    score_blocks(1)
    soft(1)

    g_two = []
    for h in range(2):
        if h == 1:
            g_one.append(attn_products(1))
        pair = []
        for t in range(2):
            arrived(g_one[h][t])
            pair.append(gather_two(h, t))
        g_two.append(pair)

    arrived([w_sib])
    wa, wb = ww.at[0], ww.at[1]

    def whole(ref, *at):
        value = ref[at]
        return value.reshape(4 * HALF, value.shape[-1])

    mix_acc[...] = jnp.zeros_like(mix_acc)

    def mix_one(h):
        def step(i, carry):
            left, right = whole(ga, h, 0, i), whole(gb, h, 0, i)
            mix_acc[h, 0] += dot(left, whole(wa, i), TN) + dot(right, whole(wb, i), TN)
            mix_acc[h, 1] += dot(left, whole(pa, i), TN) + dot(right, whole(pb, i), TN)
            return carry

        arrived(g_two[h][0])
        lax.fori_loop(0, 4, step, 0)
        mix_out[h, 0] = mix_acc[h, 0].astype(BF)
        return remote(mix_out.at[h, 0], mix_in.at[h, 0], partner)

    def mix_two(h):
        def step(i, carry):
            mix_acc[h, 1] += dot(whole(ga, h, 1, i), whole(wa, i), TN) + dot(
                whole(gb, h, 1, i), whole(wb, i), TN
            )
            return carry

        arrived(g_two[h][1])
        lax.fori_loop(0, 4, step, 0)
        mix_out[h, 1] = mix_acc[h, 1].astype(BF)
        return remote(mix_out.at[h, 1], mix_in.at[h, 1], partner)

    m_one = [mix_one(0)]
    m_two = [mix_two(0)]
    m_one.append(mix_one(1))

    s_base = (
        (lax.broadcasted_iota(jnp.int32, (COLS, TOK), 1) + s * SHARE) * WIDE
        + lax.broadcasted_iota(jnp.int32, (COLS, TOK), 0)
        + fs * COLS
    ) * jnp.int32(MIX[0]) + seeded

    def sign_cols(i, carry):
        bit = sign_bit(s_base + i * jnp.int32(wrap(TOK * WIDE * MIX[0])))
        sgn[:, lanes(i * TOK, TOK)] = jnp.where(bit == 0, F32(math.sqrt(D)), F32(-math.sqrt(D)))
        return carry

    lax.fori_loop(0, SHARE // TOK, sign_cols, 0)

    tgt_load.wait()

    def scatter_one(h, t):
        copies = []
        for d in (1, 2, 3):
            copies.append(remote(sa.at[h, t, (z + d) % 4], ra1.at[h, t, d - 1], zp(d)))
            copies.append(remote(sb.at[h, t, (x + d) % 4], rb1.at[h, t, d - 1], xp(d)))
        return copies

    def back_one(h):
        arrived([m_one[h]])
        resid = tok[span(h), lanes(own_cols, PART)].astype(F32) - tgt[span(h), :].astype(F32)
        resid = resid + (mix_acc[h, 0] + mix_in[h, 0].astype(F32))
        grads[0, span(h)] = (resid * (1 / 1024)).astype(BF)

        def step(i, carry):
            grad = grads[0, span(h)]
            sa[h, 0, i] = dot(whole(wa, i), grad, NT).astype(BF).reshape(4, HALF, SPAN)
            sb[h, 0, i] = dot(whole(wb, i), grad, NT).astype(BF).reshape(4, HALF, SPAN)
            return carry

        lax.fori_loop(0, 4, step, 0)
        copies = scatter_one(h, 0)

        def probe_step(i, carry):
            grad = grads[0, span(h)]
            back_acc[h, 0, i] = dot(whole(pa, i), grad, NT)
            back_acc[h, 1, i] = dot(whole(pb, i), grad, NT)
            return carry

        lax.fori_loop(0, 4, probe_step, 0)
        return copies

    def back_two(h):
        arrived([m_two[h]])
        grads[1, span(h)] = ((mix_acc[h, 1] + mix_in[h, 1].astype(F32)) * (1 / 1024)).astype(BF)

        def step(i, carry):
            grad = grads[1, span(h)]
            sa[h, 1, i] = (
                (dot(whole(wa, i), grad, NT) + back_acc[h, 0, i]).astype(BF).reshape(4, HALF, SPAN)
            )
            sb[h, 1, i] = (
                (dot(whole(wb, i), grad, NT) + back_acc[h, 1, i]).astype(BF).reshape(4, HALF, SPAN)
            )
            return carry

        lax.fori_loop(0, 4, step, 0)
        return scatter_one(h, 1)

    def total_of(own, others):
        total = own.astype(F32)
        for other in others:
            total = total + other.astype(F32)
        return total

    def scatter_two(h, t):
        sa2[h, t] = total_of(sa[h, t, z], [ra1[h, t, k] for k in range(3)]).astype(BF)
        sb2[h, t] = total_of(sb[h, t, x], [rb1[h, t, k] for k in range(3)]).astype(BF)
        copies = []
        for d in (1, 2, 3):
            copies.append(remote(sa2.at[h, t, (x + d) % 4], ra2.at[h, t, d - 1], xp(d)))
            copies.append(remote(sb2.at[h, t, (z + d) % 4], rb2.at[h, t, d - 1], zp(d)))
        return copies

    def scattered(h, t):
        first = total_of(sa2[h, t, x], [ra2[h, t, k] for k in range(3)])
        second = total_of(sb2[h, t, z], [rb2[h, t, k] for k in range(3)])
        return jnp.concatenate([first.astype(BF), second.astype(BF)], axis=0)

    r_one = [[back_one(0)], []]
    r_one[0].append(back_two(0))
    m_two.append(mix_two(1))
    r_one[1].append(back_one(1))
    r_two = [[], []]
    arrived(r_one[0][0])
    r_two[0].append(scatter_two(0, 0))
    r_one[1].append(back_two(1))
    arrived(r_one[0][1])
    r_two[0].append(scatter_two(0, 1))

    def out_terms(i, carry):
        both = grads[...].reshape(2 * TOK, PART)

        def joined(ref):
            return jnp.concatenate([whole(ref, h, t, i) for t in (1, 0) for h in (0, 1)], axis=1)

        ha[i] = dot(joined(ga), both, NN).astype(BF).reshape(4, HALF, PART)
        hb[i] = dot(joined(gb), both, NN).astype(BF).reshape(4, HALF, PART)
        return carry

    lax.fori_loop(0, 4, out_terms, 0)
    o_core = []
    for k in range(2):
        o_core.append(remote(ha.at[:, 2 * k + 1 - c], ca.at[k], sib))
        o_core.append(remote(hb.at[2 * k + 1 - c], cb.at[k], sib))
    arrived(r_one[1][0])
    r_two[1].append(scatter_two(1, 0))
    arrived(o_core)
    far = 1 - yh
    xa[...] = total_of(ha[:, 2 * far + c], [ca[far]]).astype(BF)
    xb[...] = total_of(hb[2 * far + c], [cb[far]]).astype(BF)
    o_crs = [remote(xa, ya, crs), remote(xb, yb, crs)]

    cv_acc[...] = jnp.zeros_like(cv_acc)
    ck_acc[...] = jnp.zeros_like(ck_acc)

    def soft_back(i, carry):
        at = pl.ds(pl.multiple_of(i * 32, 32), 32)
        weights, moved = prob[at, :], prob_tan[at, :]
        pulled, pulled_tan = score[at, :], score_tan[at, :]
        base = jnp.sum(weights * pulled, axis=-1, keepdims=True)
        base_tan = jnp.sum(moved * pulled + weights * pulled_tan, axis=-1, keepdims=True)
        less = pulled - base
        slope[at, :] = (weights * less).astype(BF)
        slope_tan[at, :] = (moved * less + weights * (pulled_tan - base_tan)).astype(BF)
        return carry

    def value_terms(h, g, g_tan):
        def step(b, carry):
            at = keys_of(b)
            cv_acc[b] += dot(g, rnd_tan[span(h), at], NN) + dot(g_tan, rnd[span(h), at], NN)
            return carry

        lax.fori_loop(0, 4, step, 0)

    def slopes(h, g, g_tan):
        g_both = jnp.concatenate([g_tan, g], axis=0)

        def step(b, carry):
            at = keys_of(b)
            score[span(h), at] = dot(g, gkv[b, KEYS : KEYS + HS], TN)
            score_tan[span(h), at] = dot(g_both, gkv[b, KEYS : KEYS + 2 * HS], TN)
            return carry

        lax.fori_loop(0, 4, step, 0)
        lax.fori_loop(h * SPAN // 32, (h + 1) * SPAN // 32, soft_back, 0)

    def key_terms(h):
        left, left_tan = q[:, span(h)], q_tan[:, span(h)]

        def step(b, carry):
            at = keys_of(b)
            ck_acc[b] += dot(left, slope_tan[span(h), at], NN) + dot(left_tan, slope[span(h), at], NN)
            return carry

        lax.fori_loop(0, 4, step, 0)

    def chip_sums(own, other, kept):
        for k in range(2):
            kept[k] = total_of(own[2 * k + c], [other[k]]).astype(BF)

    arrived(r_two[0][0])
    arrived(r_two[0][1])
    g_first, g_first_tan = scattered(0, 0), scattered(0, 1)
    value_terms(0, g_first, g_first_tan)
    arrived(r_one[1][1])
    r_two[1].append(scatter_two(1, 1))
    slopes(0, g_first, g_first_tan)
    key_terms(0)

    arrived(r_two[1][0])
    arrived(r_two[1][1])
    arrived(n_one)
    n_two = []
    for d in (1, 2, 3):
        at0 = nb.at[b0, rows(z * 64, 64)]
        at1 = nb.at[b1, rows(x * 64, 64)]
        n_two.append(remote(at0, at0, zp(d)))
        n_two.append(remote(at1, at1, xp(d)))
    g_second, g_second_tan = scattered(1, 0), scattered(1, 1)
    value_terms(1, g_second, g_second_tan)
    cv[...] = cv_acc[...].astype(BF)
    v_core = [remote(cv.at[2 * k + 1 - c], cvr.at[k], sib) for k in range(2)]
    slopes(1, g_second, g_second_tan)
    arrived(v_core)
    chip_sums(cv, cvr, cvs)
    v_far = remote(cvs, cvf, crs)
    key_terms(1)
    ck[...] = (ck_acc[...] * root).astype(BF)

    k_core = [remote(ck.at[2 * k + 1 - c], ckr.at[k], sib) for k in range(2)]

    def query_block(b, held):
        at = keys_of(b)
        return held + dot(gkv[b, 0:HS], slope_tan[:, at], NT) + dot(gkv[b, HS : 2 * HS], slope[:, at], NT)

    cot_query = lax.fori_loop(0, 4, query_block, jnp.zeros((HS, TOK), F32)) * root
    cot[s, 0:HS] = rotate(cot_query.astype(BF).astype(F32), own_trig, -1.0).astype(BF)
    q_far = remote(cot.at[s, pl.ds(0, HS)], cot.at[s, pl.ds(0, HS)], crs)
    arrived(k_core)
    chip_sums(ck, ckr, cks)
    k_far = remote(cks, ckf, crs)

    arrived(o_crs)
    fa[...] = total_of(ha[:, s], [ca[yh], ya[...]]).astype(BF)
    fb[...] = total_of(hb[s], [cb[yh], yb[...]]).astype(BF)
    o_fin = []
    for d in (1, 2, 3):
        other = (z + d) % 4
        o_fin.append(remote(fa.at[other], oa.at[z], fin(d)))
        o_fin.append(remote(fb.at[other], ob.at[z], fin(d)))
    o_far = [
        remote(fa.at[z], oa.at[z], fin(0), begin=False),
        remote(fb.at[z], ob.at[z], fin(0), begin=False),
    ]
    near = local_count[0]
    o_near = [
        pltpu.make_async_copy(fa.at[z], oa.at[z], local.at[near]),
        pltpu.make_async_copy(fb.at[z], ob.at[z], local.at[near + 1]),
    ]

    @pl.when(x != s)
    def _():
        for copy in o_far:
            copy.start()

    @pl.when(x == s)
    def _():
        for copy in o_near:
            copy.start()

    arrived([v_far])
    for k in range(2):
        cot[2 * k + c, 2 * HS : 3 * HS] = total_of(cvs[k], [cvf[k]]).astype(BF)
    turns = [
        trig(jnp.broadcast_to(gkv[2 * k + c, KEYS - 16 : KEYS].astype(F32)[0:1], (ROT, TOK)))
        for k in range(2)
    ]
    arrived([k_far])
    for k in range(2):
        both = total_of(cks[k], [ckf[k]]).astype(BF).astype(F32)
        cot[2 * k + c, HS : 2 * HS] = rotate(both, turns[k], -1.0).astype(BF)
    arrived([q_far])
    t_sib = [remote(cot.at[2 * k + c], cot.at[2 * k + c], sib) for k in range(2)]
    arrived([n_sib] + n_two)

    def first_terms(i, carry):
        at = lanes(i * TOK, TOK)
        part[:, at] = dot(cot[s], nrm[:, lanes(s * SHARE + i * TOK, TOK)], NN) + dot(
            cot[s_crs], nb[s_crs, :, at], NN
        )
        return carry

    lax.fori_loop(0, SHARE // TOK, first_terms, 0)
    arrived(o_fin)

    @pl.when(x != s)
    def _():
        for copy in o_far:
            copy.wait_recv()
            copy.wait_send()

    @pl.when(x == s)
    def _():
        for copy in o_near:
            copy.wait()

    e_base = (
        lax.broadcasted_iota(jnp.int32, (HALF, PART), 0) * D
        + lax.broadcasted_iota(jnp.int32, (HALF, PART), 1)
        + (D * WIDE + fs * HS * D + s * SHARE)
    ) * jnp.int32(MIX[0]) + seeded
    scale = math.sqrt(INNER)
    for half, ref in enumerate((oa, ob)):
        for k in range(4):
            bit = sign_bit(e_base + jnp.int32(wrap((half * HALF * D + k * PART) * MIX[0])))
            oo[half * HALF : (half + 1) * HALF, k * PART : (k + 1) * PART] = (
                ref[k].astype(F32) * jnp.where(bit == 0, F32(scale), F32(-scale))
            ).astype(BF)


    arrived(t_sib)

    def last_terms(i, carry):
        at = lanes(i * TOK, TOK)
        total = part[:, at] + (dot(cot[s_sib], nb[s_sib, :, at], NN) + dot(cot[s_crd], nb[s_crd, :, at], NN))
        oq[:, at] = (total * sgn[:, at]).astype(BF)
        return carry

    lax.fori_loop(0, SHARE // TOK, last_terms, 0)

    for copy in sent:
        copy.wait_send()


def widen(product_in, out_in, product, out):
    product[...] = product_in[...].astype(F32)
    out[...] = out_in[...].astype(F32)


def tables():
    rate = 10000.0 ** (-2.0 * np.arange(ROT // 2) / ROT)
    rate = np.concatenate([rate, rate])[:, None]
    within = np.arange(TOK)[None, :] * rate
    blocks = np.arange(4)[:, None, None] * float(TOK) * rate[None] + np.zeros((1, 1, TOK))
    tab_t = np.stack([np.cos(within), np.sin(within)]).astype(np.float32)
    tab_b = np.stack([np.cos(blocks), np.sin(blocks)], axis=1).astype(np.float32)
    return tab_t, tab_b


def per_device(tokens, target, norm_gain, qkv_weight, out_weight, probe_seed, block_order):
    tab_t, tab_b = tables()
    anywhere = pl.BlockSpec(memory_space=pl.ANY)
    vmem = pl.BlockSpec(memory_space=pltpu.VMEM)
    smem = pl.BlockSpec(memory_space=pltpu.SMEM)
    v = pltpu.VMEM
    scratch = [
        v((TOK, D), BF), v((TOK, PART), BF), v((COLS, D), BF), v((TOK, D), BF), v((2, COLS, TOK), F32),
        v((2, TOK, 128), F32), v((4, TOK, SHARE), BF), v((4, 4 * HS + 16, TOK), BF),
        v((4, 4, HALF, PART), BF), v((2, 4, 4, HALF, PART), BF),
        v((4, 4, HALF, PART), BF), v((4, 4, HALF, PART), BF),
        v((2, 2, 4, 4, HALF, SPAN), BF), v((2, 2, 4, 4, HALF, SPAN), BF),
        v((TOK, 1024), F32), v((TOK, 1024), F32), v((TOK, 1024), F32), v((TOK, 1024), F32),
        v((TOK, 1024), BF), v((TOK, 1024), BF), v((TOK, 1024), BF), v((TOK, 1024), BF),
        v((4, HS, TOK), F32), v((4, HS, TOK), F32),
        v((2, 2, SPAN, PART), F32), v((2, 2, SPAN, PART), BF), v((2, 2, SPAN, PART), BF), v((2, TOK, PART), BF),
        v((2, 2, 4, 4 * HALF, SPAN), F32),
        v((2, 2, 4, 4, HALF, SPAN), BF), v((2, 2, 4, 4, HALF, SPAN), BF),
        v((2, 2, 3, 4, HALF, SPAN), BF), v((2, 2, 3, 4, HALF, SPAN), BF),
        v((2, 2, 4, HALF, SPAN), BF), v((2, 2, 4, HALF, SPAN), BF),
        v((2, 2, 3, HALF, SPAN), BF), v((2, 2, 3, HALF, SPAN), BF),
        v((4, 4, HALF, PART), BF), v((4, 4, HALF, PART), BF),
        v((2, 4, HALF, PART), BF), v((2, 4, HALF, PART), BF),
        v((4, HALF, PART), BF), v((4, HALF, PART), BF), v((4, HALF, PART), BF), v((4, HALF, PART), BF),
        v((4, HALF, PART), BF), v((4, HALF, PART), BF), v((4, HALF, PART), BF), v((4, HALF, PART), BF),
        v((4, HS, TOK), BF), v((2, HS, TOK), BF), v((2, HS, TOK), BF), v((2, HS, TOK), BF),
        v((4, HS, TOK), BF), v((2, HS, TOK), BF), v((2, HS, TOK), BF), v((2, HS, TOK), BF),
        v((4, 3 * HS, TOK), BF), v((COLS, SHARE), F32), v((COLS, SHARE), F32),
        pltpu.SemaphoreType.DMA((N_REMOTE,)), pltpu.SemaphoreType.DMA((N_REMOTE,)),
        pltpu.SemaphoreType.DMA((N_LOCAL,)),
    ]
    product, out_curv = pl.pallas_call(
        kernel,
        out_shape=(
            jax.ShapeDtypeStruct((COLS, SHARE), BF),
            jax.ShapeDtypeStruct((HS, SHARE), BF),
        ),
        in_specs=[anywhere, anywhere, vmem, anywhere, anywhere, smem, smem, vmem, vmem],
        out_specs=(vmem, vmem),
        scratch_shapes=scratch,
        compiler_params=pltpu.CompilerParams(
            collective_id=0, has_side_effects=True, vmem_limit_bytes=60 * 2**20
        ),
    )(
        tokens, target, norm_gain.reshape(1, D), qkv_weight.T, out_weight, probe_seed, block_order,
        jnp.asarray(tab_t), jnp.asarray(tab_b),
    )
    product, out_curv = pl.pallas_call(
        widen,
        grid=(3,),
        out_shape=(
            jax.ShapeDtypeStruct((COLS, SHARE), F32),
            jax.ShapeDtypeStruct((HS, SHARE), F32),
        ),
        in_specs=[pl.BlockSpec((COLS, SHARE // 3), lambda i: (0, i)), pl.BlockSpec((HS, SHARE // 3), lambda i: (0, i))],
        out_specs=(pl.BlockSpec((COLS, SHARE // 3), lambda i: (0, i)), pl.BlockSpec((HS, SHARE // 3), lambda i: (0, i))),
    )(product, out_curv)
    return product.T, out_curv


def solution(mesh):
    placed = (P("seq", None), P("seq", None), P(), P(None, "fsdp"), P("fsdp", None), P(), P("seq"))
    return jax.shard_map(
        per_device,
        mesh=mesh,
        in_specs=placed,
        out_specs=(P("seq", "fsdp"), P("fsdp", "seq")),
        check_vma=False,
    )
```

```python
import functools
import math

import jax
import jax.numpy as jnp
import numpy as np
from jax import lax
from jax.experimental import pallas as pl
from jax.experimental.pallas import tpu as pltpu
from jax.sharding import PartitionSpec as P

MESH = pl.DeviceIdType.MESH
BF = jnp.bfloat16
F32 = jnp.float32
D = 6144
HS = 96
ROT = 24
TOK = 256
COLS = 288
WIDE = 9216
INNER = 3072
SHARE = 1536
PART = 384
HALF = 48
SPAN = 128
KEYS = 2 * HS + 16
STEP = 768
MIX = (-1640531535, -2048144789, -1028477387)
N_REMOTE = 120
N_LOCAL = 24


def wrap(value):
    return ((value + 2**31) % 2**32) - 2**31


def shifted(state, places):
    return lax.shift_right_logical(state, jnp.full(state.shape, places, jnp.int32))


def sign_bit(state):
    state = state ^ shifted(state, 16)
    state = state * jnp.int32(MIX[1])
    state = state ^ shifted(state, 13)
    state = state * jnp.int32(MIX[2])
    return (state ^ shifted(state, 16)) & jnp.int32(128)


def dot(a, b, contract):
    return lax.dot_general(a, b, (contract, ((), ())), preferred_element_type=F32)


NN = ((1,), (0,))
NT = ((1,), (1,))
TN = ((0,), (0,))


def kernel(
    tok_in, tgt_in, gain_in, wq_in, wo_in, seed, block, tab_t_in, tab_b_in,
    oq_out, oo_out,
    oq, oo, gain, tab_t, tab_b, tok, tgt, wq, nrm, acc,
    stat, nb, gkv,
    wt, ww, pp, wpt, ga, gb,
    qq, qk, gg, score, prob, prob_tan, rnd, slope, cv_acc, ck_acc, cq_acc,
    mix_acc, mix_out, mix_in, grads, grad, turn, resid,
    sab, ra1, rb1, sa2, sb2, ra2, rb2,
    ha, hb, ca, cb, xa, xb, ya, yb, fa, fb, oa, ob,
    cv, cvr, cvs, cvf, ck, ckr, cks, ckf, cot, sgn, part,
    send, recv, local,
):
    fs = lax.axis_index("fsdp")
    s = lax.axis_index("seq")
    x = fs // 8
    yl = (fs // 4) % 2
    z = fs % 4
    yh = s // 2
    c = s % 2
    s_sib = yh * 2 + (1 - c)
    s_crs = (1 - yh) * 2 + c
    s_crd = (1 - yh) * 2 + (1 - c)
    own_cols = (x * 4 + z) * PART

    def device(px, py, pz, ps):
        return ((px * 2 + py) * 4 + pz, ps)

    def xp(d):
        return device((x + d) % 4, yl, z, s)

    def zp(d):
        return device(x, yl, (z + d) % 4, s)

    def fin(d):
        return device(s, yl, (z + d) % 4, x)

    partner = device(x, 1 - yl, z, s)
    sib = device(x, yl, z, s_sib)
    crs = device(x, yl, z, s_crs)
    crd = device(x, yl, z, s_crd)

    count = [0]
    sent = []

    def remote(src, dst, to, begin=True):
        i = count[0]
        count[0] += 1
        copy = pltpu.make_async_remote_copy(
            src_ref=src, dst_ref=dst, send_sem=send.at[i], recv_sem=recv.at[i],
            device_id=to, device_id_type=MESH,
        )
        if begin:
            copy.start()
            sent.append(copy)
        return copy

    local_count = [0]

    def stay(src, dst):
        i = local_count[0]
        local_count[0] += 1
        copy = pltpu.make_async_copy(src, dst, local.at[i])
        copy.start()
        return copy

    def nearby(src, dst):
        i = local_count[0]
        local_count[0] += 1
        return pltpu.make_async_copy(src, dst, local.at[i])

    def arrived(copies):
        for copy in copies:
            copy.wait_recv()

    def lanes(start, size):
        return pl.ds(pl.multiple_of(start, 128), size)

    def rows(start, size):
        return pl.ds(pl.multiple_of(start, 16), size)

    tok_loads = [stay(tok_in.at[pl.ds(k * 64, 64)], tok.at[pl.ds(k * 64, 64)]) for k in range(4)]
    tab_loads = [stay(gain_in, gain), stay(tab_t_in, tab_t), stay(tab_b_in, tab_b)]
    tgt_load = stay(tgt_in.at[:, lanes(own_cols, PART)], tgt)
    first, second = jnp.where(c == 0, x, z), jnp.where(c == 0, z, x)

    def column(a, k):
        return jnp.where(c == 0, a * 4 + k, k * 4 + a) * PART

    own_w = [
        stay(wo_in.at[rows(c * HALF, HALF), lanes(column(first, k), PART)], wt.at[first, k])
        for k in range(4)
    ]

    barrier = pltpu.get_barrier_semaphore()

    def greet(to):
        pl.semaphore_signal(barrier, inc=1, device_id=to, device_id_type=MESH)

    for d in (1, 2, 3):
        greet(xp(d))
        greet(zp(d))
    for to in (partner, sib, crs, crd):
        greet(to)

    @pl.when(x != s)
    def _():
        for d in range(4):
            greet(fin(d))


    def norm_sums(i, carry):
        at = rows(i * 16, 16)
        totals = [jnp.zeros((16, 128), F32) for _ in range(2)]
        for k in range(D // 128):
            totals[k % 2] += tok[at, k * 128 : (k + 1) * 128].astype(F32)
        stat[0, at, :] = totals[0] + totals[1]
        return carry

    for k in range(4):
        tok_loads[k].wait()
        lax.fori_loop(k * 4, (k + 1) * 4, norm_sums, 0, unroll=2)
    wq_load = stay(wq_in, wq)
    average = jnp.sum(stat[0], axis=-1, keepdims=True) * (1 / D)
    stat[0] = jnp.broadcast_to(average, (TOK, 128))

    def norm_squares(i, carry):
        at = rows(i * 16, 16)
        middle = stat[0, at, :]
        totals = [jnp.zeros((16, 128), F32) for _ in range(2)]
        for k in range(D // 128):
            centred = tok[at, k * 128 : (k + 1) * 128].astype(F32) - middle
            totals[k % 2] += centred * centred
        stat[1, at, :] = totals[0] + totals[1]
        return carry

    lax.fori_loop(0, TOK // 16, norm_squares, 0, unroll=2)
    spread = jnp.sum(stat[1], axis=-1, keepdims=True) * (1 / D)
    stat[1] = jnp.broadcast_to(lax.rsqrt(spread + 1e-05), (TOK, 128))

    pl.semaphore_wait(barrier, jnp.where(x != s, 14, 10))

    def along_first(d):
        return device(
            jnp.where(c == 0, (x + d) % 4, x), yl, jnp.where(c == 0, z, (z + d) % 4), s
        )

    def along_second(d):
        return device(
            jnp.where(c == 0, x, (x + d) % 4), yl, jnp.where(c == 0, (z + d) % 4, z), s
        )

    w_one = []
    for d in (1, 2, 3):
        for k in range(4):
            w_one.append(
                remote(
                    wo_in.at[rows(c * HALF, HALF), lanes(column((first + d) % 4, k), PART)],
                    wt.at[first, k], along_first(d),
                )
            )

    for copy in tab_loads:
        copy.wait()

    def norm_rows(i, carry):
        at = rows(i * 16, 16)
        middle, factor = stat[0, at, :], stat[1, at, :]
        for k in range(D // 128):
            cols = slice(k * 128, (k + 1) * 128)
            nrm[at, cols] = ((tok[at, cols].astype(F32) - middle) * factor * gain[:, cols]).astype(BF)
        return carry

    lax.fori_loop(0, TOK // 16, norm_rows, 0)

    piece = jnp.where(c == 0, z * 4 + x, x * 4 + z) * 16
    n_crs = remote(
        nrm.at[rows(piece, 16), lanes(s_crs * SHARE, SHARE)], nb.at[s, rows(piece, 16)], crs
    )
    n_crd = remote(
        nrm.at[rows(piece, 16), lanes(s_crd * SHARE, SHARE)], nb.at[s, rows(piece, 16)], crd
    )
    n_sib = remote(nrm.at[:, lanes(s_sib * SHARE, SHARE)], nb.at[s], sib)

    wq_load.wait()
    acc[...] = jnp.zeros_like(acc)
    seeded = seed[0]
    q_probe = float(np.float32(1 / math.sqrt(D)).astype(jnp.bfloat16))
    o_probe = float(np.float32(1 / math.sqrt(INNER)).astype(jnp.bfloat16))

    def project(start, size):
        q_rows = lax.broadcasted_iota(jnp.int32, (size, STEP), 1)
        q_cols = lax.broadcasted_iota(jnp.int32, (size, STEP), 0)
        q_base = (q_rows * WIDE + q_cols + (fs * COLS + start)) * jnp.int32(MIX[0]) + seeded
        to = pl.ds(start, size)

        def step(i, carry):
            at = pl.ds(pl.multiple_of(i * STEP, STEP), STEP)
            bit = sign_bit(q_base + i * jnp.int32(wrap(STEP * WIDE * MIX[0])))
            probe = jnp.where(bit == 0, F32(q_probe), F32(-q_probe)).astype(BF)
            both = dot(jnp.concatenate([wq[to, at], probe], axis=0), nrm[:, at], NT)
            acc[0, to] += both[:size]
            acc[1, to] += both[size:]
            return carry

        lax.fori_loop(0, D // STEP, step, 0)

    project(HS, 2 * HS)

    number = block[0]
    low = lax.broadcasted_iota(jnp.int32, (ROT, TOK), 0) < ROT // 2

    def trig(here):
        cos_b = jnp.zeros((ROT, TOK), F32)
        sin_b = jnp.zeros((ROT, TOK), F32)
        for k in range(4):
            cos_b = jnp.where(here == k, tab_b[k, 0], cos_b)
            sin_b = jnp.where(here == k, tab_b[k, 1], sin_b)
        cos = cos_b * tab_t[0] - sin_b * tab_t[1]
        sin = sin_b * tab_t[0] + cos_b * tab_t[1]
        return cos, jnp.where(low, -sin, sin)

    own_trig = trig(jnp.full((ROT, TOK), number, jnp.int32))

    def rotate(field, turns, sign=1.0):
        cos, sin = turns
        head = field[:ROT]
        swapped = pltpu.roll(head, ROT // 2, 0)
        return jnp.concatenate([head * cos + swapped * (sin * sign), field[ROT:]], axis=0)

    for k in range(2):
        gkv[s, k * HS : (k + 1) * HS] = rotate(acc[k, HS : 2 * HS], own_trig).astype(BF)
    gkv[s, KEYS - 16 : KEYS] = jnp.full((16, TOK), number, jnp.int32).astype(F32).astype(BF)
    k_part, v_part = pl.ds(0, KEYS), pl.ds(KEYS, 2 * HS)

    def spread_kv(slot, part, to):
        return remote(gkv.at[slot, part], gkv.at[slot, part], to)

    k_crs = spread_kv(s, k_part, crs)
    k_sib = spread_kv(s, k_part, sib)
    for k in range(2):
        gkv[s, KEYS + k * HS : KEYS + (k + 1) * HS] = acc[k, 2 * HS : 3 * HS].astype(BF)
    v_crs = spread_kv(s, v_part, crs)
    v_sib = spread_kv(s, v_part, sib)

    def span(h):
        return slice(h * SPAN, (h + 1) * SPAN)

    tgt_load.wait()
    project(0, HS)
    q = rotate(acc[0, :HS], own_trig).astype(BF)
    q_tan = rotate(acc[1, :HS], own_trig).astype(BF)
    for h in range(2):
        one, two = q[:, span(h)], q_tan[:, span(h)]
        qq[h] = jnp.concatenate(
            [jnp.concatenate([one, two], axis=1), jnp.concatenate([jnp.zeros_like(one), one], axis=1)],
            axis=0,
        ).astype(F32).T.astype(BF)
        qk[h] = jnp.concatenate([one, two], axis=1)
    resid[...] = (tok[:, lanes(own_cols, PART)].astype(F32) - tgt[...].astype(F32)).T

    b0 = (1 - yh) * 2
    b1 = b0 + 1
    arrived([n_crs, n_crd])
    n_one = []
    for d in (1, 2, 3):
        at0 = nb.at[b0, rows((z * 4 + x) * 16, 16)]
        at1 = nb.at[b1, rows((x * 4 + z) * 16, 16)]
        n_one.append(remote(at0, at0, xp(d)))
        n_one.append(remote(at1, at1, zp(d)))

    for copy in own_w:
        copy.wait()
    arrived(w_one)
    w_two = []
    for d in (1, 2, 3):
        w_two.append(remote(wt.at[:, (second + d) % 4], ww.at[c, second], along_second(d)))
    own_ww = stay(wt.at[:, second], ww.at[c, second])

    o_rows = lax.broadcasted_iota(jnp.int32, (HALF, PART), 0)
    o_lanes = lax.broadcasted_iota(jnp.int32, (HALF, PART), 1)
    o_base = (o_rows * D + o_lanes + (D * WIDE + own_cols)) * jnp.int32(MIX[0]) + seeded

    def probe_piece(i, carry):
        for k in range(4):
            first = ((k * 2 + yl) * 4 + i) * HS
            second = ((i * 2 + yl) * 4 + k) * HS + HALF
            bit = sign_bit(o_base + first * jnp.int32(wrap(D * MIX[0])))
            pp[0, i, k] = jnp.where(bit == 0, F32(o_probe), F32(-o_probe)).astype(BF)
            bit = sign_bit(o_base + second * jnp.int32(wrap(D * MIX[0])))
            pp[1, i, k] = jnp.where(bit == 0, F32(o_probe), F32(-o_probe)).astype(BF)
        return carry

    lax.fori_loop(0, 4, probe_piece, 0)

    def turned(source, start):
        def turn(i, carry):
            for a in range(2):
                value = source[a, i].reshape(4 * HALF, PART).astype(F32)
                wpt[a, i, start : start + PART] = value.T.astype(BF)
            return carry

        lax.fori_loop(0, 4, turn, 0)

    turned(pp, PART)

    arrived([k_crs])
    k_rel = spread_kv(s_crs, k_part, sib)
    arrived([v_crs])
    v_rel = spread_kv(s_crs, v_part, sib)

    arrived([k_sib, k_rel])
    root = 1 / math.sqrt(HS)

    def keys_of(b):
        return lanes(b * TOK, TOK)

    def pulls(left, part, h):
        def pull(b, carry):
            score[h, :, keys_of(b)] = dot(left[h], gkv[b, part], NN)
            return carry

        lax.fori_loop(0, 4, pull, 0, unroll=2)

    along = lax.broadcasted_iota(jnp.int32, (1, TOK), 1).astype(F32)
    key_pos = jnp.concatenate(
        [gkv[b, KEYS - 16 : KEYS].astype(F32)[0:1] * float(TOK) + along for b in range(4)], axis=1
    )
    number_f = jnp.full((32, 1), number, jnp.int32).astype(F32)
    down = lax.broadcasted_iota(jnp.int32, (32, 1), 0)

    def soft(h):
        def soft_rows(i, carry):
            at = pl.ds(pl.multiple_of(h * SPAN + i * 32, 32), 32)
            low, high = pl.ds(pl.multiple_of(i * 32, 32), 32), pl.ds(pl.multiple_of(SPAN + i * 32, 32), 32)
            query_pos = number_f * float(TOK) + (down + (h * SPAN + i * 32)).astype(F32)
            allowed = key_pos <= query_pos
            values = jnp.where(allowed, score[h, low, :] * root, -1e30)
            highest = jnp.max(values, axis=-1, keepdims=True)
            weights = jnp.exp(values - highest)
            weights = weights * (1.0 / jnp.sum(weights, axis=-1, keepdims=True))
            moved = weights * (score[h, high, :] * root)
            moved = moved - weights * jnp.sum(moved, axis=-1, keepdims=True)
            prob[at, :] = weights
            prob_tan[at, :] = moved
            rnd[h, high, :] = weights.astype(BF)
            rnd[h, low, :] = moved.astype(BF)
            return carry

        lax.fori_loop(0, SPAN // 32, soft_rows, 0, unroll=2)

    def joint(part, ref, h):
        def term(b, held):
            return held + dot(gkv[b, part], ref[h, :, keys_of(b)], NT)

        return lax.fori_loop(0, 4, term, jnp.zeros((2 * HS, 2 * SPAN), F32))

    def attn_products(h):
        terms = joint(v_part, rnd, h)
        both = jnp.concatenate([terms[:HS, SPAN:], terms[:HS, :SPAN] + terms[HS:, SPAN:]], axis=1)
        both = both.astype(BF)
        ga[h, z, x] = both[:HALF]
        gb[h, x, z] = both[HALF:]
        copies = []
        for d in (1, 2, 3):
            copies.append(remote(ga.at[h, z, x], ga.at[h, z, x], xp(d)))
            copies.append(remote(gb.at[h, x, z], gb.at[h, x, z], zp(d)))
        return copies

    def gather_two(h):
        copies = []
        for d in (1, 2, 3):
            copies.append(remote(ga.at[h, z], ga.at[h, z], zp(d)))
            copies.append(remote(gb.at[h, x], gb.at[h, x], xp(d)))
        return copies

    pulls(qq, pl.ds(0, 2 * HS), 0)
    soft(0)
    arrived([v_sib, v_rel])
    g_one = [attn_products(0)]
    pulls(qq, pl.ds(0, 2 * HS), 1)
    own_ww.wait()
    arrived(w_two)
    w_sib = remote(ww.at[c], ww.at[c], sib)
    soft(1)

    arrived(g_one[0])
    g_two = [gather_two(0)]
    g_one.append(attn_products(1))

    arrived([w_sib])
    turned(ww, 0)
    arrived(g_one[1])
    g_two.append(gather_two(1))

    def mix(h):
        arrived(g_two[h])
        total = jnp.zeros((2 * PART, 2 * SPAN), F32)
        for a, ref in enumerate((ga, gb)):
            for i in range(4):
                total = total + dot(wpt[a, i], ref[h, i].reshape(4 * HALF, 2 * SPAN), NN)
        mix_acc[h, :, 0:SPAN] = total[:PART, :SPAN]
        mix_acc[h, :, SPAN:] = total[:PART, SPAN:] + total[PART:, :SPAN]
        mix_out[h] = mix_acc[h].astype(BF)
        return remote(mix_out.at[h], mix_in.at[h], partner)

    m_both = [mix(0)]

    s_base = (
        (lax.broadcasted_iota(jnp.int32, (COLS, TOK), 1) + s * SHARE) * WIDE
        + lax.broadcasted_iota(jnp.int32, (COLS, TOK), 0)
        + fs * COLS
    ) * jnp.int32(MIX[0]) + seeded

    def sign_cols(i, carry):
        bit = sign_bit(s_base + i * jnp.int32(wrap(TOK * WIDE * MIX[0])))
        sgn[:, lanes(i * TOK, TOK)] = jnp.where(bit == 0, F32(math.sqrt(D)), F32(-math.sqrt(D)))
        return carry

    lax.fori_loop(0, SHARE // TOK, sign_cols, 0)

    def back(h):
        arrived([m_both[h]])
        grads[h] = mix_acc[h] + mix_in[h].astype(F32)
        grads[h, :, 0:SPAN] += resid[:, span(h)]
        grad[h] = (grads[h] * (1 / 1024)).astype(BF)

        def step(a, carry):
            for i in range(4):
                first = dot(ww[a, i].reshape(4 * HALF, PART), grad[h], NN)
                second = dot(pp[a, i].reshape(4 * HALF, PART), grad[h, :, 0:SPAN], NN)
                sab[h, a, i, :, :, 0:SPAN] = first[:, :SPAN].astype(BF).reshape(4, HALF, SPAN)
                sab[h, a, i, :, :, SPAN:] = (first[:, SPAN:] + second).astype(BF).reshape(4, HALF, SPAN)
            return carry

        lax.fori_loop(0, 2, step, 0)
        copies = []
        for d in (1, 2, 3):
            copies.append(remote(sab.at[h, 0, (z + d) % 4], ra1.at[h, d - 1], zp(d)))
            copies.append(remote(sab.at[h, 1, (x + d) % 4], rb1.at[h, d - 1], xp(d)))
        return copies

    def total_of(own, others):
        total = own.astype(F32)
        for other in others:
            total = total + other.astype(F32)
        return total

    def scatter_two(h):
        arrived(r_one[h])
        sa2[h] = total_of(sab[h, 0, z], [ra1[h, k] for k in range(3)]).astype(BF)
        sb2[h] = total_of(sab[h, 1, x], [rb1[h, k] for k in range(3)]).astype(BF)
        copies = []
        for d in (1, 2, 3):
            copies.append(remote(sa2.at[h, (x + d) % 4], ra2.at[h, d - 1], xp(d)))
            copies.append(remote(sb2.at[h, (z + d) % 4], rb2.at[h, d - 1], zp(d)))
        return copies

    def scattered(h):
        arrived(r_two[h])
        first = total_of(sa2[h, x], [ra2[h, k] for k in range(3)])
        second = total_of(sb2[h, z], [rb2[h, k] for k in range(3)])
        return jnp.concatenate([first.astype(BF), second.astype(BF)], axis=0)

    r_one = [back(0)]
    m_both.append(mix(1))
    r_one.append(back(1))
    r_two = [scatter_two(0)]

    for h in range(2):
        for k in range(2):
            at = slice((2 * h + k) * SPAN, (2 * h + k + 1) * SPAN)
            turn[at] = grad[h, :, (1 - k) * SPAN : (2 - k) * SPAN].astype(F32).T.astype(BF)

    def out_terms(i, carry):
        def joined(ref):
            return jnp.concatenate([ref[h, i].reshape(4 * HALF, 2 * SPAN) for h in range(2)], axis=1)

        ha[i] = dot(joined(ga), turn[...], NN).astype(BF).reshape(4, HALF, PART)
        hb[i] = dot(joined(gb), turn[...], NN).astype(BF).reshape(4, HALF, PART)
        return carry

    lax.fori_loop(0, 4, out_terms, 0)
    o_core = []
    for k in range(2):
        o_core.append(remote(ha.at[:, 2 * k + 1 - c], ca.at[k], sib))
        o_core.append(remote(hb.at[2 * k + 1 - c], cb.at[k], sib))
    arrived(o_core)
    far = 1 - yh
    xa[...] = total_of(ha[:, 2 * far + c], [ca[far]]).astype(BF)
    xb[...] = total_of(hb[2 * far + c], [cb[far]]).astype(BF)
    o_crs = [remote(xa, ya, crs), remote(xb, yb, crs)]

    cv_acc[...] = jnp.zeros_like(cv_acc)
    ck_acc[...] = jnp.zeros_like(ck_acc)

    def soft_back(h):
        def rows_back(i, carry):
            at = pl.ds(pl.multiple_of(h * SPAN + i * 32, 32), 32)
            low, high = pl.ds(pl.multiple_of(i * 32, 32), 32), pl.ds(pl.multiple_of(SPAN + i * 32, 32), 32)
            weights, moved = prob[at, :], prob_tan[at, :]
            pulled, pulled_tan = score[h, low, :], score[h, high, :]
            base = jnp.sum(weights * pulled, axis=-1, keepdims=True)
            base_tan = jnp.sum(moved * pulled + weights * pulled_tan, axis=-1, keepdims=True)
            less = pulled - base
            slope[h, high, :] = (weights * less).astype(BF)
            slope[h, low, :] = (moved * less + weights * (pulled_tan - base_tan)).astype(BF)
            return carry

        lax.fori_loop(0, SPAN // 32, rows_back, 0, unroll=2)

    def value_terms(h, g):
        def step(b, carry):
            cv_acc[b] += dot(g, rnd[h, :, keys_of(b)], NN)
            return carry

        lax.fori_loop(0, 4, step, 0, unroll=2)

    def slopes(h, g):
        one, two = g[:, :SPAN], g[:, SPAN:]
        gg[h] = jnp.concatenate(
            [jnp.concatenate([one, two], axis=1), jnp.concatenate([jnp.zeros_like(one), one], axis=1)],
            axis=0,
        ).astype(F32).T.astype(BF)
        pulls(gg, v_part, h)
        soft_back(h)

    def key_terms(h):
        def step(b, carry):
            ck_acc[b] += dot(qk[h], slope[h, :, keys_of(b)], NN)
            return carry

        lax.fori_loop(0, 4, step, 0, unroll=2)

    def query_terms(h):
        terms = joint(pl.ds(0, 2 * HS), slope, h)
        cq_acc[:, span(h)] = terms[:HS, :SPAN] + terms[HS:, SPAN:]

    def chip_sums(own, other, kept):
        for k in range(2):
            kept[k] = total_of(own[2 * k + c], [other[k]]).astype(BF)

    g_first = scattered(0)
    value_terms(0, g_first)
    r_two.append(scatter_two(1))
    slopes(0, g_first)
    key_terms(0)
    query_terms(0)

    arrived(o_crs)
    fa[...] = total_of(ha[:, s], [ca[yh], ya[...]]).astype(BF)
    fb[...] = total_of(hb[s], [cb[yh], yb[...]]).astype(BF)
    o_fin = []
    for d in (1, 2, 3):
        other = (z + d) % 4
        o_fin.append(remote(fa.at[other], oa.at[z], fin(d)))
        o_fin.append(remote(fb.at[other], ob.at[z], fin(d)))
    o_far = [
        remote(fa.at[z], oa.at[z], fin(0), begin=False),
        remote(fb.at[z], ob.at[z], fin(0), begin=False),
    ]
    o_near = [nearby(fa.at[z], oa.at[z]), nearby(fb.at[z], ob.at[z])]

    @pl.when(x != s)
    def _():
        for copy in o_far:
            copy.start()

    @pl.when(x == s)
    def _():
        for copy in o_near:
            copy.start()

    g_second = scattered(1)
    arrived(n_one)
    n_two = []
    for d in (1, 2, 3):
        at0 = nb.at[b0, rows(z * 64, 64)]
        at1 = nb.at[b1, rows(x * 64, 64)]
        n_two.append(remote(at0, at0, zp(d)))
        n_two.append(remote(at1, at1, xp(d)))
    value_terms(1, g_second)
    cv[...] = cv_acc[...].astype(BF)
    v_core = [remote(cv.at[2 * k + 1 - c], cvr.at[k], sib) for k in range(2)]
    slopes(1, g_second)
    arrived(v_core)
    chip_sums(cv, cvr, cvs)
    v_far = remote(cvs, cvf, crs)
    key_terms(1)
    ck[...] = (ck_acc[...] * root).astype(BF)

    k_core = [remote(ck.at[2 * k + 1 - c], ckr.at[k], sib) for k in range(2)]

    query_terms(1)
    cot_query = cq_acc[...] * root
    cot[s, 0:HS] = rotate(cot_query.astype(BF).astype(F32), own_trig, -1.0).astype(BF)
    q_far = remote(cot.at[s, pl.ds(0, HS)], cot.at[s, pl.ds(0, HS)], crs)
    arrived(k_core)
    chip_sums(ck, ckr, cks)
    k_far = remote(cks, ckf, crs)

    arrived([v_far])
    for k in range(2):
        cot[2 * k + c, 2 * HS : 3 * HS] = total_of(cvs[k], [cvf[k]]).astype(BF)
    turns = [
        trig(jnp.broadcast_to(gkv[2 * k + c, KEYS - 16 : KEYS].astype(F32)[0:1], (ROT, TOK)))
        for k in range(2)
    ]
    arrived([k_far])
    for k in range(2):
        both = total_of(cks[k], [ckf[k]]).astype(BF).astype(F32)
        cot[2 * k + c, HS : 2 * HS] = rotate(both, turns[k], -1.0).astype(BF)
    arrived([q_far])
    t_sib = [remote(cot.at[2 * k + c], cot.at[2 * k + c], sib) for k in range(2)]
    arrived([n_sib] + n_two)

    def first_terms(i, carry):
        at = lanes(i * TOK, TOK)
        part[:, at] = dot(cot[s], nrm[:, lanes(s * SHARE + i * TOK, TOK)], NN) + dot(
            cot[s_crs], nb[s_crs, :, at], NN
        )
        return carry

    lax.fori_loop(0, SHARE // TOK, first_terms, 0)
    arrived(o_fin)

    @pl.when(x != s)
    def _():
        for copy in o_far:
            copy.wait_recv()
            copy.wait_send()

    @pl.when(x == s)
    def _():
        for copy in o_near:
            copy.wait()

    e_base = (
        lax.broadcasted_iota(jnp.int32, (HALF, PART), 0) * D
        + lax.broadcasted_iota(jnp.int32, (HALF, PART), 1)
        + (D * WIDE + fs * HS * D + s * SHARE)
    ) * jnp.int32(MIX[0]) + seeded
    scale = math.sqrt(INNER)
    for half, ref in enumerate((oa, ob)):
        for k in range(4):
            bit = sign_bit(e_base + jnp.int32(wrap((half * HALF * D + k * PART) * MIX[0])))
            oo[half * HALF : (half + 1) * HALF, k * PART : (k + 1) * PART] = (
                ref[k].astype(F32) * jnp.where(bit == 0, F32(scale), F32(-scale))
            ).astype(BF)


    arrived(t_sib)

    def last_terms(i, carry):
        at = lanes(i * TOK, TOK)
        total = part[:, at] + (dot(cot[s_sib], nb[s_sib, :, at], NN) + dot(cot[s_crd], nb[s_crd, :, at], NN))
        oq[:, at] = (total * sgn[:, at]).astype(BF)
        return carry

    leaving = [stay(oo, oo_out)]
    for k in range(2):
        lax.fori_loop(k * 3, k * 3 + 3, last_terms, 0)
        cols = pl.ds(k * SHARE // 2, SHARE // 2)
        leaving.append(stay(oq.at[:, cols], oq_out.at[:, cols]))
    for copy in leaving:
        copy.wait()

    for copy in sent:
        copy.wait_send()


def widen(product_in, out_in, product, out, narrow, narrow_out, wide, wide_out, loads, stores):
    thirds = [pl.ds(k * SHARE // 3, SHARE // 3) for k in range(3)]
    parts = [(product_in.at[:, at], narrow.at[k], wide.at[k], product.at[:, at]) for k, at in enumerate(thirds)]
    parts.append((out_in, narrow_out, wide_out, out))
    arrive = [pltpu.make_async_copy(part[0], part[1], loads.at[k]) for k, part in enumerate(parts)]
    leave = [pltpu.make_async_copy(part[2], part[3], stores.at[k]) for k, part in enumerate(parts)]
    for copy in arrive:
        copy.start()
    for k, part in enumerate(parts):
        arrive[k].wait()
        part[2][...] = part[1][...].astype(F32)
        leave[k].start()
    for copy in leave:
        copy.wait()


def tables():
    rate = 10000.0 ** (-2.0 * np.arange(ROT // 2) / ROT)
    rate = np.concatenate([rate, rate])[:, None]
    within = np.arange(TOK)[None, :] * rate
    blocks = np.arange(4)[:, None, None] * float(TOK) * rate[None] + np.zeros((1, 1, TOK))
    tab_t = np.stack([np.cos(within), np.sin(within)]).astype(np.float32)
    tab_b = np.stack([np.cos(blocks), np.sin(blocks)], axis=1).astype(np.float32)
    return tab_t, tab_b


def per_device(tokens, target, norm_gain, qkv_weight, out_weight, probe_seed, block_order):
    tab_t, tab_b = tables()
    anywhere = pl.BlockSpec(memory_space=pl.ANY)
    smem = pl.BlockSpec(memory_space=pltpu.SMEM)
    v = pltpu.VMEM
    scratch = [
        v((COLS, SHARE), BF), v((HS, SHARE), BF), v((1, D), F32), v((2, ROT, TOK), F32), v((4, 2, ROT, TOK), F32),
        v((TOK, D), BF), v((TOK, PART), BF), v((COLS, D), BF), v((TOK, D), BF), v((2, COLS, TOK), F32),
        v((2, TOK, 128), F32), v((4, TOK, SHARE), BF), v((4, 4 * HS + 16, TOK), BF),
        v((4, 4, HALF, PART), BF), v((2, 4, 4, HALF, PART), BF), v((2, 4, 4, HALF, PART), BF),
        v((2, 4, 2 * PART, 4 * HALF), BF),
        v((2, 4, 4, HALF, 2 * SPAN), BF), v((2, 4, 4, HALF, 2 * SPAN), BF),
        v((2, 2 * SPAN, 2 * HS), BF), v((2, HS, 2 * SPAN), BF), v((2, 2 * SPAN, 2 * HS), BF),
        v((2, 2 * SPAN, 1024), F32), v((TOK, 1024), F32), v((TOK, 1024), F32),
        v((2, 2 * SPAN, 1024), BF), v((2, 2 * SPAN, 1024), BF),
        v((4, HS, TOK), F32), v((4, HS, TOK), F32), v((HS, TOK), F32),
        v((2, PART, 2 * SPAN), F32), v((2, PART, 2 * SPAN), BF), v((2, PART, 2 * SPAN), BF),
        v((2, PART, 2 * SPAN), F32), v((2, PART, 2 * SPAN), BF), v((4 * SPAN, PART), BF), v((PART, TOK), F32),
        v((2, 2, 4, 4, HALF, 2 * SPAN), BF),
        v((2, 3, 4, HALF, 2 * SPAN), BF), v((2, 3, 4, HALF, 2 * SPAN), BF),
        v((2, 4, HALF, 2 * SPAN), BF), v((2, 4, HALF, 2 * SPAN), BF),
        v((2, 3, HALF, 2 * SPAN), BF), v((2, 3, HALF, 2 * SPAN), BF),
        v((4, 4, HALF, PART), BF), v((4, 4, HALF, PART), BF),
        v((2, 4, HALF, PART), BF), v((2, 4, HALF, PART), BF),
        v((4, HALF, PART), BF), v((4, HALF, PART), BF), v((4, HALF, PART), BF), v((4, HALF, PART), BF),
        v((4, HALF, PART), BF), v((4, HALF, PART), BF), v((4, HALF, PART), BF), v((4, HALF, PART), BF),
        v((4, HS, TOK), BF), v((2, HS, TOK), BF), v((2, HS, TOK), BF), v((2, HS, TOK), BF),
        v((4, HS, TOK), BF), v((2, HS, TOK), BF), v((2, HS, TOK), BF), v((2, HS, TOK), BF),
        v((4, 3 * HS, TOK), BF), v((COLS, SHARE), F32), v((COLS, SHARE), F32),
        pltpu.SemaphoreType.DMA((N_REMOTE,)), pltpu.SemaphoreType.DMA((N_REMOTE,)),
        pltpu.SemaphoreType.DMA((N_LOCAL,)),
    ]
    product, out_curv = pl.pallas_call(
        kernel,
        out_shape=(
            jax.ShapeDtypeStruct((COLS, SHARE), BF),
            jax.ShapeDtypeStruct((HS, SHARE), BF),
        ),
        in_specs=[anywhere, anywhere, anywhere, anywhere, anywhere, smem, smem, anywhere, anywhere],
        out_specs=(anywhere, anywhere),
        scratch_shapes=scratch,
        compiler_params=pltpu.CompilerParams(
            collective_id=0, has_side_effects=True, vmem_limit_bytes=60 * 2**20
        ),
    )(
        tokens, target, norm_gain.reshape(1, D), qkv_weight.T, out_weight, probe_seed, block_order,
        jnp.asarray(tab_t), jnp.asarray(tab_b),
    )
    product, out_curv = pl.pallas_call(
        widen,
        out_shape=(
            jax.ShapeDtypeStruct((COLS, SHARE), F32),
            jax.ShapeDtypeStruct((HS, SHARE), F32),
        ),
        in_specs=[anywhere, anywhere],
        out_specs=(anywhere, anywhere),
        scratch_shapes=[
            v((3, COLS, SHARE // 3), BF), v((HS, SHARE), BF),
            v((3, COLS, SHARE // 3), F32), v((HS, SHARE), F32),
            pltpu.SemaphoreType.DMA((4,)), pltpu.SemaphoreType.DMA((4,)),
        ],
    )(product, out_curv)
    return product.T, out_curv


def solution(mesh):
    placed = (P("seq", None), P("seq", None), P(), P(None, "fsdp"), P("fsdp", None), P(), P("seq"))
    return jax.shard_map(
        per_device,
        mesh=mesh,
        in_specs=placed,
        out_specs=(P("seq", "fsdp"), P("fsdp", "seq")),
        check_vma=False,
    )
```

```python
import functools
import math

import jax
import jax.numpy as jnp
import numpy as np
from jax import lax
from jax.experimental import pallas as pl
from jax.experimental.pallas import tpu as pltpu
from jax.sharding import PartitionSpec as P

MESH = pl.DeviceIdType.MESH
BF = jnp.bfloat16
F32 = jnp.float32
D = 6144
HS = 96
ROT = 24
TOK = 256
COLS = 288
WIDE = 9216
INNER = 3072
SHARE = 1536
PART = 384
HALF = 48
SPAN = 128
KEYS = 2 * HS + 16
STEP = 768
MIX = (-1640531535, -2048144789, -1028477387)
N_REMOTE = 40
N_LOCAL = 25


def wrap(value):
    return ((value + 2**31) % 2**32) - 2**31


def shifted(state, places):
    return lax.shift_right_logical(state, jnp.full(state.shape, places, jnp.int32))


def sign_bit(state):
    state = state ^ shifted(state, 16)
    state = state * jnp.int32(MIX[1])
    state = state ^ shifted(state, 13)
    state = state * jnp.int32(MIX[2])
    return (state ^ shifted(state, 16)) & jnp.int32(128)


def dot(a, b, contract):
    return lax.dot_general(a, b, (contract, ((), ())), preferred_element_type=F32)


NN = ((1,), (0,))
NT = ((1,), (1,))
TN = ((0,), (0,))


class Group:
    def __init__(self, size, send, recv):
        self.size, self.send, self.recv = size, send, recv

    def wait_recv(self):
        pltpu.make_async_copy(self.size, self.size, self.recv).wait()

    def wait_send(self):
        pltpu.make_async_copy(self.size, self.size, self.send).wait()


def kernel(
    tok_in, tgt_in, gain_in, wq_in, wo_in, seed_in, block_in, tab_t_in, tab_b_in,
    oq_out, oo_out,
    seed, block, oq, oo, gain, tab_t, tab_b, tok, tgt, wq, nrm, acc,
    stat, nb, gkv,
    wt, ww, pp, wpt, ga, gb,
    qq, qk, gg, score, prob, prob_tan, rnd, slope, cv_acc, ck_acc, cq_acc,
    mix_acc, mix_out, mix_in, grads, grad, turn, resid,
    sab, ra1, rb1, sa2, sb2, ra2, rb2,
    ha, hb, ca, cb, xa, xb, ya, yb, fa, fb, oa, ob,
    cv, cvr, cvs, cvf, ck, ckr, cks, ckf, cot, sgn, acc_q, out_acc,
    send, recv, local,
):
    fs = lax.axis_index("fsdp")
    s = lax.axis_index("seq")
    x = fs // 8
    yl = (fs // 4) % 2
    z = fs % 4
    yh = s // 2
    c = s % 2
    s_sib = yh * 2 + (1 - c)
    s_crs = (1 - yh) * 2 + c
    s_crd = (1 - yh) * 2 + (1 - c)
    own_cols = (x * 4 + z) * PART

    def device(px, py, pz, ps):
        return ((px * 2 + py) * 4 + pz, ps)

    def xp(d):
        return device((x + d) % 4, yl, z, s)

    def zp(d):
        return device(x, yl, (z + d) % 4, s)

    def fin(d):
        return device(s, yl, (z + d) % 4, x)

    partner = device(x, 1 - yl, z, s)
    sib = device(x, yl, z, s_sib)
    crs = device(x, yl, z, s_crs)
    crd = device(x, yl, z, s_crd)

    count = [0]
    sent = []

    def group(size):
        i = count[0]
        count[0] += 1
        sent.append(Group(size, send.at[i], recv.at[i]))
        return sent[-1]

    def remote(src, dst, to, within=None, begin=True):
        held = within or group(dst)
        copy = pltpu.make_async_remote_copy(
            src_ref=src, dst_ref=dst, send_sem=held.send, recv_sem=held.recv,
            device_id=to, device_id_type=MESH,
        )
        if begin:
            copy.start()
        return copy if not begin else held

    local_count = [0]

    def stay(src, dst):
        i = local_count[0]
        local_count[0] += 1
        copy = pltpu.make_async_copy(src, dst, local.at[i])
        copy.start()
        return copy

    def nearby(src, dst):
        i = local_count[0]
        local_count[0] += 1
        return pltpu.make_async_copy(src, dst, local.at[i])

    def arrived(copies):
        for copy in copies:
            copy.wait_recv()

    def lanes(start, size):
        return pl.ds(pl.multiple_of(start, 128), size)

    def rows(start, size):
        return pl.ds(pl.multiple_of(start, 16), size)

    tok_loads = [stay(tok_in.at[pl.ds(k * 64, 64)], tok.at[pl.ds(k * 64, 64)]) for k in range(4)]
    tab_loads = [stay(seed_in, seed), stay(block_in, block), stay(gain_in, gain), stay(tab_t_in, tab_t), stay(tab_b_in, tab_b)]
    tgt_load = stay(tgt_in.at[:, lanes(own_cols, PART)], tgt)
    first, second = jnp.where(c == 0, x, z), jnp.where(c == 0, z, x)

    def column(a, k):
        return jnp.where(c == 0, a * 4 + k, k * 4 + a) * PART

    own_w = [
        stay(wo_in.at[rows(c * HALF, HALF), lanes(column(first, k), PART)], wt.at[first, k])
        for k in range(4)
    ]

    barrier = pltpu.get_barrier_semaphore()

    def greet(to):
        pl.semaphore_signal(barrier, inc=1, device_id=to, device_id_type=MESH)

    for d in (1, 2, 3):
        greet(xp(d))
        greet(zp(d))
    for to in (partner, sib, crs, crd):
        greet(to)

    @pl.when(x != s)
    def _():
        for d in range(4):
            greet(fin(d))


    def norm_sums(i, carry):
        at = rows(i * 16, 16)
        totals = [jnp.zeros((16, 128), F32) for _ in range(2)]
        for k in range(D // 128):
            totals[k % 2] += tok[at, k * 128 : (k + 1) * 128].astype(F32)
        stat[0, at, :] = totals[0] + totals[1]
        return carry

    for k in range(4):
        tok_loads[k].wait()
        lax.fori_loop(k * 4, (k + 1) * 4, norm_sums, 0, unroll=2)
    wq_load = stay(wq_in, wq)
    average = jnp.sum(stat[0], axis=-1, keepdims=True) * (1 / D)
    stat[0] = jnp.broadcast_to(average, (TOK, 128))

    def norm_squares(i, carry):
        at = rows(i * 16, 16)
        middle = stat[0, at, :]
        totals = [jnp.zeros((16, 128), F32) for _ in range(2)]
        for k in range(D // 128):
            centred = tok[at, k * 128 : (k + 1) * 128].astype(F32) - middle
            totals[k % 2] += centred * centred
        stat[1, at, :] = totals[0] + totals[1]
        return carry

    lax.fori_loop(0, TOK // 16, norm_squares, 0, unroll=2)
    spread = jnp.sum(stat[1], axis=-1, keepdims=True) * (1 / D)
    stat[1] = jnp.broadcast_to(lax.rsqrt(spread + 1e-05), (TOK, 128))

    pl.semaphore_wait(barrier, jnp.where(x != s, 14, 10))

    def along_first(d):
        return device(
            jnp.where(c == 0, (x + d) % 4, x), yl, jnp.where(c == 0, z, (z + d) % 4), s
        )

    def along_second(d):
        return device(
            jnp.where(c == 0, x, (x + d) % 4), yl, jnp.where(c == 0, (z + d) % 4, z), s
        )

    w_one = group(wt.at[pl.ds(0, 3)])
    for d in (1, 2, 3):
        for k in range(4):
            remote(
                wo_in.at[rows(c * HALF, HALF), lanes(column((first + d) % 4, k), PART)],
                wt.at[first, k], along_first(d), w_one,
            )

    for copy in tab_loads:
        copy.wait()

    def norm_rows(i, carry):
        at = rows(i * 16, 16)
        middle, factor = stat[0, at, :], stat[1, at, :]
        for k in range(D // 128):
            cols = slice(k * 128, (k + 1) * 128)
            nrm[at, cols] = ((tok[at, cols].astype(F32) - middle) * factor * gain[:, cols]).astype(BF)
        return carry

    lax.fori_loop(0, TOK // 16, norm_rows, 0)

    piece = jnp.where(c == 0, z * 4 + x, x * 4 + z) * 16
    n_far = group(nb.at[0, pl.ds(0, 32)])
    remote(
        nrm.at[rows(piece, 16), lanes(s_crs * SHARE, SHARE)], nb.at[s, rows(piece, 16)], crs, n_far
    )
    remote(
        nrm.at[rows(piece, 16), lanes(s_crd * SHARE, SHARE)], nb.at[s, rows(piece, 16)], crd, n_far
    )
    n_sib = remote(nrm.at[:, lanes(s_sib * SHARE, SHARE)], nb.at[s], sib)

    wq_load.wait()
    acc[...] = jnp.zeros_like(acc)
    seeded = seed[0]
    q_probe = float(np.float32(1 / math.sqrt(D)).astype(jnp.bfloat16))
    o_probe = float(np.float32(1 / math.sqrt(INNER)).astype(jnp.bfloat16))

    def project(start, size):
        q_rows = lax.broadcasted_iota(jnp.int32, (size, STEP), 1)
        q_cols = lax.broadcasted_iota(jnp.int32, (size, STEP), 0)
        q_base = (q_rows * WIDE + q_cols + (fs * COLS + start)) * jnp.int32(MIX[0]) + seeded
        to = pl.ds(start, size)

        def step(i, carry):
            at = pl.ds(pl.multiple_of(i * STEP, STEP), STEP)
            bit = sign_bit(q_base + i * jnp.int32(wrap(STEP * WIDE * MIX[0])))
            probe = jnp.where(bit == 0, F32(q_probe), F32(-q_probe)).astype(BF)
            both = dot(jnp.concatenate([wq[to, at], probe], axis=0), nrm[:, at], NT)
            acc[0, to] += both[:size]
            acc[1, to] += both[size:]
            return carry

        lax.fori_loop(0, D // STEP, step, 0)

    project(HS, 2 * HS)

    number = block[0]
    low = lax.broadcasted_iota(jnp.int32, (ROT, TOK), 0) < ROT // 2

    def trig(here):
        cos_b = jnp.zeros((ROT, TOK), F32)
        sin_b = jnp.zeros((ROT, TOK), F32)
        for k in range(4):
            cos_b = jnp.where(here == k, tab_b[k, 0], cos_b)
            sin_b = jnp.where(here == k, tab_b[k, 1], sin_b)
        cos = cos_b * tab_t[0] - sin_b * tab_t[1]
        sin = sin_b * tab_t[0] + cos_b * tab_t[1]
        return cos, jnp.where(low, -sin, sin)

    own_trig = trig(jnp.full((ROT, TOK), number, jnp.int32))

    def rotate(field, turns, sign=1.0):
        cos, sin = turns
        head = field[:ROT]
        swapped = pltpu.roll(head, ROT // 2, 0)
        return jnp.concatenate([head * cos + swapped * (sin * sign), field[ROT:]], axis=0)

    for k in range(2):
        gkv[s, k * HS : (k + 1) * HS] = rotate(acc[k, HS : 2 * HS], own_trig).astype(BF)
    gkv[s, KEYS - 16 : KEYS] = jnp.full((16, TOK), number, jnp.int32).astype(F32).astype(BF)
    k_part, v_part = pl.ds(0, KEYS), pl.ds(KEYS, 2 * HS)

    def spread_kv(slot, part, to):
        return remote(gkv.at[slot, part], gkv.at[slot, part], to)

    k_crs = spread_kv(s, k_part, crs)
    k_sib = spread_kv(s, k_part, sib)
    for k in range(2):
        gkv[s, KEYS + k * HS : KEYS + (k + 1) * HS] = acc[k, 2 * HS : 3 * HS].astype(BF)
    v_crs = spread_kv(s, v_part, crs)
    v_sib = spread_kv(s, v_part, sib)

    def span(h):
        return slice(h * SPAN, (h + 1) * SPAN)

    tgt_load.wait()
    project(0, HS)
    q = rotate(acc[0, :HS], own_trig).astype(BF)
    q_tan = rotate(acc[1, :HS], own_trig).astype(BF)
    for h in range(2):
        one, two = q[:, span(h)], q_tan[:, span(h)]
        qq[h] = jnp.concatenate(
            [jnp.concatenate([one, two], axis=1), jnp.concatenate([jnp.zeros_like(one), one], axis=1)],
            axis=0,
        ).astype(F32).T.astype(BF)
        qk[h] = jnp.concatenate([one, two], axis=1)
    resid[...] = (tok[:, lanes(own_cols, PART)].astype(F32) - tgt[...].astype(F32)).T

    b0 = (1 - yh) * 2
    b1 = b0 + 1
    arrived([n_far])
    n_one = group(nb.at[0, pl.ds(0, 96)])
    for d in (1, 2, 3):
        at0 = nb.at[b0, rows((z * 4 + x) * 16, 16)]
        at1 = nb.at[b1, rows((x * 4 + z) * 16, 16)]
        remote(at0, at0, xp(d), n_one)
        remote(at1, at1, zp(d), n_one)

    for copy in own_w:
        copy.wait()
    arrived([w_one])
    w_two = group(ww.at[0, pl.ds(0, 3)])
    for d in (1, 2, 3):
        remote(wt.at[:, (second + d) % 4], ww.at[c, second], along_second(d), w_two)
    own_ww = stay(wt.at[:, second], ww.at[c, second])

    o_rows = lax.broadcasted_iota(jnp.int32, (HALF, PART), 0)
    o_lanes = lax.broadcasted_iota(jnp.int32, (HALF, PART), 1)
    o_base = (o_rows * D + o_lanes + (D * WIDE + own_cols)) * jnp.int32(MIX[0]) + seeded

    def probe_piece(i, carry):
        for k in range(4):
            first = ((k * 2 + yl) * 4 + i) * HS
            second = ((i * 2 + yl) * 4 + k) * HS + HALF
            bit = sign_bit(o_base + first * jnp.int32(wrap(D * MIX[0])))
            pp[0, i, k] = jnp.where(bit == 0, F32(o_probe), F32(-o_probe)).astype(BF)
            bit = sign_bit(o_base + second * jnp.int32(wrap(D * MIX[0])))
            pp[1, i, k] = jnp.where(bit == 0, F32(o_probe), F32(-o_probe)).astype(BF)
        return carry

    lax.fori_loop(0, 4, probe_piece, 0)

    def turned(source, start):
        def turn(i, carry):
            for a in range(2):
                value = source[a, i].reshape(4 * HALF, PART).astype(F32)
                wpt[a, i, start : start + PART] = value.T.astype(BF)
            return carry

        lax.fori_loop(0, 4, turn, 0)

    turned(pp, PART)

    def spread_normed(cols):
        held = group(nb.at[pl.ds(0, 2), pl.ds(0, 192), cols])
        for d in (1, 2, 3):
            at0 = nb.at[b0, rows(z * 64, 64), cols]
            at1 = nb.at[b1, rows(x * 64, 64), cols]
            remote(at0, at0, zp(d), held)
            remote(at1, at1, xp(d), held)
        return held

    arrived([k_crs])
    k_rel = spread_kv(s_crs, k_part, sib)
    arrived([v_crs])
    v_rel = spread_kv(s_crs, v_part, sib)

    arrived([k_sib, k_rel])
    root = 1 / math.sqrt(HS)

    def keys_of(b):
        return lanes(b * TOK, TOK)

    def pulls(left, part, h):
        def pull(b, carry):
            score[h, :, keys_of(b)] = dot(left[h], gkv[b, part], NN)
            return carry

        lax.fori_loop(0, 4, pull, 0, unroll=2)

    along = lax.broadcasted_iota(jnp.int32, (1, TOK), 1).astype(F32)
    key_pos = jnp.concatenate(
        [gkv[b, KEYS - 16 : KEYS].astype(F32)[0:1] * float(TOK) + along for b in range(4)], axis=1
    )
    number_f = jnp.full((32, 1), number, jnp.int32).astype(F32)
    down = lax.broadcasted_iota(jnp.int32, (32, 1), 0)

    def soft(h):
        def soft_rows(i, carry):
            at = pl.ds(pl.multiple_of(h * SPAN + i * 32, 32), 32)
            low, high = pl.ds(pl.multiple_of(i * 32, 32), 32), pl.ds(pl.multiple_of(SPAN + i * 32, 32), 32)
            query_pos = number_f * float(TOK) + (down + (h * SPAN + i * 32)).astype(F32)
            allowed = key_pos <= query_pos
            values = jnp.where(allowed, score[h, low, :] * root, -1e30)
            highest = jnp.max(values, axis=-1, keepdims=True)
            weights = jnp.exp(values - highest)
            weights = weights * (1.0 / jnp.sum(weights, axis=-1, keepdims=True))
            moved = weights * (score[h, high, :] * root)
            moved = moved - weights * jnp.sum(moved, axis=-1, keepdims=True)
            prob[at, :] = weights
            prob_tan[at, :] = moved
            rnd[h, high, :] = weights.astype(BF)
            rnd[h, low, :] = moved.astype(BF)
            return carry

        lax.fori_loop(0, SPAN // 32, soft_rows, 0, unroll=2)

    def joint(part, ref, h):
        def term(b, held):
            return held + dot(gkv[b, part], ref[h, :, keys_of(b)], NT)

        return lax.fori_loop(0, 4, term, jnp.zeros((2 * HS, 2 * SPAN), F32))

    def attn_products(h):
        terms = joint(v_part, rnd, h)
        both = jnp.concatenate([terms[:HS, SPAN:], terms[:HS, :SPAN] + terms[HS:, SPAN:]], axis=1)
        both = both.astype(BF)
        ga[h, z, x] = both[:HALF]
        gb[h, x, z] = both[HALF:]
        held = group(ra1.at[0, pl.ds(0, 3), pl.ds(0, 2)])
        for d in (1, 2, 3):
            remote(ga.at[h, z, x], ga.at[h, z, x], xp(d), held)
            remote(gb.at[h, x, z], gb.at[h, x, z], zp(d), held)
        return held

    def gather_two(h):
        held = group(ra1)
        for d in (1, 2, 3):
            remote(ga.at[h, z], ga.at[h, z], zp(d), held)
            remote(gb.at[h, x], gb.at[h, x], xp(d), held)
        return held

    pulls(qq, pl.ds(0, 2 * HS), 0)
    soft(0)
    arrived([v_sib, v_rel])
    g_one = [attn_products(0)]
    pulls(qq, pl.ds(0, 2 * HS), 1)
    own_ww.wait()
    arrived([w_two])
    w_sib = remote(ww.at[c], ww.at[c], sib)
    soft(1)

    g_one.append(attn_products(1))

    arrived([g_one[0]])
    g_two = [gather_two(0)]
    arrived([w_sib])
    turned(ww, 0)
    arrived([g_one[1]])
    g_two.append(gather_two(1))
    arrived([n_one])
    n_two = [spread_normed(pl.ds(0, SHARE // 2))]

    def mix(h):
        arrived([g_two[h]])
        total = jnp.zeros((2 * PART, 2 * SPAN), F32)
        for a, ref in enumerate((ga, gb)):
            for i in range(4):
                total = total + dot(wpt[a, i], ref[h, i].reshape(4 * HALF, 2 * SPAN), NN)
        mix_acc[h, :, 0:SPAN] = total[:PART, :SPAN]
        mix_acc[h, :, SPAN:] = total[:PART, SPAN:] + total[PART:, :SPAN]
        mix_out[h] = mix_acc[h].astype(BF)
        return remote(mix_out.at[h], mix_in.at[h], partner)

    m_both = [mix(0), mix(1)]

    s_base = (
        (lax.broadcasted_iota(jnp.int32, (COLS, TOK), 1) + s * SHARE) * WIDE
        + lax.broadcasted_iota(jnp.int32, (COLS, TOK), 0)
        + fs * COLS
    ) * jnp.int32(MIX[0]) + seeded

    def sign_cols(i, carry):
        bit = sign_bit(s_base + i * jnp.int32(wrap(TOK * WIDE * MIX[0])))
        sgn[:, lanes(i * TOK, TOK)] = jnp.where(bit == 0, F32(math.sqrt(D)), F32(-math.sqrt(D)))
        return carry

    lax.fori_loop(0, SHARE // TOK, sign_cols, 0)

    def back(h):
        arrived([m_both[h]])
        grads[h] = mix_acc[h] + mix_in[h].astype(F32)
        grads[h, :, 0:SPAN] += resid[:, span(h)]
        grad[h] = (grads[h] * (1 / 1024)).astype(BF)

        def step(a, carry):
            for i in range(4):
                first = dot(ww[a, i].reshape(4 * HALF, PART), grad[h], NN)
                second = dot(pp[a, i].reshape(4 * HALF, PART), grad[h, :, 0:SPAN], NN)
                sab[h, a, i, :, :, 0:SPAN] = first[:, :SPAN].astype(BF).reshape(4, HALF, SPAN)
                sab[h, a, i, :, :, SPAN:] = (first[:, SPAN:] + second).astype(BF).reshape(4, HALF, SPAN)
            return carry

        lax.fori_loop(0, 2, step, 0)
        held = group(ra1)
        for d in (1, 2, 3):
            remote(sab.at[h, 0, (z + d) % 4], ra1.at[h, d - 1], zp(d), held)
            remote(sab.at[h, 1, (x + d) % 4], rb1.at[h, d - 1], xp(d), held)
        return held

    def total_of(own, others):
        total = own.astype(F32)
        for other in others:
            total = total + other.astype(F32)
        return total

    def scatter_two(h):
        arrived([r_one[h]])
        sa2[h] = total_of(sab[h, 0, z], [ra1[h, k] for k in range(3)]).astype(BF)
        sb2[h] = total_of(sab[h, 1, x], [rb1[h, k] for k in range(3)]).astype(BF)
        held = group(ra2)
        for d in (1, 2, 3):
            remote(sa2.at[h, (x + d) % 4], ra2.at[h, d - 1], xp(d), held)
            remote(sb2.at[h, (z + d) % 4], rb2.at[h, d - 1], zp(d), held)
        return held

    def scattered(h):
        arrived([r_two[h]])
        first = total_of(sa2[h, x], [ra2[h, k] for k in range(3)])
        second = total_of(sb2[h, z], [rb2[h, k] for k in range(3)])
        return jnp.concatenate([first.astype(BF), second.astype(BF)], axis=0)

    def out_terms(h):
        for k in range(2):
            at = slice((2 * h + k) * SPAN, (2 * h + k + 1) * SPAN)
            turn[at] = grad[h, :, (1 - k) * SPAN : (2 - k) * SPAN].astype(F32).T.astype(BF)

        def term(i, carry):
            right = turn[2 * h * SPAN : 2 * (h + 1) * SPAN]
            for a, (ref, to) in enumerate(((ga, ha), (gb, hb))):
                total = dot(ref[h, i].reshape(4 * HALF, 2 * SPAN), right, NN)
                if h == 0:
                    out_acc[a, i] = total
                else:
                    to[i] = (out_acc[a, i] + total).astype(BF).reshape(4, HALF, PART)
            return carry

        lax.fori_loop(0, 4, term, 0)

    r_one = [back(0)]
    out_terms(0)
    r_one.append(back(1))
    out_terms(1)

    o_core = group(ha)
    for k in range(2):
        remote(ha.at[:, 2 * k + 1 - c], ca.at[k], sib, o_core)
        remote(hb.at[2 * k + 1 - c], cb.at[k], sib, o_core)
    r_two = [scatter_two(0)]

    arrived([o_core])
    far = 1 - yh
    xa[...] = total_of(ha[:, 2 * far + c], [ca[far]]).astype(BF)
    xb[...] = total_of(hb[2 * far + c], [cb[far]]).astype(BF)
    o_crs = group(ca)
    remote(xa, ya, crs, o_crs)
    remote(xb, yb, crs, o_crs)

    cv_acc[...] = jnp.zeros_like(cv_acc)
    ck_acc[...] = jnp.zeros_like(ck_acc)

    def soft_back(h):
        def rows_back(i, carry):
            at = pl.ds(pl.multiple_of(h * SPAN + i * 32, 32), 32)
            low, high = pl.ds(pl.multiple_of(i * 32, 32), 32), pl.ds(pl.multiple_of(SPAN + i * 32, 32), 32)
            weights, moved = prob[at, :], prob_tan[at, :]
            pulled, pulled_tan = score[h, low, :], score[h, high, :]
            base = jnp.sum(weights * pulled, axis=-1, keepdims=True)
            base_tan = jnp.sum(moved * pulled + weights * pulled_tan, axis=-1, keepdims=True)
            less = pulled - base
            slope[h, high, :] = (weights * less).astype(BF)
            slope[h, low, :] = (moved * less + weights * (pulled_tan - base_tan)).astype(BF)
            return carry

        lax.fori_loop(0, SPAN // 32, rows_back, 0, unroll=2)

    def value_terms(h, g):
        def step(b, carry):
            cv_acc[b] += dot(g, rnd[h, :, keys_of(b)], NN)
            return carry

        lax.fori_loop(0, 4, step, 0, unroll=2)

    def slopes(h, g):
        one, two = g[:, :SPAN], g[:, SPAN:]
        gg[h] = jnp.concatenate(
            [jnp.concatenate([one, two], axis=1), jnp.concatenate([jnp.zeros_like(one), one], axis=1)],
            axis=0,
        ).astype(F32).T.astype(BF)
        pulls(gg, v_part, h)
        soft_back(h)

    def key_terms(h):
        def step(b, carry):
            ck_acc[b] += dot(qk[h], slope[h, :, keys_of(b)], NN)
            return carry

        lax.fori_loop(0, 4, step, 0, unroll=2)

    def query_terms(h):
        terms = joint(pl.ds(0, 2 * HS), slope, h)
        cq_acc[:, span(h)] = terms[:HS, :SPAN] + terms[HS:, SPAN:]

    def chip_sums(own, other, kept):
        for k in range(2):
            kept[k] = total_of(own[2 * k + c], [other[k]]).astype(BF)

    g_first = scattered(0)
    value_terms(0, g_first)
    r_two.append(scatter_two(1))
    slopes(0, g_first)
    key_terms(0)
    query_terms(0)

    g_second = scattered(1)
    n_two.append(spread_normed(pl.ds(SHARE // 2, SHARE // 2)))
    value_terms(1, g_second)
    cv[...] = cv_acc[...].astype(BF)
    v_core = group(cvr)
    for k in range(2):
        remote(cv.at[2 * k + 1 - c], cvr.at[k], sib, v_core)
    arrived([o_crs])
    fa[...] = total_of(ha[:, s], [ca[yh], ya[...]]).astype(BF)
    fb[...] = total_of(hb[s], [cb[yh], yb[...]]).astype(BF)
    o_fin = group(ca.at[0, pl.ds(0, 3)])
    o_fin_b = group(ca.at[0, pl.ds(0, 3)])
    for d in (1, 2, 3):
        other = (z + d) % 4
        remote(fa.at[other], oa.at[z], fin(d), o_fin)
        remote(fb.at[other], ob.at[z], fin(d), o_fin_b)
    lone = [Group(fa.at[z], send.at[count[0] + k], recv.at[count[0] + k]) for k in range(2)]
    count[0] += 2
    o_far = [
        remote(fa.at[z], oa.at[z], fin(0), lone[0], begin=False),
        remote(fb.at[z], ob.at[z], fin(0), lone[1], begin=False),
    ]
    o_near = [nearby(fa.at[z], oa.at[z]), nearby(fb.at[z], ob.at[z])]

    @pl.when(x != s)
    def _():
        for copy in o_far:
            copy.start()

    @pl.when(x == s)
    def _():
        for copy in o_near:
            copy.start()

    slopes(1, g_second)
    arrived([v_core])
    chip_sums(cv, cvr, cvs)
    v_far = remote(cvs, cvf, crs)
    key_terms(1)
    ck[...] = (ck_acc[...] * root).astype(BF)

    k_core = group(ckr)
    for k in range(2):
        remote(ck.at[2 * k + 1 - c], ckr.at[k], sib, k_core)
    query_terms(1)
    q_part, k_rows, head_part = pl.ds(0, HS), pl.ds(HS, HS), pl.ds(0, 2 * HS)
    tail_part = pl.ds(2 * HS, HS)
    cot[s, q_part] = rotate((cq_acc[...] * root).astype(BF).astype(F32), own_trig, -1.0).astype(BF)
    arrived([k_core])
    chip_sums(ck, ckr, cks)
    k_far = remote(cks, ckf, crs)
    q_far = remote(cot.at[s, q_part], cot.at[s, q_part], crs)

    arrived([v_far])
    for k in range(2):
        cot[2 * k + c, tail_part] = total_of(cvs[k], [cvf[k]]).astype(BF)
    t_tail = group(cvr)
    for k in range(2):
        remote(cot.at[2 * k + c, tail_part], cot.at[2 * k + c, tail_part], sib, t_tail)
    turns = [
        trig(jnp.broadcast_to(gkv[2 * k + c, KEYS - 16 : KEYS].astype(F32)[0:1], (ROT, TOK)))
        for k in range(2)
    ]
    arrived([n_sib] + n_two)

    def first_terms(part):
        def term(i, carry):
            at = lanes(i * TOK, TOK)
            acc_q[part, at] = dot(cot[s, part], nrm[:, lanes(s * SHARE + i * TOK, TOK)], NN) + dot(
                cot[s_crs, part], nb[s_crs, :, at], NN
            )
            return carry

        lax.fori_loop(0, SHARE // TOK, term, 0, unroll=2)

    def last_terms(part, start, stop):
        def term(i, carry):
            at = lanes(i * TOK, TOK)
            total = acc_q[part, at] + (
                dot(cot[s_sib, part], nb[s_sib, :, at], NN) + dot(cot[s_crd, part], nb[s_crd, :, at], NN)
            )
            oq[part, at] = (total * sgn[part, at]).astype(BF)
            return carry

        lax.fori_loop(start, stop, term, 0, unroll=3)

    first_terms(tail_part)
    arrived([t_tail])
    last_terms(tail_part, 0, 6)
    leaving = [stay(oq.at[tail_part], oq_out.at[tail_part])]

    arrived([k_far])
    for k in range(2):
        both = total_of(cks[k], [ckf[k]]).astype(BF).astype(F32)
        cot[2 * k + c, k_rows] = rotate(both, turns[k], -1.0).astype(BF)
    arrived([q_far])
    t_head = group(cot.at[pl.ds(0, 2), head_part])
    for k in range(2):
        remote(cot.at[2 * k + c, head_part], cot.at[2 * k + c, head_part], sib, t_head)
    first_terms(head_part)

    arrived([o_fin, o_fin_b])

    @pl.when(x != s)
    def _():
        for copy in o_far:
            copy.wait_recv()
            copy.wait_send()

    @pl.when(x == s)
    def _():
        for copy in o_near:
            copy.wait()

    e_base = (
        lax.broadcasted_iota(jnp.int32, (HALF, PART), 0) * D
        + lax.broadcasted_iota(jnp.int32, (HALF, PART), 1)
        + (D * WIDE + fs * HS * D + s * SHARE)
    ) * jnp.int32(MIX[0]) + seeded
    scale = math.sqrt(INNER)
    for half, ref in enumerate((oa, ob)):
        for k in range(4):
            bit = sign_bit(e_base + jnp.int32(wrap((half * HALF * D + k * PART) * MIX[0])))
            oo[half * HALF : (half + 1) * HALF, k * PART : (k + 1) * PART] = (
                ref[k].astype(F32) * jnp.where(bit == 0, F32(scale), F32(-scale))
            ).astype(BF)


    leaving.append(stay(oo, oo_out))
    arrived([t_head])
    for k in range(2):
        last_terms(head_part, k * 3, k * 3 + 3)
        cols = pl.ds(k * SHARE // 2, SHARE // 2)
        leaving.append(stay(oq.at[head_part, cols], oq_out.at[head_part, cols]))
    for copy in leaving:
        copy.wait()

    for copy in sent:
        copy.wait_send()


def widen(product_in, out_in, product, out, narrow, narrow_out, wide, wide_out, loads, stores):
    thirds = [pl.ds(k * SHARE // 3, SHARE // 3) for k in range(3)]
    parts = [(product_in.at[:, at], narrow.at[k], wide.at[k], product.at[:, at]) for k, at in enumerate(thirds)]
    parts.append((out_in, narrow_out, wide_out, out))
    arrive = [pltpu.make_async_copy(part[0], part[1], loads.at[k]) for k, part in enumerate(parts)]
    leave = [pltpu.make_async_copy(part[2], part[3], stores.at[k]) for k, part in enumerate(parts)]
    for copy in arrive:
        copy.start()
    for k, part in enumerate(parts):
        arrive[k].wait()
        part[2][...] = part[1][...].astype(F32)
        leave[k].start()
    for copy in leave:
        copy.wait()


def tables():
    rate = 10000.0 ** (-2.0 * np.arange(ROT // 2) / ROT)
    rate = np.concatenate([rate, rate])[:, None]
    within = np.arange(TOK)[None, :] * rate
    blocks = np.arange(4)[:, None, None] * float(TOK) * rate[None] + np.zeros((1, 1, TOK))
    tab_t = np.stack([np.cos(within), np.sin(within)]).astype(np.float32)
    tab_b = np.stack([np.cos(blocks), np.sin(blocks)], axis=1).astype(np.float32)
    return tab_t, tab_b


def per_device(tokens, target, norm_gain, qkv_weight, out_weight, probe_seed, block_order):
    tab_t, tab_b = tables()
    anywhere = pl.BlockSpec(memory_space=pl.ANY)
    v = pltpu.VMEM
    scratch = [
        pltpu.SMEM((1,), jnp.int32), pltpu.SMEM((1,), jnp.int32),
        v((COLS, SHARE), BF), v((HS, SHARE), BF), v((1, D), F32), v((2, ROT, TOK), F32), v((4, 2, ROT, TOK), F32),
        v((TOK, D), BF), v((TOK, PART), BF), v((COLS, D), BF), v((TOK, D), BF), v((2, COLS, TOK), F32),
        v((2, TOK, 128), F32), v((4, TOK, SHARE), BF), v((4, 4 * HS + 16, TOK), BF),
        v((4, 4, HALF, PART), BF), v((2, 4, 4, HALF, PART), BF), v((2, 4, 4, HALF, PART), BF),
        v((2, 4, 2 * PART, 4 * HALF), BF),
        v((2, 4, 4, HALF, 2 * SPAN), BF), v((2, 4, 4, HALF, 2 * SPAN), BF),
        v((2, 2 * SPAN, 2 * HS), BF), v((2, HS, 2 * SPAN), BF), v((2, 2 * SPAN, 2 * HS), BF),
        v((2, 2 * SPAN, 1024), F32), v((TOK, 1024), F32), v((TOK, 1024), F32),
        v((2, 2 * SPAN, 1024), BF), v((2, 2 * SPAN, 1024), BF),
        v((4, HS, TOK), F32), v((4, HS, TOK), F32), v((HS, TOK), F32),
        v((2, PART, 2 * SPAN), F32), v((2, PART, 2 * SPAN), BF), v((2, PART, 2 * SPAN), BF),
        v((2, PART, 2 * SPAN), F32), v((2, PART, 2 * SPAN), BF), v((4 * SPAN, PART), BF), v((PART, TOK), F32),
        v((2, 2, 4, 4, HALF, 2 * SPAN), BF),
        v((2, 3, 4, HALF, 2 * SPAN), BF), v((2, 3, 4, HALF, 2 * SPAN), BF),
        v((2, 4, HALF, 2 * SPAN), BF), v((2, 4, HALF, 2 * SPAN), BF),
        v((2, 3, HALF, 2 * SPAN), BF), v((2, 3, HALF, 2 * SPAN), BF),
        v((4, 4, HALF, PART), BF), v((4, 4, HALF, PART), BF),
        v((2, 4, HALF, PART), BF), v((2, 4, HALF, PART), BF),
        v((4, HALF, PART), BF), v((4, HALF, PART), BF), v((4, HALF, PART), BF), v((4, HALF, PART), BF),
        v((4, HALF, PART), BF), v((4, HALF, PART), BF), v((4, HALF, PART), BF), v((4, HALF, PART), BF),
        v((4, HS, TOK), BF), v((2, HS, TOK), BF), v((2, HS, TOK), BF), v((2, HS, TOK), BF),
        v((4, HS, TOK), BF), v((2, HS, TOK), BF), v((2, HS, TOK), BF), v((2, HS, TOK), BF),
        v((4, 3 * HS, TOK), BF), v((COLS, SHARE), F32), v((COLS, SHARE), F32), v((2, 4, 4 * HALF, PART), F32),
        pltpu.SemaphoreType.DMA((N_REMOTE,)), pltpu.SemaphoreType.DMA((N_REMOTE,)),
        pltpu.SemaphoreType.DMA((N_LOCAL,)),
    ]
    product, out_curv = pl.pallas_call(
        kernel,
        out_shape=(
            jax.ShapeDtypeStruct((COLS, SHARE), BF),
            jax.ShapeDtypeStruct((HS, SHARE), BF),
        ),
        in_specs=[anywhere] * 9,
        out_specs=(anywhere, anywhere),
        scratch_shapes=scratch,
        compiler_params=pltpu.CompilerParams(
            collective_id=0, has_side_effects=True, vmem_limit_bytes=60 * 2**20
        ),
    )(
        tokens, target, norm_gain.reshape(1, D), qkv_weight.T, out_weight, probe_seed, block_order,
        jnp.asarray(tab_t), jnp.asarray(tab_b),
    )
    product, out_curv = pl.pallas_call(
        widen,
        out_shape=(
            jax.ShapeDtypeStruct((COLS, SHARE), F32),
            jax.ShapeDtypeStruct((HS, SHARE), F32),
        ),
        in_specs=[anywhere, anywhere],
        out_specs=(anywhere, anywhere),
        scratch_shapes=[
            v((3, COLS, SHARE // 3), BF), v((HS, SHARE), BF),
            v((3, COLS, SHARE // 3), F32), v((HS, SHARE), F32),
            pltpu.SemaphoreType.DMA((4,)), pltpu.SemaphoreType.DMA((4,)),
        ],
    )(product, out_curv)
    return product.T, out_curv


def solution(mesh):
    placed = (P("seq", None), P("seq", None), P(), P(None, "fsdp"), P("fsdp", None), P(), P("seq"))
    return jax.shard_map(
        per_device,
        mesh=mesh,
        in_specs=placed,
        out_specs=(P("seq", "fsdp"), P("fsdp", "seq")),
        check_vma=False,
    )
```

```python
import functools
import math

import jax
import jax.numpy as jnp
import numpy as np
from jax import lax
from jax.experimental import pallas as pl
from jax.experimental.pallas import tpu as pltpu
from jax.sharding import PartitionSpec as P

MESH = pl.DeviceIdType.MESH
BF = jnp.bfloat16
F32 = jnp.float32
D = 6144
HS = 96
ROT = 24
TOK = 256
COLS = 288
WIDE = 9216
INNER = 3072
SHARE = 1536
PART = 384
HALF = 48
SPAN = 128
KEYS = 2 * HS + 16
STEP = 768
MIX = (-1640531535, -2048144789, -1028477387)
N_REMOTE = 48
N_LOCAL = 25


def wrap(value):
    return ((value + 2**31) % 2**32) - 2**31


def shifted(state, places):
    return lax.shift_right_logical(state, jnp.full(state.shape, places, jnp.int32))


def sign_bit(state):
    state = state ^ shifted(state, 16)
    state = state * jnp.int32(MIX[1])
    state = state ^ shifted(state, 13)
    state = state * jnp.int32(MIX[2])
    return (state ^ shifted(state, 16)) & jnp.int32(128)


def dot(a, b, contract):
    return lax.dot_general(a, b, (contract, ((), ())), preferred_element_type=F32)


NN = ((1,), (0,))
NT = ((1,), (1,))
TN = ((0,), (0,))


class Group:
    def __init__(self, size, send, recv):
        self.size, self.send, self.recv = size, send, recv

    def wait_recv(self):
        pltpu.make_async_copy(self.size, self.size, self.recv).wait()

    def wait_send(self):
        pltpu.make_async_copy(self.size, self.size, self.send).wait()


def kernel(
    tok_in, tgt_in, gain_in, wq_in, wo_in, seed_in, block_in, tab_t_in, tab_b_in,
    oq_out, oo_out,
    seed, block, oq, oo, gain, tab_t, tab_b, tok, tgt, wq, nrm, acc,
    stat, nb, gkv,
    wt, ww, pp, wpt, ga, gb,
    qq, qk, gg, score, prob, prob_tan, rnd, slope, cv_acc, ck_acc, cq_acc,
    mix_acc, mix_out, mix_in, back_acc, grad, turn, resid,
    sab, ra1, rb1, sa2, sb2, ra2, rb2,
    ha, hb, ca, cb, xa, xb, ya, yb, fa, fb, oa, ob,
    cv, cvr, cvs, cvf, ck, ckr, cks, ckf, cot, sgn, acc_q, out_acc,
    send, recv, local,
):
    fs = lax.axis_index("fsdp")
    s = lax.axis_index("seq")
    x = fs // 8
    yl = (fs // 4) % 2
    z = fs % 4
    yh = s // 2
    c = s % 2
    s_sib = yh * 2 + (1 - c)
    s_crs = (1 - yh) * 2 + c
    s_crd = (1 - yh) * 2 + (1 - c)
    own_cols = (x * 4 + z) * PART

    def device(px, py, pz, ps):
        return ((px * 2 + py) * 4 + pz, ps)

    def xp(d):
        return device((x + d) % 4, yl, z, s)

    def zp(d):
        return device(x, yl, (z + d) % 4, s)

    kept = (s + 2 * (x % 2)) % 4
    alone = (x == s) & (x % 2 == 0)

    def fin(d):
        return device(kept, yl, (z + d) % 4, x)

    def fin_from(d):
        return device(s, yl, (z + d) % 4, (x + 2 * (s % 2)) % 4)

    partner = device(x, 1 - yl, z, s)
    sib = device(x, yl, z, s_sib)
    crs = device(x, yl, z, s_crs)
    crd = device(x, yl, z, s_crd)

    count = [0]
    sent = []

    def group(size):
        i = count[0]
        count[0] += 1
        sent.append(Group(size, send.at[i], recv.at[i]))
        return sent[-1]

    def remote(src, dst, to, within=None, begin=True):
        held = within or group(dst)
        copy = pltpu.make_async_remote_copy(
            src_ref=src, dst_ref=dst, send_sem=held.send, recv_sem=held.recv,
            device_id=to, device_id_type=MESH,
        )
        if begin:
            copy.start()
        return copy if not begin else held

    local_count = [0]

    def stay(src, dst):
        i = local_count[0]
        local_count[0] += 1
        copy = pltpu.make_async_copy(src, dst, local.at[i])
        copy.start()
        return copy

    def nearby(src, dst):
        i = local_count[0]
        local_count[0] += 1
        return pltpu.make_async_copy(src, dst, local.at[i])

    def arrived(copies):
        for copy in copies:
            copy.wait_recv()

    def lanes(start, size):
        return pl.ds(pl.multiple_of(start, 128), size)

    def rows(start, size):
        return pl.ds(pl.multiple_of(start, 16), size)

    tok_loads = [stay(tok_in.at[pl.ds(k * 64, 64)], tok.at[pl.ds(k * 64, 64)]) for k in range(4)]
    tab_loads = [stay(seed_in, seed), stay(block_in, block), stay(gain_in, gain), stay(tab_t_in, tab_t), stay(tab_b_in, tab_b)]
    tgt_load = stay(tgt_in.at[:, lanes(own_cols, PART)], tgt)
    first, second = jnp.where(c == 0, x, z), jnp.where(c == 0, z, x)

    def column(a, k):
        return jnp.where(c == 0, a * 4 + k, k * 4 + a) * PART

    own_w = [
        stay(wo_in.at[rows(c * HALF, HALF), lanes(column(first, k), PART)], wt.at[first, k])
        for k in range(4)
    ]

    barrier = pltpu.get_barrier_semaphore()

    def greet(to):
        pl.semaphore_signal(barrier, inc=1, device_id=to, device_id_type=MESH)

    for d in (1, 2, 3):
        greet(xp(d))
        greet(zp(d))
    for to in (partner, sib, crs, crd):
        greet(to)

    for d in (1, 2, 3):
        greet(fin_from(d))

    @pl.when(jnp.logical_not(alone))
    def _():
        greet(fin_from(0))


    def norm_sums(i, carry):
        at = rows(i * 16, 16)
        totals = [jnp.zeros((16, 128), F32) for _ in range(2)]
        for k in range(D // 128):
            totals[k % 2] += tok[at, k * 128 : (k + 1) * 128].astype(F32)
        stat[0, at, :] = totals[0] + totals[1]
        return carry

    for k in range(4):
        tok_loads[k].wait()
        lax.fori_loop(k * 4, (k + 1) * 4, norm_sums, 0, unroll=2)
    wq_load = stay(wq_in, wq)
    average = jnp.sum(stat[0], axis=-1, keepdims=True) * (1 / D)
    stat[0] = jnp.broadcast_to(average, (TOK, 128))

    def norm_squares(i, carry):
        at = rows(i * 16, 16)
        middle = stat[0, at, :]
        totals = [jnp.zeros((16, 128), F32) for _ in range(2)]
        for k in range(D // 128):
            centred = tok[at, k * 128 : (k + 1) * 128].astype(F32) - middle
            totals[k % 2] += centred * centred
        stat[1, at, :] = totals[0] + totals[1]
        return carry

    lax.fori_loop(0, TOK // 16, norm_squares, 0, unroll=2)
    spread = jnp.sum(stat[1], axis=-1, keepdims=True) * (1 / D)
    stat[1] = jnp.broadcast_to(lax.rsqrt(spread + 1e-05), (TOK, 128))

    pl.semaphore_wait(barrier, jnp.where(alone, 13, 14))

    def along_first(d):
        return device(
            jnp.where(c == 0, (x + d) % 4, x), yl, jnp.where(c == 0, z, (z + d) % 4), s
        )

    def along_second(d):
        return device(
            jnp.where(c == 0, x, (x + d) % 4), yl, jnp.where(c == 0, (z + d) % 4, z), s
        )

    w_one = group(wt.at[pl.ds(0, 3)])
    for d in (1, 2, 3):
        for k in range(4):
            remote(
                wo_in.at[rows(c * HALF, HALF), lanes(column((first + d) % 4, k), PART)],
                wt.at[first, k], along_first(d), w_one,
            )

    for copy in tab_loads:
        copy.wait()

    def norm_rows(i, carry):
        at = rows(i * 16, 16)
        middle, factor = stat[0, at, :], stat[1, at, :]
        for k in range(D // 128):
            cols = slice(k * 128, (k + 1) * 128)
            nrm[at, cols] = ((tok[at, cols].astype(F32) - middle) * factor * gain[:, cols]).astype(BF)
        return carry

    lax.fori_loop(0, TOK // 16, norm_rows, 0)

    piece = jnp.where(c == 0, z * 4 + x, x * 4 + z) * 16
    n_far = group(nb.at[0, pl.ds(0, 32)])
    remote(
        nrm.at[rows(piece, 16), lanes(s_crs * SHARE, SHARE)], nb.at[s, rows(piece, 16)], crs, n_far
    )
    remote(
        nrm.at[rows(piece, 16), lanes(s_crd * SHARE, SHARE)], nb.at[s, rows(piece, 16)], crd, n_far
    )
    n_sib = remote(nrm.at[:, lanes(s_sib * SHARE, SHARE)], nb.at[s], sib)

    wq_load.wait()
    acc[...] = jnp.zeros_like(acc)
    seeded = seed[0]
    q_probe = float(np.float32(1 / math.sqrt(D)).astype(jnp.bfloat16))
    o_probe = float(np.float32(1 / math.sqrt(INNER)).astype(jnp.bfloat16))

    def project(start, size, steps=(0, D // STEP)):
        q_rows = lax.broadcasted_iota(jnp.int32, (size, STEP), 1)
        q_cols = lax.broadcasted_iota(jnp.int32, (size, STEP), 0)
        q_base = (q_rows * WIDE + q_cols + (fs * COLS + start)) * jnp.int32(MIX[0]) + seeded
        to = pl.ds(start, size)

        def step(i, carry):
            at = pl.ds(pl.multiple_of(i * STEP, STEP), STEP)
            bit = sign_bit(q_base + i * jnp.int32(wrap(STEP * WIDE * MIX[0])))
            probe = jnp.where(bit == 0, F32(q_probe), F32(-q_probe)).astype(BF)
            both = dot(jnp.concatenate([wq[to, at], probe], axis=0), nrm[:, at], NT)
            acc[0, to] += both[:size]
            acc[1, to] += both[size:]
            return carry

        lax.fori_loop(*steps, step, 0)

    project(HS, 2 * HS)

    number = block[0]
    low = lax.broadcasted_iota(jnp.int32, (ROT, TOK), 0) < ROT // 2

    def trig(here):
        cos_b = jnp.zeros((ROT, TOK), F32)
        sin_b = jnp.zeros((ROT, TOK), F32)
        for k in range(4):
            cos_b = jnp.where(here == k, tab_b[k, 0], cos_b)
            sin_b = jnp.where(here == k, tab_b[k, 1], sin_b)
        cos = cos_b * tab_t[0] - sin_b * tab_t[1]
        sin = sin_b * tab_t[0] + cos_b * tab_t[1]
        return cos, jnp.where(low, -sin, sin)

    own_trig = trig(jnp.full((ROT, TOK), number, jnp.int32))

    def rotate(field, turns, sign=1.0):
        cos, sin = turns
        head = field[:ROT]
        swapped = pltpu.roll(head, ROT // 2, 0)
        return jnp.concatenate([head * cos + swapped * (sin * sign), field[ROT:]], axis=0)

    for k in range(2):
        gkv[s, k * HS : (k + 1) * HS] = rotate(acc[k, HS : 2 * HS], own_trig).astype(BF)
    gkv[s, KEYS - 16 : KEYS] = jnp.full((16, TOK), number, jnp.int32).astype(F32).astype(BF)
    k_part, v_part = pl.ds(0, KEYS), pl.ds(KEYS, 2 * HS)

    def spread_kv(slot, part, to):
        return remote(gkv.at[slot, part], gkv.at[slot, part], to)

    k_crs = spread_kv(s, k_part, crs)
    k_sib = spread_kv(s, k_part, sib)
    for k in range(2):
        gkv[s, KEYS + k * HS : KEYS + (k + 1) * HS] = acc[k, 2 * HS : 3 * HS].astype(BF)
    v_crs = spread_kv(s, v_part, crs)
    v_sib = spread_kv(s, v_part, sib)

    def span(h):
        return slice(h * SPAN, (h + 1) * SPAN)

    tgt_load.wait()
    project(0, HS, (0, 4))

    for copy in own_w:
        copy.wait()
    arrived([w_one])
    w_two = group(ww.at[0, pl.ds(0, 3)])
    for d in (1, 2, 3):
        remote(wt.at[:, (second + d) % 4], ww.at[c, second], along_second(d), w_two)
    own_ww = stay(wt.at[:, second], ww.at[c, second])

    b0 = (1 - yh) * 2
    b1 = b0 + 1
    arrived([n_far])
    n_one = group(nb.at[0, pl.ds(0, 96)])
    for d in (1, 2, 3):
        at0 = nb.at[b0, rows((z * 4 + x) * 16, 16)]
        at1 = nb.at[b1, rows((x * 4 + z) * 16, 16)]
        remote(at0, at0, xp(d), n_one)
        remote(at1, at1, zp(d), n_one)

    project(0, HS, (4, D // STEP))

    q = rotate(acc[0, :HS], own_trig).astype(BF)
    q_tan = rotate(acc[1, :HS], own_trig).astype(BF)
    for h in range(2):
        one, two = q[:, span(h)], q_tan[:, span(h)]
        qq[h] = jnp.concatenate(
            [jnp.concatenate([one, two], axis=1), jnp.concatenate([jnp.zeros_like(one), one], axis=1)],
            axis=0,
        ).astype(F32).T.astype(BF)
        qk[h] = jnp.concatenate([one, two], axis=1)
    resid[...] = (tok[:, lanes(own_cols, PART)].astype(F32) - tgt[...].astype(F32)).T

    o_rows = lax.broadcasted_iota(jnp.int32, (HALF, PART), 0)
    o_lanes = lax.broadcasted_iota(jnp.int32, (HALF, PART), 1)
    o_base = (o_rows * D + o_lanes + (D * WIDE + own_cols)) * jnp.int32(MIX[0]) + seeded

    def probe_piece(i, carry):
        for k in range(4):
            first = ((k * 2 + yl) * 4 + i) * HS
            second = ((i * 2 + yl) * 4 + k) * HS + HALF
            bit = sign_bit(o_base + first * jnp.int32(wrap(D * MIX[0])))
            pp[0, i, k] = jnp.where(bit == 0, F32(o_probe), F32(-o_probe)).astype(BF)
            bit = sign_bit(o_base + second * jnp.int32(wrap(D * MIX[0])))
            pp[1, i, k] = jnp.where(bit == 0, F32(o_probe), F32(-o_probe)).astype(BF)
        return carry

    lax.fori_loop(0, 4, probe_piece, 0)

    def turned(source, start):
        def turn(i, carry):
            for a in range(2):
                value = source[a, i].reshape(4 * HALF, PART).astype(F32)
                wpt[a, i, start : start + PART] = value.T.astype(BF)
            return carry

        lax.fori_loop(0, 4, turn, 0)

    turned(pp, PART)

    def spread_normed(cols):
        held = group(nb.at[pl.ds(0, 2), pl.ds(0, 192), cols])
        for d in (1, 2, 3):
            at0 = nb.at[b0, rows(z * 64, 64), cols]
            at1 = nb.at[b1, rows(x * 64, 64), cols]
            remote(at0, at0, zp(d), held)
            remote(at1, at1, xp(d), held)
        return held

    arrived([k_crs])
    k_rel = spread_kv(s_crs, k_part, sib)

    root = 1 / math.sqrt(HS)

    def keys_of(b):
        return lanes(b * TOK, TOK)

    def pulls(left, part, h, blocks=range(4)):
        for b in blocks:
            score[h, :, keys_of(b)] = dot(left[h], gkv[b, part], NN)

    along = lax.broadcasted_iota(jnp.int32, (1, TOK), 1).astype(F32)
    number_f = jnp.full((32, 1), number, jnp.int32).astype(F32)
    down = lax.broadcasted_iota(jnp.int32, (32, 1), 0)

    def soft(h):
        def soft_rows(i, carry):
            at = pl.ds(pl.multiple_of(h * SPAN + i * 32, 32), 32)
            low, high = pl.ds(pl.multiple_of(i * 32, 32), 32), pl.ds(pl.multiple_of(SPAN + i * 32, 32), 32)
            query_pos = number_f * float(TOK) + (down + (h * SPAN + i * 32)).astype(F32)
            allowed = key_pos <= query_pos
            values = jnp.where(allowed, score[h, low, :] * root, -1e30)
            highest = jnp.max(values, axis=-1, keepdims=True)
            weights = jnp.exp(values - highest)
            weights = weights * (1.0 / jnp.sum(weights, axis=-1, keepdims=True))
            moved = weights * (score[h, high, :] * root)
            moved = moved - weights * jnp.sum(moved, axis=-1, keepdims=True)
            prob[at, :] = weights
            prob_tan[at, :] = moved
            rnd[h, high, :] = weights.astype(BF)
            rnd[h, low, :] = moved.astype(BF)
            return carry

        lax.fori_loop(0, SPAN // 32, soft_rows, 0, unroll=2)

    def joint(part, ref, h):
        def term(b, held):
            return held + dot(gkv[b, part], ref[h, :, keys_of(b)], NT)

        return lax.fori_loop(0, 4, term, jnp.zeros((2 * HS, 2 * SPAN), F32))

    def attn_products(h):
        terms = joint(v_part, rnd, h)
        both = jnp.concatenate([terms[:HS, SPAN:], terms[:HS, :SPAN] + terms[HS:, SPAN:]], axis=1)
        both = both.astype(BF)
        ga[h, z, x] = both[:HALF]
        gb[h, x, z] = both[HALF:]
        held = group(ra1.at[0, pl.ds(0, 3), pl.ds(0, 2)])
        for d in (1, 2, 3):
            remote(ga.at[h, z, x], ga.at[h, z, x], xp(d), held)
            remote(gb.at[h, x, z], gb.at[h, x, z], zp(d), held)
        return held

    def side(t):
        return pl.ds(t * SPAN, SPAN)

    def gather_two(h):
        groups = []
        for t in range(2):
            held = group(ra1.at[:, :, :, :, side(t)])
            for d in (1, 2, 3):
                at0, at1 = ga.at[h, z, :, :, side(t)], gb.at[h, x, :, :, side(t)]
                remote(at0, at0, zp(d), held)
                remote(at1, at1, xp(d), held)
            groups.append(held)
        return groups

    pulls(qq, pl.ds(0, 2 * HS), 0, (s, s_crs))
    pulls(qq, pl.ds(0, 2 * HS), 1, (s, s_crs))
    arrived([k_sib, k_rel])
    key_pos = jnp.concatenate(
        [gkv[b, KEYS - 16 : KEYS].astype(F32)[0:1] * float(TOK) + along for b in range(4)], axis=1
    )
    pulls(qq, pl.ds(0, 2 * HS), 0, (s_sib, s_crd))
    pulls(qq, pl.ds(0, 2 * HS), 1, (s_sib, s_crd))
    arrived([v_crs])
    v_rel = spread_kv(s_crs, v_part, sib)
    soft(0)
    arrived([v_sib, v_rel])
    g_one = [attn_products(0)]
    own_ww.wait()
    arrived([w_two])
    w_sib = remote(ww.at[c], ww.at[c], sib)
    soft(1)

    g_one.append(attn_products(1))

    arrived([g_one[0]])
    g_two = [gather_two(0)]
    arrived([w_sib])
    turned(ww, 0)
    arrived([g_one[1]])
    g_two.append(gather_two(1))
    arrived([n_one])
    n_two = [spread_normed(pl.ds(0, SHARE // 2))]

    s_base = (
        (lax.broadcasted_iota(jnp.int32, (COLS, TOK), 1) + s * SHARE) * WIDE
        + lax.broadcasted_iota(jnp.int32, (COLS, TOK), 0)
        + fs * COLS
    ) * jnp.int32(MIX[0]) + seeded

    def sign_cols(i, carry):
        bit = sign_bit(s_base + i * jnp.int32(wrap(TOK * WIDE * MIX[0])))
        sgn[:, lanes(i * TOK, TOK)] = jnp.where(bit == 0, F32(math.sqrt(D)), F32(-math.sqrt(D)))
        return carry

    lax.fori_loop(0, SHARE // TOK, sign_cols, 0)

    def products(h, t, tall):
        total = jnp.zeros((tall, SPAN), F32)
        for a, ref in enumerate((ga, gb)):
            for i in range(4):
                right = ref[h, i, :, :, t * SPAN : (t + 1) * SPAN].reshape(4 * HALF, SPAN)
                total = total + dot(wpt[a, i, 0:tall], right, NN)
        return total

    def trade(h, t):
        part = side(t)
        mix_out[h, :, part] = mix_acc[h, :, part].astype(BF)
        return remote(mix_out.at[h, :, part], mix_in.at[h, :, part], partner)

    def mix(h, t):
        arrived([g_two[h][t]])
        if t == 0:
            total = products(h, 0, 2 * PART)
            mix_acc[h, :, side(0)] = total[:PART]
            mix_acc[h, :, side(1)] = total[PART:]
        else:
            mix_acc[h, :, side(1)] += products(h, 1, PART)
        return trade(h, t)

    m_part = {}
    m_part[0, 0] = mix(0, 0)
    m_part[0, 1] = mix(0, 1)
    m_part[1, 0] = mix(1, 0)

    def back(h, t):
        arrived([m_part[h, t]])
        part = side(t)
        total = mix_acc[h, :, part] + mix_in[h, :, part].astype(F32)
        if t == 0:
            total = total + resid[:, span(h)]
        grad[h, :, part] = (total * (1 / 1024)).astype(BF)

        def step(a, carry):
            right = grad[h, :, part]
            for i in range(4):
                first = dot(ww[a, i].reshape(4 * HALF, PART), right, NN)
                if t == 0:
                    back_acc[h, a, i] = dot(pp[a, i].reshape(4 * HALF, PART), right, NN)
                else:
                    first = first + back_acc[h, a, i]
                sab[h, a, i, :, :, part] = first.astype(BF).reshape(4, HALF, SPAN)
            return carry

        lax.fori_loop(0, 2, step, 0)
        held = group(ra1.at[:, :, :, :, part])
        for d in (1, 2, 3):
            remote(
                sab.at[h, 0, (z + d) % 4, :, :, part], ra1.at[h, d - 1, :, :, part], zp(d), held
            )
            remote(
                sab.at[h, 1, (x + d) % 4, :, :, part], rb1.at[h, d - 1, :, :, part], xp(d), held
            )
        return held

    def total_of(own, others):
        total = own.astype(F32)
        for other in others:
            total = total + other.astype(F32)
        return total

    def scatter_two(h):
        arrived(r_one[h])
        sa2[h] = total_of(sab[h, 0, z], [ra1[h, k] for k in range(3)]).astype(BF)
        sb2[h] = total_of(sab[h, 1, x], [rb1[h, k] for k in range(3)]).astype(BF)
        held = group(ra2)
        for d in (1, 2, 3):
            remote(sa2.at[h, (x + d) % 4], ra2.at[h, d - 1], xp(d), held)
            remote(sb2.at[h, (z + d) % 4], rb2.at[h, d - 1], zp(d), held)
        return held

    def scattered(h):
        arrived([r_two[h]])
        first = total_of(sa2[h, x], [ra2[h, k] for k in range(3)])
        second = total_of(sb2[h, z], [rb2[h, k] for k in range(3)])
        return jnp.concatenate([first.astype(BF), second.astype(BF)], axis=0)

    def out_terms(h):
        for k in range(2):
            at = slice((2 * h + k) * SPAN, (2 * h + k + 1) * SPAN)
            turn[at] = grad[h, :, (1 - k) * SPAN : (2 - k) * SPAN].astype(F32).T.astype(BF)

        def term(i, carry):
            right = turn[2 * h * SPAN : 2 * (h + 1) * SPAN]
            for a, (ref, to) in enumerate(((ga, ha), (gb, hb))):
                total = dot(ref[h, i].reshape(4 * HALF, 2 * SPAN), right, NN)
                if h == 0:
                    out_acc[a, i] = total
                else:
                    to[i] = (out_acc[a, i] + total).astype(BF).reshape(4, HALF, PART)
            return carry

        lax.fori_loop(0, 4, term, 0)

    r_one = [[back(0, 0)], []]
    m_part[1, 1] = mix(1, 1)
    r_one[0].append(back(0, 1))
    out_terms(0)
    r_one[1].append(back(1, 0))
    r_one[1].append(back(1, 1))
    out_terms(1)

    o_core = group(ha)
    for k in range(2):
        remote(ha.at[:, 2 * k + 1 - c], ca.at[k], sib, o_core)
        remote(hb.at[2 * k + 1 - c], cb.at[k], sib, o_core)
    arrived([o_core])
    near, far = kept // 2, 1 - kept // 2
    xa[...] = total_of(ha[:, 2 * far + c], [ca[far]]).astype(BF)
    xb[...] = total_of(hb[2 * far + c], [cb[far]]).astype(BF)
    o_crs = group(ca)
    remote(xa, ya, crs, o_crs)
    remote(xb, yb, crs, o_crs)

    r_two = [scatter_two(0)]

    cv_acc[...] = jnp.zeros_like(cv_acc)
    ck_acc[...] = jnp.zeros_like(ck_acc)

    def soft_back(h):
        def rows_back(i, carry):
            at = pl.ds(pl.multiple_of(h * SPAN + i * 32, 32), 32)
            low, high = pl.ds(pl.multiple_of(i * 32, 32), 32), pl.ds(pl.multiple_of(SPAN + i * 32, 32), 32)
            weights, moved = prob[at, :], prob_tan[at, :]
            pulled, pulled_tan = score[h, low, :], score[h, high, :]
            base = jnp.sum(weights * pulled, axis=-1, keepdims=True)
            base_tan = jnp.sum(moved * pulled + weights * pulled_tan, axis=-1, keepdims=True)
            less = pulled - base
            slope[h, high, :] = (weights * less).astype(BF)
            slope[h, low, :] = (moved * less + weights * (pulled_tan - base_tan)).astype(BF)
            return carry

        lax.fori_loop(0, SPAN // 32, rows_back, 0, unroll=2)

    def value_terms(h, g):
        def step(b, carry):
            cv_acc[b] += dot(g, rnd[h, :, keys_of(b)], NN)
            return carry

        lax.fori_loop(0, 4, step, 0, unroll=2)

    def slopes(h, g):
        one, two = g[:, :SPAN], g[:, SPAN:]
        gg[h] = jnp.concatenate(
            [jnp.concatenate([one, two], axis=1), jnp.concatenate([jnp.zeros_like(one), one], axis=1)],
            axis=0,
        ).astype(F32).T.astype(BF)
        pulls(gg, v_part, h)
        soft_back(h)

    def key_terms(h):
        def step(b, carry):
            ck_acc[b] += dot(qk[h], slope[h, :, keys_of(b)], NN)
            return carry

        lax.fori_loop(0, 4, step, 0, unroll=2)

    def query_terms(h):
        terms = joint(pl.ds(0, 2 * HS), slope, h)
        cq_acc[:, span(h)] = terms[:HS, :SPAN] + terms[HS:, SPAN:]

    def chip_sums(own, other, kept):
        for k in range(2):
            kept[k] = total_of(own[2 * k + c], [other[k]]).astype(BF)

    r_two.append(scatter_two(1))
    g_first = scattered(0)
    value_terms(0, g_first)
    slopes(0, g_first)
    key_terms(0)
    query_terms(0)

    g_second = scattered(1)
    n_two.append(spread_normed(pl.ds(SHARE // 2, SHARE // 2)))
    value_terms(1, g_second)
    cv[...] = cv_acc[...].astype(BF)
    v_core = group(cvr)
    for k in range(2):
        remote(cv.at[2 * k + 1 - c], cvr.at[k], sib, v_core)
    slopes(1, g_second)
    arrived([v_core])
    chip_sums(cv, cvr, cvs)
    v_far = remote(cvs, cvf, crs)
    key_terms(1)
    ck[...] = (ck_acc[...] * root).astype(BF)

    k_core = group(ckr)
    for k in range(2):
        remote(ck.at[2 * k + 1 - c], ckr.at[k], sib, k_core)
    query_terms(1)
    q_part, k_rows, head_part = pl.ds(0, HS), pl.ds(HS, HS), pl.ds(0, 2 * HS)
    tail_part = pl.ds(2 * HS, HS)
    cot[s, q_part] = rotate((cq_acc[...] * root).astype(BF).astype(F32), own_trig, -1.0).astype(BF)
    arrived([k_core])
    chip_sums(ck, ckr, cks)
    k_far = remote(cks, ckf, crs)
    q_far = remote(cot.at[s, q_part], cot.at[s, q_part], crs)

    arrived([o_crs])
    fa[...] = total_of(ha[:, kept], [ca[near], ya[...]]).astype(BF)
    fb[...] = total_of(hb[kept], [cb[near], yb[...]]).astype(BF)
    o_fin = group(ca.at[0, pl.ds(0, 3)])
    o_fin_b = group(ca.at[0, pl.ds(0, 3)])
    for d in (1, 2, 3):
        other = (z + d) % 4
        remote(fa.at[other], oa.at[z], fin(d), o_fin)
        remote(fb.at[other], ob.at[z], fin(d), o_fin_b)
    lone = [Group(fa.at[z], send.at[count[0] + k], recv.at[count[0] + k]) for k in range(2)]
    count[0] += 2
    o_far = [
        remote(fa.at[z], oa.at[z], fin(0), lone[0], begin=False),
        remote(fb.at[z], ob.at[z], fin(0), lone[1], begin=False),
    ]
    o_near = [nearby(fa.at[z], oa.at[z]), nearby(fb.at[z], ob.at[z])]

    @pl.when(jnp.logical_not(alone))
    def _():
        for copy in o_far:
            copy.start()

    @pl.when(alone)
    def _():
        for copy in o_near:
            copy.start()

    arrived([v_far])
    for k in range(2):
        cot[2 * k + c, tail_part] = total_of(cvs[k], [cvf[k]]).astype(BF)
    t_tail = group(cvr)
    for k in range(2):
        remote(cot.at[2 * k + c, tail_part], cot.at[2 * k + c, tail_part], sib, t_tail)
    turns = [
        trig(jnp.broadcast_to(gkv[2 * k + c, KEYS - 16 : KEYS].astype(F32)[0:1], (ROT, TOK)))
        for k in range(2)
    ]
    arrived([n_sib] + n_two)

    def first_terms(part):
        def term(i, carry):
            at = lanes(i * TOK, TOK)
            acc_q[part, at] = dot(cot[s, part], nrm[:, lanes(s * SHARE + i * TOK, TOK)], NN) + dot(
                cot[s_crs, part], nb[s_crs, :, at], NN
            )
            return carry

        lax.fori_loop(0, SHARE // TOK, term, 0, unroll=2)

    def last_terms(part, start, stop):
        def term(i, carry):
            at = lanes(i * TOK, TOK)
            total = acc_q[part, at] + (
                dot(cot[s_sib, part], nb[s_sib, :, at], NN) + dot(cot[s_crd, part], nb[s_crd, :, at], NN)
            )
            oq[part, at] = (total * sgn[part, at]).astype(BF)
            return carry

        lax.fori_loop(start, stop, term, 0, unroll=3)

    first_terms(tail_part)
    arrived([t_tail])
    last_terms(tail_part, 0, 6)
    leaving = [stay(oq.at[tail_part], oq_out.at[tail_part])]

    arrived([k_far])
    for k in range(2):
        both = total_of(cks[k], [ckf[k]]).astype(BF).astype(F32)
        cot[2 * k + c, k_rows] = rotate(both, turns[k], -1.0).astype(BF)
    arrived([q_far])
    t_head = group(cot.at[pl.ds(0, 2), head_part])
    for k in range(2):
        remote(cot.at[2 * k + c, head_part], cot.at[2 * k + c, head_part], sib, t_head)
    first_terms(head_part)

    arrived([o_fin, o_fin_b])

    @pl.when(jnp.logical_not(alone))
    def _():
        for copy in o_far:
            copy.wait_recv()
            copy.wait_send()

    @pl.when(alone)
    def _():
        for copy in o_near:
            copy.wait()

    e_base = (
        lax.broadcasted_iota(jnp.int32, (HALF, PART), 0) * D
        + lax.broadcasted_iota(jnp.int32, (HALF, PART), 1)
        + (D * WIDE + fs * HS * D + s * SHARE)
    ) * jnp.int32(MIX[0]) + seeded
    scale = math.sqrt(INNER)
    for half, ref in enumerate((oa, ob)):
        for k in range(4):
            bit = sign_bit(e_base + jnp.int32(wrap((half * HALF * D + k * PART) * MIX[0])))
            oo[half * HALF : (half + 1) * HALF, k * PART : (k + 1) * PART] = (
                ref[k].astype(F32) * jnp.where(bit == 0, F32(scale), F32(-scale))
            ).astype(BF)


    leaving.append(stay(oo, oo_out))
    arrived([t_head])
    for k in range(2):
        last_terms(head_part, k * 3, k * 3 + 3)
        cols = pl.ds(k * SHARE // 2, SHARE // 2)
        leaving.append(stay(oq.at[head_part, cols], oq_out.at[head_part, cols]))
    for copy in leaving:
        copy.wait()

    for copy in sent:
        copy.wait_send()


def widen(product_in, out_in, product, out, narrow, narrow_out, wide, wide_out, loads, stores):
    thirds = [pl.ds(k * SHARE // 3, SHARE // 3) for k in range(3)]
    parts = [(product_in.at[:, at], narrow.at[k], wide.at[k], product.at[:, at]) for k, at in enumerate(thirds)]
    parts.append((out_in, narrow_out, wide_out, out))
    arrive = [pltpu.make_async_copy(part[0], part[1], loads.at[k]) for k, part in enumerate(parts)]
    leave = [pltpu.make_async_copy(part[2], part[3], stores.at[k]) for k, part in enumerate(parts)]
    for copy in arrive:
        copy.start()
    for k, part in enumerate(parts):
        arrive[k].wait()
        part[2][...] = part[1][...].astype(F32)
        leave[k].start()
    for copy in leave:
        copy.wait()


def tables():
    rate = 10000.0 ** (-2.0 * np.arange(ROT // 2) / ROT)
    rate = np.concatenate([rate, rate])[:, None]
    within = np.arange(TOK)[None, :] * rate
    blocks = np.arange(4)[:, None, None] * float(TOK) * rate[None] + np.zeros((1, 1, TOK))
    tab_t = np.stack([np.cos(within), np.sin(within)]).astype(np.float32)
    tab_b = np.stack([np.cos(blocks), np.sin(blocks)], axis=1).astype(np.float32)
    return tab_t, tab_b


def per_device(tokens, target, norm_gain, qkv_weight, out_weight, probe_seed, block_order):
    tab_t, tab_b = tables()
    anywhere = pl.BlockSpec(memory_space=pl.ANY)
    v = pltpu.VMEM
    scratch = [
        pltpu.SMEM((1,), jnp.int32), pltpu.SMEM((1,), jnp.int32),
        v((COLS, SHARE), BF), v((HS, SHARE), BF), v((1, D), F32), v((2, ROT, TOK), F32), v((4, 2, ROT, TOK), F32),
        v((TOK, D), BF), v((TOK, PART), BF), v((COLS, D), BF), v((TOK, D), BF), v((2, COLS, TOK), F32),
        v((2, TOK, 128), F32), v((4, TOK, SHARE), BF), v((4, 4 * HS + 16, TOK), BF),
        v((4, 4, HALF, PART), BF), v((2, 4, 4, HALF, PART), BF), v((2, 4, 4, HALF, PART), BF),
        v((2, 4, 2 * PART, 4 * HALF), BF),
        v((2, 4, 4, HALF, 2 * SPAN), BF), v((2, 4, 4, HALF, 2 * SPAN), BF),
        v((2, 2 * SPAN, 2 * HS), BF), v((2, HS, 2 * SPAN), BF), v((2, 2 * SPAN, 2 * HS), BF),
        v((2, 2 * SPAN, 1024), F32), v((TOK, 1024), F32), v((TOK, 1024), F32),
        v((2, 2 * SPAN, 1024), BF), v((2, 2 * SPAN, 1024), BF),
        v((4, HS, TOK), F32), v((4, HS, TOK), F32), v((HS, TOK), F32),
        v((2, PART, 2 * SPAN), F32), v((2, PART, 2 * SPAN), BF), v((2, PART, 2 * SPAN), BF),
        v((2, 2, 4, 4 * HALF, SPAN), F32), v((2, PART, 2 * SPAN), BF), v((4 * SPAN, PART), BF), v((PART, TOK), F32),
        v((2, 2, 4, 4, HALF, 2 * SPAN), BF),
        v((2, 3, 4, HALF, 2 * SPAN), BF), v((2, 3, 4, HALF, 2 * SPAN), BF),
        v((2, 4, HALF, 2 * SPAN), BF), v((2, 4, HALF, 2 * SPAN), BF),
        v((2, 3, HALF, 2 * SPAN), BF), v((2, 3, HALF, 2 * SPAN), BF),
        v((4, 4, HALF, PART), BF), v((4, 4, HALF, PART), BF),
        v((2, 4, HALF, PART), BF), v((2, 4, HALF, PART), BF),
        v((4, HALF, PART), BF), v((4, HALF, PART), BF), v((4, HALF, PART), BF), v((4, HALF, PART), BF),
        v((4, HALF, PART), BF), v((4, HALF, PART), BF), v((4, HALF, PART), BF), v((4, HALF, PART), BF),
        v((4, HS, TOK), BF), v((2, HS, TOK), BF), v((2, HS, TOK), BF), v((2, HS, TOK), BF),
        v((4, HS, TOK), BF), v((2, HS, TOK), BF), v((2, HS, TOK), BF), v((2, HS, TOK), BF),
        v((4, 3 * HS, TOK), BF), v((COLS, SHARE), F32), v((COLS, SHARE), F32), v((2, 4, 4 * HALF, PART), F32),
        pltpu.SemaphoreType.DMA((N_REMOTE,)), pltpu.SemaphoreType.DMA((N_REMOTE,)),
        pltpu.SemaphoreType.DMA((N_LOCAL,)),
    ]
    product, out_curv = pl.pallas_call(
        kernel,
        out_shape=(
            jax.ShapeDtypeStruct((COLS, SHARE), BF),
            jax.ShapeDtypeStruct((HS, SHARE), BF),
        ),
        in_specs=[anywhere] * 9,
        out_specs=(anywhere, anywhere),
        scratch_shapes=scratch,
        compiler_params=pltpu.CompilerParams(
            collective_id=0, has_side_effects=True, vmem_limit_bytes=60 * 2**20
        ),
    )(
        tokens, target, norm_gain.reshape(1, D), qkv_weight.T, out_weight, probe_seed, block_order,
        jnp.asarray(tab_t), jnp.asarray(tab_b),
    )
    product, out_curv = pl.pallas_call(
        widen,
        out_shape=(
            jax.ShapeDtypeStruct((COLS, SHARE), F32),
            jax.ShapeDtypeStruct((HS, SHARE), F32),
        ),
        in_specs=[anywhere, anywhere],
        out_specs=(anywhere, anywhere),
        scratch_shapes=[
            v((3, COLS, SHARE // 3), BF), v((HS, SHARE), BF),
            v((3, COLS, SHARE // 3), F32), v((HS, SHARE), F32),
            pltpu.SemaphoreType.DMA((4,)), pltpu.SemaphoreType.DMA((4,)),
        ],
    )(product, out_curv)
    return product.T, out_curv


def solution(mesh):
    placed = (P("seq", None), P("seq", None), P(), P(None, "fsdp"), P("fsdp", None), P(), P("seq"))
    return jax.shard_map(
        per_device,
        mesh=mesh,
        in_specs=placed,
        out_specs=(P("seq", "fsdp"), P("fsdp", "seq")),
        check_vma=False,
    )
```

```python
import functools
import math

import jax
import jax.numpy as jnp
import numpy as np
from jax import lax
from jax.experimental import pallas as pl
from jax.experimental.pallas import tpu as pltpu
from jax.sharding import PartitionSpec as P

MESH = pl.DeviceIdType.MESH
BF = jnp.bfloat16
F32 = jnp.float32
D = 6144
HS = 96
ROT = 24
TOK = 256
COLS = 288
WIDE = 9216
INNER = 3072
SHARE = 1536
PART = 384
HALF = 48
SPAN = 128
KEYS = 2 * HS + 16
STEP = 768
MIX = (-1640531535, -2048144789, -1028477387)
N_REMOTE = 52
N_LOCAL = 25


def wrap(value):
    return ((value + 2**31) % 2**32) - 2**31


def shifted(state, places):
    return lax.shift_right_logical(state, jnp.full(state.shape, places, jnp.int32))


def sign_bit(state):
    state = state ^ shifted(state, 16)
    state = state * jnp.int32(MIX[1])
    state = state ^ shifted(state, 13)
    state = state * jnp.int32(MIX[2])
    return (state ^ shifted(state, 16)) & jnp.int32(128)


def dot(a, b, contract):
    return lax.dot_general(a, b, (contract, ((), ())), preferred_element_type=F32)


NN = ((1,), (0,))
NT = ((1,), (1,))
TN = ((0,), (0,))


class Group:
    def __init__(self, size, send, recv):
        self.size, self.send, self.recv = size, send, recv

    def wait_recv(self):
        pltpu.make_async_copy(self.size, self.size, self.recv).wait()

    def wait_send(self):
        pltpu.make_async_copy(self.size, self.size, self.send).wait()


def kernel(
    tok_in, tgt_in, gain_in, wq_in, wo_in, seed_in, block_in, tab_t_in, tab_b_in,
    oq_out, oo_out,
    seed, block, oq, oo, gain, tab_t, tab_b, tok, tgt, wq, nrm, acc,
    stat, few, nb, gkv,
    wt, ww, pp, wpt, ga, gb,
    qq, qk, gg, score, prob, prob_tan, rnd, slope, cv_acc, ck_acc,
    mix_acc, mix_out, mix_in, back_acc, grad, resid,
    sab, ra1, rb1, sa2, sb2, ra2, rb2,
    ha, hb, ca, cb, xa, xb, ya, yb, fa, fb, oa, ob,
    cv, cvr, cvs, cvf, ck, ckr, cks, ckf, cot, sgn, acc_q, out_acc,
    send, recv, local,
):
    fs = lax.axis_index("fsdp")
    s = lax.axis_index("seq")
    x = fs // 8
    yl = (fs // 4) % 2
    z = fs % 4
    yh = s // 2
    c = s % 2
    s_sib = yh * 2 + (1 - c)
    s_crs = (1 - yh) * 2 + c
    s_crd = (1 - yh) * 2 + (1 - c)
    own_cols = (x * 4 + z) * PART

    def device(px, py, pz, ps):
        return ((px * 2 + py) * 4 + pz, ps)

    def xp(d):
        return device((x + d) % 4, yl, z, s)

    def zp(d):
        return device(x, yl, (z + d) % 4, s)

    kept = (s + 2 * (x % 2)) % 4
    alone = (x == s) & (x % 2 == 0)

    def fin(d):
        return device(kept, yl, (z + d) % 4, x)

    def fin_from(d):
        return device(s, yl, (z + d) % 4, (x + 2 * (s % 2)) % 4)

    partner = device(x, 1 - yl, z, s)
    sib = device(x, yl, z, s_sib)
    crs = device(x, yl, z, s_crs)
    crd = device(x, yl, z, s_crd)

    count = [0]
    sent = []

    def group(size):
        i = count[0]
        count[0] += 1
        sent.append(Group(size, send.at[i], recv.at[i]))
        return sent[-1]

    def remote(src, dst, to, within=None, begin=True):
        held = within or group(dst)
        copy = pltpu.make_async_remote_copy(
            src_ref=src, dst_ref=dst, send_sem=held.send, recv_sem=held.recv,
            device_id=to, device_id_type=MESH,
        )
        if begin:
            copy.start()
        return copy if not begin else held

    local_count = [0]

    def stay(src, dst):
        i = local_count[0]
        local_count[0] += 1
        copy = pltpu.make_async_copy(src, dst, local.at[i])
        copy.start()
        return copy

    def nearby(src, dst):
        i = local_count[0]
        local_count[0] += 1
        return pltpu.make_async_copy(src, dst, local.at[i])

    def arrived(copies):
        for copy in copies:
            copy.wait_recv()

    def lanes(start, size):
        return pl.ds(pl.multiple_of(start, 128), size)

    def rows(start, size):
        return pl.ds(pl.multiple_of(start, 16), size)

    tok_loads = [stay(tok_in.at[pl.ds(k * 64, 64)], tok.at[pl.ds(k * 64, 64)]) for k in range(4)]
    tab_loads = [stay(seed_in, seed), stay(block_in, block), stay(gain_in, gain), stay(tab_t_in, tab_t), stay(tab_b_in, tab_b)]
    tgt_load = stay(tgt_in.at[:, lanes(own_cols, PART)], tgt)
    first, second = jnp.where(c == 0, x, z), jnp.where(c == 0, z, x)

    def column(a, k):
        return jnp.where(c == 0, a * 4 + k, k * 4 + a) * PART

    own_w = [
        stay(wo_in.at[rows(c * HALF, HALF), lanes(column(first, k), PART)], wt.at[first, k])
        for k in range(4)
    ]

    barrier = pltpu.get_barrier_semaphore()

    def greet(to):
        pl.semaphore_signal(barrier, inc=1, device_id=to, device_id_type=MESH)

    for d in (1, 2, 3):
        greet(xp(d))
        greet(zp(d))
    for to in (partner, sib, crs, crd):
        greet(to)

    for d in (1, 2, 3):
        greet(fin_from(d))

    @pl.when(jnp.logical_not(alone))
    def _():
        greet(fin_from(0))


    def norm_sums(i, carry):
        at = rows(i * 16, 16)
        totals = [jnp.zeros((16, 128), F32) for _ in range(2)]
        for k in range(D // 128):
            totals[k % 2] += tok[at, k * 128 : (k + 1) * 128].astype(F32)
        stat[0, at, :] = totals[0] + totals[1]
        return carry

    for k in range(4):
        tok_loads[k].wait()
        lax.fori_loop(k * 4, (k + 1) * 4, norm_sums, 0, unroll=2)
    wq_load = stay(wq_in, wq)
    average = jnp.sum(stat[0], axis=-1, keepdims=True) * (1 / D)
    stat[0] = jnp.broadcast_to(average, (TOK, 128))

    def norm_squares(i, carry):
        at = rows(i * 16, 16)
        middle = stat[0, at, :]
        totals = [jnp.zeros((16, 128), F32) for _ in range(2)]
        for k in range(D // 128):
            centred = tok[at, k * 128 : (k + 1) * 128].astype(F32) - middle
            totals[k % 2] += centred * centred
        stat[1, at, :] = totals[0] + totals[1]
        return carry

    lax.fori_loop(0, TOK // 16, norm_squares, 0, unroll=2)
    spread = jnp.sum(stat[1], axis=-1, keepdims=True) * (1 / D)
    stat[1] = jnp.broadcast_to(lax.rsqrt(spread + 1e-05), (TOK, 128))

    pl.semaphore_wait(barrier, jnp.where(alone, 13, 14))

    def along_first(d):
        return device(
            jnp.where(c == 0, (x + d) % 4, x), yl, jnp.where(c == 0, z, (z + d) % 4), s
        )

    def along_second(d):
        return device(
            jnp.where(c == 0, x, (x + d) % 4), yl, jnp.where(c == 0, (z + d) % 4, z), s
        )

    w_one = group(wt.at[pl.ds(0, 3)])
    for d in (1, 2, 3):
        for k in range(4):
            remote(
                wo_in.at[rows(c * HALF, HALF), lanes(column((first + d) % 4, k), PART)],
                wt.at[first, k], along_first(d), w_one,
            )

    for copy in tab_loads:
        copy.wait()

    def norm_into(to, start, at):
        middle, factor = stat[0, at, :], stat[1, at, :]
        for k in range(D // 128):
            cols = slice(k * 128, (k + 1) * 128)
            to[start, cols] = ((tok[at, cols].astype(F32) - middle) * factor * gain[:, cols]).astype(BF)

    def norm_rows(i, carry):
        norm_into(nrm, rows(i * 16, 16), rows(i * 16, 16))
        return carry

    piece = jnp.where(c == 0, z * 4 + x, x * 4 + z) * 16
    norm_into(few, slice(0, 16), rows(piece, 16))
    n_far = group(nb.at[0, pl.ds(0, 32)])
    remote(
        few.at[:, lanes(s_crs * SHARE, SHARE)], nb.at[s, rows(piece, 16)], crs, n_far
    )
    remote(
        few.at[:, lanes(s_crd * SHARE, SHARE)], nb.at[s, rows(piece, 16)], crd, n_far
    )


    lax.fori_loop(0, TOK // 16, norm_rows, 0)

    n_sib = remote(nrm.at[:, lanes(s_sib * SHARE, SHARE)], nb.at[s], sib)

    wq_load.wait()
    acc[...] = jnp.zeros_like(acc)
    seeded = seed[0]
    q_probe = float(np.float32(1 / math.sqrt(D)).astype(jnp.bfloat16))
    o_probe = float(np.float32(1 / math.sqrt(INNER)).astype(jnp.bfloat16))

    def project(start, size, steps=(0, D // STEP)):
        q_rows = lax.broadcasted_iota(jnp.int32, (size, STEP), 1)
        q_cols = lax.broadcasted_iota(jnp.int32, (size, STEP), 0)
        q_base = (q_rows * WIDE + q_cols + (fs * COLS + start)) * jnp.int32(MIX[0]) + seeded
        to = pl.ds(start, size)

        def step(i, carry):
            at = pl.ds(pl.multiple_of(i * STEP, STEP), STEP)
            bit = sign_bit(q_base + i * jnp.int32(wrap(STEP * WIDE * MIX[0])))
            probe = jnp.where(bit == 0, F32(q_probe), F32(-q_probe)).astype(BF)
            both = dot(jnp.concatenate([wq[to, at], probe], axis=0), nrm[:, at], NT)
            acc[0, to] += both[:size]
            acc[1, to] += both[size:]
            return carry

        lax.fori_loop(*steps, step, 0)

    project(HS, 2 * HS)

    number = block[0]
    low = lax.broadcasted_iota(jnp.int32, (ROT, TOK), 0) < ROT // 2

    def trig(here):
        cos_b = jnp.zeros((ROT, TOK), F32)
        sin_b = jnp.zeros((ROT, TOK), F32)
        for k in range(4):
            cos_b = jnp.where(here == k, tab_b[k, 0], cos_b)
            sin_b = jnp.where(here == k, tab_b[k, 1], sin_b)
        cos = cos_b * tab_t[0] - sin_b * tab_t[1]
        sin = sin_b * tab_t[0] + cos_b * tab_t[1]
        return cos, jnp.where(low, -sin, sin)

    own_trig = trig(jnp.full((ROT, TOK), number, jnp.int32))

    def rotate(field, turns, sign=1.0, cols=slice(0, TOK)):
        cos, sin = turns[0][:, cols], turns[1][:, cols]
        head = field[:ROT]
        swapped = pltpu.roll(head, ROT // 2, 0)
        return jnp.concatenate([head * cos + swapped * (sin * sign), field[ROT:]], axis=0)

    for k in range(2):
        gkv[s, k * HS : (k + 1) * HS] = rotate(acc[k, HS : 2 * HS], own_trig).astype(BF)
    gkv[s, KEYS - 16 : KEYS] = jnp.full((16, TOK), number, jnp.int32).astype(F32).astype(BF)
    k_part, v_part = pl.ds(0, KEYS), pl.ds(KEYS, 2 * HS)

    def spread_kv(slot, part, to):
        return remote(gkv.at[slot, part], gkv.at[slot, part], to)

    k_crs = spread_kv(s, k_part, crs)
    k_sib = spread_kv(s, k_part, sib)
    for k in range(2):
        gkv[s, KEYS + k * HS : KEYS + (k + 1) * HS] = acc[k, 2 * HS : 3 * HS].astype(BF)
    v_crs = spread_kv(s, v_part, crs)
    v_sib = spread_kv(s, v_part, sib)

    b0 = (1 - yh) * 2
    b1 = b0 + 1
    arrived([n_far])
    n_one = group(nb.at[0, pl.ds(0, 96)])
    for d in (1, 2, 3):
        at0 = nb.at[b0, rows((z * 4 + x) * 16, 16)]
        at1 = nb.at[b1, rows((x * 4 + z) * 16, 16)]
        remote(at0, at0, xp(d), n_one)
        remote(at1, at1, zp(d), n_one)

    def span(h):
        return slice(h * SPAN, (h + 1) * SPAN)

    tgt_load.wait()
    project(0, HS, (0, 4))

    for copy in own_w:
        copy.wait()
    arrived([w_one])
    w_two = group(ww.at[0, pl.ds(0, 3)])
    for d in (1, 2, 3):
        remote(wt.at[:, (second + d) % 4], ww.at[c, second], along_second(d), w_two)
    own_ww = stay(wt.at[:, second], ww.at[c, second])

    project(0, HS, (4, D // STEP))

    q = rotate(acc[0, :HS], own_trig).astype(BF)
    q_tan = rotate(acc[1, :HS], own_trig).astype(BF)
    for h in range(2):
        one, two = q[:, span(h)], q_tan[:, span(h)]
        qq[h] = jnp.concatenate(
            [jnp.concatenate([one, two], axis=1), jnp.concatenate([jnp.zeros_like(one), one], axis=1)],
            axis=0,
        ).astype(F32).T.astype(BF)
        qk[h] = jnp.concatenate([one, two], axis=1)
    resid[...] = (tok[:, lanes(own_cols, PART)].astype(F32) - tgt[...].astype(F32)).T

    o_rows = lax.broadcasted_iota(jnp.int32, (HALF, PART), 0)
    o_lanes = lax.broadcasted_iota(jnp.int32, (HALF, PART), 1)
    o_base = (o_rows * D + o_lanes + (D * WIDE + own_cols)) * jnp.int32(MIX[0]) + seeded

    def probe_piece(i, carry):
        for k in range(4):
            first = ((k * 2 + yl) * 4 + i) * HS
            second = ((i * 2 + yl) * 4 + k) * HS + HALF
            bit = sign_bit(o_base + first * jnp.int32(wrap(D * MIX[0])))
            pp[0, i, k] = jnp.where(bit == 0, F32(o_probe), F32(-o_probe)).astype(BF)
            bit = sign_bit(o_base + second * jnp.int32(wrap(D * MIX[0])))
            pp[1, i, k] = jnp.where(bit == 0, F32(o_probe), F32(-o_probe)).astype(BF)
        return carry

    lax.fori_loop(0, 4, probe_piece, 0)

    def turned(source, start):
        def turn(i, carry):
            for a in range(2):
                value = source[a, pl.ds(2 * i, 2)].reshape(8 * HALF, PART).astype(F32)
                wpt[a, start : start + PART, lanes(i * 8 * HALF, 8 * HALF)] = value.T.astype(BF)
            return carry

        lax.fori_loop(0, 2, turn, 0)

    turned(pp, PART)

    def spread_normed(cols):
        held = group(nb.at[pl.ds(0, 2), pl.ds(0, 192), cols])
        for d in (1, 2, 3):
            at0 = nb.at[b0, rows(z * 64, 64), cols]
            at1 = nb.at[b1, rows(x * 64, 64), cols]
            remote(at0, at0, zp(d), held)
            remote(at1, at1, xp(d), held)
        return held

    arrived([k_crs])
    k_rel = spread_kv(s_crs, k_part, sib)

    root = 1 / math.sqrt(HS)

    def keys_of(b):
        return lanes(b * TOK, TOK)

    def pulls(left, part, h, blocks=range(4)):
        for b in blocks:
            score[h, :, keys_of(b)] = dot(left[h], gkv[b, part], NN)

    along = lax.broadcasted_iota(jnp.int32, (1, TOK), 1).astype(F32)
    number_f = jnp.full((32, 1), number, jnp.int32).astype(F32)
    down = lax.broadcasted_iota(jnp.int32, (32, 1), 0)

    def soft(h):
        def soft_rows(i, carry):
            at = pl.ds(pl.multiple_of(h * SPAN + i * 32, 32), 32)
            low, high = pl.ds(pl.multiple_of(i * 32, 32), 32), pl.ds(pl.multiple_of(SPAN + i * 32, 32), 32)
            query_pos = number_f * float(TOK) + (down + (h * SPAN + i * 32)).astype(F32)
            allowed = key_pos <= query_pos
            values = jnp.where(allowed, score[h, low, :] * root, -1e30)
            highest = jnp.max(values, axis=-1, keepdims=True)
            weights = jnp.exp(values - highest)
            weights = weights * (1.0 / jnp.sum(weights, axis=-1, keepdims=True))
            moved = weights * (score[h, high, :] * root)
            moved = moved - weights * jnp.sum(moved, axis=-1, keepdims=True)
            prob[at, :] = weights
            prob_tan[at, :] = moved
            rnd[h, high, :] = weights.astype(BF)
            rnd[h, low, :] = moved.astype(BF)
            return carry

        lax.fori_loop(0, SPAN // 32, soft_rows, 0, unroll=2)

    def joint(part, ref, h):
        def term(b, held):
            return held + dot(gkv[b, part], ref[h, :, keys_of(b)], NT)

        return lax.fori_loop(0, 4, term, jnp.zeros((2 * HS, 2 * SPAN), F32))

    def attn_products(h):
        terms = joint(v_part, rnd, h)
        both = jnp.concatenate([terms[:HS, SPAN:], terms[:HS, :SPAN] + terms[HS:, SPAN:]], axis=1)
        both = both.astype(BF)
        ga[h, z, x] = both[:HALF]
        gb[h, x, z] = both[HALF:]
        held = group(ra1.at[0, pl.ds(0, 3), pl.ds(0, 2)])
        for d in (1, 2, 3):
            remote(ga.at[h, z, x], ga.at[h, z, x], xp(d), held)
            remote(gb.at[h, x, z], gb.at[h, x, z], zp(d), held)
        return held

    def side(t):
        return pl.ds(t * SPAN, SPAN)

    def gather_two(h):
        groups = []
        for t in range(2):
            held = group(ra1.at[:, :, :, :, side(t)])
            for d in (1, 2, 3):
                at0, at1 = ga.at[h, z, :, :, side(t)], gb.at[h, x, :, :, side(t)]
                remote(at0, at0, zp(d), held)
                remote(at1, at1, xp(d), held)
            groups.append(held)
        return groups

    pulls(qq, pl.ds(0, 2 * HS), 0, (s, s_crs))
    pulls(qq, pl.ds(0, 2 * HS), 1, (s, s_crs))
    arrived([k_sib, k_rel])
    key_pos = jnp.concatenate(
        [gkv[b, KEYS - 16 : KEYS].astype(F32)[0:1] * float(TOK) + along for b in range(4)], axis=1
    )
    pulls(qq, pl.ds(0, 2 * HS), 0, (s_sib, s_crd))
    pulls(qq, pl.ds(0, 2 * HS), 1, (s_sib, s_crd))
    arrived([v_crs])
    v_rel = spread_kv(s_crs, v_part, sib)
    soft(0)
    arrived([v_sib, v_rel])
    g_one = [attn_products(0)]
    own_ww.wait()
    arrived([w_two])
    w_sib = remote(ww.at[c], ww.at[c], sib)
    soft(1)

    g_one.append(attn_products(1))

    arrived([g_one[0]])
    g_two = [gather_two(0)]
    arrived([w_sib])
    turned(ww, 0)
    arrived([g_one[1]])
    g_two.append(gather_two(1))
    arrived([n_one])
    n_two = [spread_normed(pl.ds(0, SHARE // 2))]

    s_base = (
        (lax.broadcasted_iota(jnp.int32, (COLS, TOK), 1) + s * SHARE) * WIDE
        + lax.broadcasted_iota(jnp.int32, (COLS, TOK), 0)
        + fs * COLS
    ) * jnp.int32(MIX[0]) + seeded

    def sign_cols(i, carry):
        bit = sign_bit(s_base + i * jnp.int32(wrap(TOK * WIDE * MIX[0])))
        sgn[:, lanes(i * TOK, TOK)] = jnp.where(bit == 0, F32(math.sqrt(D)), F32(-math.sqrt(D)))
        return carry

    lax.fori_loop(0, SHARE // TOK, sign_cols, 0)

    def products(h, t, tall):
        right = [
            ref[h, :, :, :, t * SPAN : (t + 1) * SPAN].reshape(16 * HALF, SPAN) for ref in (ga, gb)
        ]
        return dot(wpt[0, 0:tall], right[0], NN) + dot(wpt[1, 0:tall], right[1], NN)

    def trade(h, t):
        part = side(t)
        mix_out[h, :, part] = mix_acc[h, :, part].astype(BF)
        return remote(mix_out.at[h, :, part], mix_in.at[h, :, part], partner)

    def mix(h, t):
        arrived([g_two[h][t]])
        if t == 0:
            total = products(h, 0, 2 * PART)
            mix_acc[h, :, side(0)] = total[:PART]
            mix_acc[h, :, side(1)] = total[PART:]
        else:
            mix_acc[h, :, side(1)] += products(h, 1, PART)
        return trade(h, t)

    m_part = {}
    m_part[0, 0] = mix(0, 0)
    m_part[0, 1] = mix(0, 1)
    m_part[1, 0] = mix(1, 0)

    def back(h, t):
        arrived([m_part[h, t]])
        part = side(t)
        total = mix_acc[h, :, part] + mix_in[h, :, part].astype(F32)
        if t == 0:
            total = total + resid[:, span(h)]
        grad[h, :, part] = (total * (1 / 1024)).astype(BF)

        right = grad[h, :, part]
        for a in range(2):
            first = dot(ww[a].reshape(16 * HALF, PART), right, NN)
            if t == 1:
                first = first + back_acc[h, a]
            sab[h, a, :, :, :, part] = first.astype(BF).reshape(4, 4, HALF, SPAN)
        held = group(ra1.at[:, :, :, :, part])
        for d in (1, 2, 3):
            remote(
                sab.at[h, 0, (z + d) % 4, :, :, part], ra1.at[h, d - 1, :, :, part], zp(d), held
            )
            remote(
                sab.at[h, 1, (x + d) % 4, :, :, part], rb1.at[h, d - 1, :, :, part], xp(d), held
            )
        if t == 0:
            for a in range(2):
                back_acc[h, a] = dot(pp[a].reshape(16 * HALF, PART), right, NN)
        return held

    def total_of(own, others):
        total = own.astype(F32)
        for other in others:
            total = total + other.astype(F32)
        return total

    def scatter_two(h):
        arrived(r_one[h])
        sa2[h] = total_of(sab[h, 0, z], [ra1[h, k] for k in range(3)]).astype(BF)
        sb2[h] = total_of(sab[h, 1, x], [rb1[h, k] for k in range(3)]).astype(BF)
        held = group(ra2)
        for d in (1, 2, 3):
            remote(sa2.at[h, (x + d) % 4], ra2.at[h, d - 1], xp(d), held)
            remote(sb2.at[h, (z + d) % 4], rb2.at[h, d - 1], zp(d), held)
        return held

    def scattered(h):
        arrived([r_two[h]])
        first = total_of(sa2[h, x], [ra2[h, k] for k in range(3)])
        second = total_of(sb2[h, z], [rb2[h, k] for k in range(3)])
        return jnp.concatenate([first.astype(BF), second.astype(BF)], axis=0)

    def out_terms(h, t):
        right = grad[h, :, side(t)].astype(F32).T.astype(BF)
        for a, (ref, to) in enumerate(((ga, ha), (gb, hb))):
            left = ref[h, :, :, :, (1 - t) * SPAN : (2 - t) * SPAN].reshape(16 * HALF, SPAN)
            total = dot(left, right, NN)
            if (h, t) == (0, 0):
                out_acc[a] = total
            elif (h, t) == (1, 1):
                to[...] = (out_acc[a] + total).astype(BF).reshape(4, 4, HALF, PART)
                half, come = ((ha, ca), (hb, cb))[a]
                held = group(come)
                for k in range(2):
                    from_one = half.at[:, 2 * k + 1 - c] if a == 0 else half.at[2 * k + 1 - c]
                    remote(from_one, come.at[k], sib, held)
                o_core.append(held)
            else:
                out_acc[a] += total

    o_core = []
    r_one = [[back(0, 0)], []]
    m_part[1, 1] = mix(1, 1)
    r_one[0].append(back(0, 1))
    out_terms(0, 0)
    out_terms(0, 1)
    r_one[1].append(back(1, 0))
    out_terms(1, 0)
    r_one[1].append(back(1, 1))
    out_terms(1, 1)

    r_two = [scatter_two(0)]

    near, far = kept // 2, 1 - kept // 2
    arrived([o_core[0]])
    xa[...] = total_of(ha[:, 2 * far + c], [ca[far]]).astype(BF)
    o_crs = [remote(xa, ya, crs)]
    arrived([o_core[1]])
    xb[...] = total_of(hb[2 * far + c], [cb[far]]).astype(BF)
    o_crs.append(remote(xb, yb, crs))

    cv_acc[...] = jnp.zeros_like(cv_acc)
    ck_acc[...] = jnp.zeros_like(ck_acc)

    def soft_back(h):
        def rows_back(i, carry):
            at = pl.ds(pl.multiple_of(h * SPAN + i * 32, 32), 32)
            low, high = pl.ds(pl.multiple_of(i * 32, 32), 32), pl.ds(pl.multiple_of(SPAN + i * 32, 32), 32)
            weights, moved = prob[at, :], prob_tan[at, :]
            pulled, pulled_tan = score[h, low, :], score[h, high, :]
            base = jnp.sum(weights * pulled, axis=-1, keepdims=True)
            base_tan = jnp.sum(moved * pulled + weights * pulled_tan, axis=-1, keepdims=True)
            less = pulled - base
            slope[h, high, :] = (weights * less).astype(BF)
            slope[h, low, :] = (moved * less + weights * (pulled_tan - base_tan)).astype(BF)
            return carry

        lax.fori_loop(0, SPAN // 32, rows_back, 0, unroll=2)

    def value_terms(h, g):
        def step(b, carry):
            cv_acc[b] += dot(g, rnd[h, :, keys_of(b)], NN)
            return carry

        lax.fori_loop(0, 4, step, 0, unroll=2)

    def slopes(h, g):
        one, two = g[:, :SPAN], g[:, SPAN:]
        gg[h] = jnp.concatenate(
            [jnp.concatenate([one, two], axis=1), jnp.concatenate([jnp.zeros_like(one), one], axis=1)],
            axis=0,
        ).astype(F32).T.astype(BF)
        pulls(gg, v_part, h)
        soft_back(h)

    def key_terms(h):
        def step(b, carry):
            ck_acc[b] += dot(qk[h], slope[h, :, keys_of(b)], NN)
            return carry

        lax.fori_loop(0, 4, step, 0, unroll=2)

    def query_terms(h):
        terms = joint(pl.ds(0, 2 * HS), slope, h)
        total = (terms[:HS, :SPAN] + terms[HS:, SPAN:]) * root
        turned_back = rotate(total.astype(BF).astype(F32), own_trig, -1.0, span(h))
        cot[s, 0:HS, span(h)] = turned_back.astype(BF)

    def send_query(h, within):
        at = cot.at[s, pl.ds(0, HS), pl.ds(h * SPAN, SPAN)]
        return remote(at, at, crs, within)

    def chip_sums(own, other, kept):
        for k in range(2):
            kept[k] = total_of(own[2 * k + c], [other[k]]).astype(BF)

    r_two.append(scatter_two(1))
    g_first = scattered(0)
    value_terms(0, g_first)
    slopes(0, g_first)
    key_terms(0)
    query_terms(0)
    q_far = group(cot.at[0, pl.ds(0, HS)])
    send_query(0, q_far)

    def hand_out(k, source, to):
        held = group(ca.at[0, pl.ds(0, 3)])
        for d in (1, 2, 3):
            remote(source.at[(z + d) % 4], to.at[z], fin(d), held)
        lone = Group(source.at[z], send.at[count[0]], recv.at[count[0]])
        count[0] += 1
        there = remote(source.at[z], to.at[z], fin(0), lone, begin=False)
        here = nearby(source.at[z], to.at[z])

        @pl.when(jnp.logical_not(alone))
        def _():
            there.start()

        @pl.when(alone)
        def _():
            here.start()

        return held, there, here

    arrived([o_crs[0]])
    fa[...] = total_of(ha[:, kept], [ca[near], ya[...]]).astype(BF)
    o_fin = [hand_out(0, fa, oa)]

    g_second = scattered(1)
    n_two.append(spread_normed(pl.ds(SHARE // 2, SHARE // 2)))
    value_terms(1, g_second)
    cv[...] = cv_acc[...].astype(BF)
    v_core = group(cvr)
    for k in range(2):
        remote(cv.at[2 * k + 1 - c], cvr.at[k], sib, v_core)
    slopes(1, g_second)

    arrived([v_core])
    chip_sums(cv, cvr, cvs)
    v_far = remote(cvs, cvf, crs)
    key_terms(1)
    ck[...] = (ck_acc[...] * root).astype(BF)

    k_core = group(ckr)
    for k in range(2):
        remote(ck.at[2 * k + 1 - c], ckr.at[k], sib, k_core)
    query_terms(1)
    k_rows, head_part = pl.ds(HS, HS), pl.ds(0, 2 * HS)
    tail_part = pl.ds(2 * HS, HS)
    arrived([k_core])
    chip_sums(ck, ckr, cks)
    k_far = remote(cks, ckf, crs)
    send_query(1, q_far)

    arrived([o_crs[1]])
    fb[...] = total_of(hb[kept], [cb[near], yb[...]]).astype(BF)
    o_fin.append(hand_out(1, fb, ob))


    e_base = (
        lax.broadcasted_iota(jnp.int32, (HALF, PART), 0) * D
        + lax.broadcasted_iota(jnp.int32, (HALF, PART), 1)
        + (D * WIDE + fs * HS * D + s * SHARE)
    ) * jnp.int32(MIX[0]) + seeded
    scale = math.sqrt(INNER)
    leaving = []

    def result(half):
        held, there, here = o_fin[half]
        arrived([held])

        @pl.when(jnp.logical_not(alone))
        def _():
            there.wait_recv()
            there.wait_send()

        @pl.when(alone)
        def _():
            here.wait()

        at = pl.ds(half * HALF, HALF)
        for k in range(4):
            bit = sign_bit(e_base + jnp.int32(wrap((half * HALF * D + k * PART) * MIX[0])))
            signed = (oa, ob)[half][k].astype(F32) * jnp.where(bit == 0, F32(scale), F32(-scale))
            oo[at, k * PART : (k + 1) * PART] = signed.astype(BF)
        leaving.append(stay(oo.at[at], oo_out.at[at]))


    arrived([v_far])
    for k in range(2):
        cot[2 * k + c, tail_part] = total_of(cvs[k], [cvf[k]]).astype(BF)
    t_tail = group(cvr)
    for k in range(2):
        remote(cot.at[2 * k + c, tail_part], cot.at[2 * k + c, tail_part], sib, t_tail)
    turns = [
        trig(jnp.broadcast_to(gkv[2 * k + c, KEYS - 16 : KEYS].astype(F32)[0:1], (ROT, TOK)))
        for k in range(2)
    ]
    arrived([n_sib] + n_two)

    def first_terms(part):
        def term(i, carry):
            at = lanes(i * TOK, TOK)
            acc_q[part, at] = dot(cot[s, part], nrm[:, lanes(s * SHARE + i * TOK, TOK)], NN) + dot(
                cot[s_crs, part], nb[s_crs, :, at], NN
            )
            return carry

        lax.fori_loop(0, SHARE // TOK, term, 0, unroll=2)

    def last_terms(part, start, stop):
        def term(i, carry):
            at = lanes(i * TOK, TOK)
            total = acc_q[part, at] + (
                dot(cot[s_sib, part], nb[s_sib, :, at], NN) + dot(cot[s_crd, part], nb[s_crd, :, at], NN)
            )
            oq[part, at] = (total * sgn[part, at]).astype(BF)
            return carry

        lax.fori_loop(start, stop, term, 0, unroll=3)

    first_terms(tail_part)
    arrived([t_tail])
    last_terms(tail_part, 0, 6)
    leaving.append(stay(oq.at[tail_part], oq_out.at[tail_part]))

    arrived([k_far])
    for k in range(2):
        both = total_of(cks[k], [ckf[k]]).astype(BF).astype(F32)
        cot[2 * k + c, k_rows] = rotate(both, turns[k], -1.0).astype(BF)
    arrived([q_far])
    t_head = group(cot.at[pl.ds(0, 2), head_part])
    for k in range(2):
        remote(cot.at[2 * k + c, head_part], cot.at[2 * k + c, head_part], sib, t_head)
    first_terms(head_part)

    result(0)

    arrived([t_head])
    for k in range(2):
        last_terms(head_part, k * 3, k * 3 + 3)
        cols = pl.ds(k * SHARE // 2, SHARE // 2)
        leaving.append(stay(oq.at[head_part, cols], oq_out.at[head_part, cols]))
    result(1)
    for copy in leaving:
        copy.wait()

    for copy in sent:
        copy.wait_send()


def widen(product_in, out_in, product, out, narrow, narrow_out, wide, wide_out, loads, stores):
    pieces = [pl.ds(k * SHARE // 6, SHARE // 6) for k in range(6)]
    parts = [(product_in.at[:, at], narrow.at[k], wide.at[k], product.at[:, at]) for k, at in enumerate(pieces)]
    parts.append((out_in, narrow_out, wide_out, out))
    arrive = [pltpu.make_async_copy(part[0], part[1], loads.at[k]) for k, part in enumerate(parts)]
    leave = [pltpu.make_async_copy(part[2], part[3], stores.at[k]) for k, part in enumerate(parts)]
    for copy in arrive:
        copy.start()
    for k, part in enumerate(parts):
        arrive[k].wait()
        part[2][...] = part[1][...].astype(F32)
        leave[k].start()
    for copy in leave:
        copy.wait()


def tables():
    rate = 10000.0 ** (-2.0 * np.arange(ROT // 2) / ROT)
    rate = np.concatenate([rate, rate])[:, None]
    within = np.arange(TOK)[None, :] * rate
    blocks = np.arange(4)[:, None, None] * float(TOK) * rate[None] + np.zeros((1, 1, TOK))
    tab_t = np.stack([np.cos(within), np.sin(within)]).astype(np.float32)
    tab_b = np.stack([np.cos(blocks), np.sin(blocks)], axis=1).astype(np.float32)
    return tab_t, tab_b


def per_device(tokens, target, norm_gain, qkv_weight, out_weight, probe_seed, block_order):
    tab_t, tab_b = tables()
    anywhere = pl.BlockSpec(memory_space=pl.ANY)
    v = pltpu.VMEM
    scratch = [
        pltpu.SMEM((1,), jnp.int32), pltpu.SMEM((1,), jnp.int32),
        v((COLS, SHARE), BF), v((HS, SHARE), BF), v((1, D), F32), v((2, ROT, TOK), F32), v((4, 2, ROT, TOK), F32),
        v((TOK, D), BF), v((TOK, PART), BF), v((COLS, D), BF), v((TOK, D), BF), v((2, COLS, TOK), F32),
        v((2, TOK, 128), F32), v((16, D), BF), v((4, TOK, SHARE), BF), v((4, 4 * HS + 16, TOK), BF),
        v((4, 4, HALF, PART), BF), v((2, 4, 4, HALF, PART), BF), v((2, 4, 4, HALF, PART), BF),
        v((2, 2 * PART, 16 * HALF), BF),
        v((2, 4, 4, HALF, 2 * SPAN), BF), v((2, 4, 4, HALF, 2 * SPAN), BF),
        v((2, 2 * SPAN, 2 * HS), BF), v((2, HS, 2 * SPAN), BF), v((2, 2 * SPAN, 2 * HS), BF),
        v((2, 2 * SPAN, 1024), F32), v((TOK, 1024), F32), v((TOK, 1024), F32),
        v((2, 2 * SPAN, 1024), BF), v((2, 2 * SPAN, 1024), BF),
        v((4, HS, TOK), F32), v((4, HS, TOK), F32),
        v((2, PART, 2 * SPAN), F32), v((2, PART, 2 * SPAN), BF), v((2, PART, 2 * SPAN), BF),
        v((2, 2, 16 * HALF, SPAN), F32), v((2, PART, 2 * SPAN), BF), v((PART, TOK), F32),
        v((2, 2, 4, 4, HALF, 2 * SPAN), BF),
        v((2, 3, 4, HALF, 2 * SPAN), BF), v((2, 3, 4, HALF, 2 * SPAN), BF),
        v((2, 4, HALF, 2 * SPAN), BF), v((2, 4, HALF, 2 * SPAN), BF),
        v((2, 3, HALF, 2 * SPAN), BF), v((2, 3, HALF, 2 * SPAN), BF),
        v((4, 4, HALF, PART), BF), v((4, 4, HALF, PART), BF),
        v((2, 4, HALF, PART), BF), v((2, 4, HALF, PART), BF),
        v((4, HALF, PART), BF), v((4, HALF, PART), BF), v((4, HALF, PART), BF), v((4, HALF, PART), BF),
        v((4, HALF, PART), BF), v((4, HALF, PART), BF), v((4, HALF, PART), BF), v((4, HALF, PART), BF),
        v((4, HS, TOK), BF), v((2, HS, TOK), BF), v((2, HS, TOK), BF), v((2, HS, TOK), BF),
        v((4, HS, TOK), BF), v((2, HS, TOK), BF), v((2, HS, TOK), BF), v((2, HS, TOK), BF),
        v((4, 3 * HS, TOK), BF), v((COLS, SHARE), F32), v((COLS, SHARE), F32), v((2, 16 * HALF, PART), F32),
        pltpu.SemaphoreType.DMA((N_REMOTE,)), pltpu.SemaphoreType.DMA((N_REMOTE,)),
        pltpu.SemaphoreType.DMA((N_LOCAL,)),
    ]
    product, out_curv = pl.pallas_call(
        kernel,
        out_shape=(
            jax.ShapeDtypeStruct((COLS, SHARE), BF),
            jax.ShapeDtypeStruct((HS, SHARE), BF),
        ),
        in_specs=[anywhere] * 9,
        out_specs=(anywhere, anywhere),
        scratch_shapes=scratch,
        compiler_params=pltpu.CompilerParams(
            collective_id=0, has_side_effects=True, vmem_limit_bytes=60 * 2**20
        ),
    )(
        tokens, target, norm_gain.reshape(1, D), qkv_weight.T, out_weight, probe_seed, block_order,
        jnp.asarray(tab_t), jnp.asarray(tab_b),
    )
    product, out_curv = pl.pallas_call(
        widen,
        out_shape=(
            jax.ShapeDtypeStruct((COLS, SHARE), F32),
            jax.ShapeDtypeStruct((HS, SHARE), F32),
        ),
        in_specs=[anywhere, anywhere],
        out_specs=(anywhere, anywhere),
        scratch_shapes=[
            v((6, COLS, SHARE // 6), BF), v((HS, SHARE), BF),
            v((6, COLS, SHARE // 6), F32), v((HS, SHARE), F32),
            pltpu.SemaphoreType.DMA((7,)), pltpu.SemaphoreType.DMA((7,)),
        ],
    )(product, out_curv)
    return product.T, out_curv


def solution(mesh):
    placed = (P("seq", None), P("seq", None), P(), P(None, "fsdp"), P("fsdp", None), P(), P("seq"))
    return jax.shard_map(
        per_device,
        mesh=mesh,
        in_specs=placed,
        out_specs=(P("seq", "fsdp"), P("fsdp", "seq")),
        check_vma=False,
    )
```

```python
import functools
import math

import jax
import jax.numpy as jnp
import numpy as np
from jax import lax
from jax.experimental import pallas as pl
from jax.experimental.pallas import tpu as pltpu
from jax.sharding import PartitionSpec as P

MESH = pl.DeviceIdType.MESH
BF = jnp.bfloat16
F32 = jnp.float32
D = 6144
HS = 96
ROT = 24
TOK = 256
COLS = 288
WIDE = 9216
INNER = 3072
SHARE = 1536
PART = 384
HALF = 48
SPAN = 128
KEYS = 2 * HS + 16
STEP = 768
MIX = (-1640531535, -2048144789, -1028477387)
N_REMOTE = 52
N_LOCAL = 25


def wrap(value):
    return ((value + 2**31) % 2**32) - 2**31


def shifted(state, places):
    return lax.shift_right_logical(state, jnp.full(state.shape, places, jnp.int32))


def sign_bit(state):
    state = state ^ shifted(state, 16)
    state = state * jnp.int32(MIX[1])
    state = state ^ shifted(state, 13)
    state = state * jnp.int32(MIX[2])
    return (state ^ shifted(state, 16)) & jnp.int32(128)


def dot(a, b, contract):
    return lax.dot_general(a, b, (contract, ((), ())), preferred_element_type=F32)


NN = ((1,), (0,))
NT = ((1,), (1,))
TN = ((0,), (0,))


class Group:
    def __init__(self, size, send, recv):
        self.size, self.send, self.recv = size, send, recv

    def wait_recv(self):
        pltpu.make_async_copy(self.size, self.size, self.recv).wait()

    def wait_send(self):
        pltpu.make_async_copy(self.size, self.size, self.send).wait()


def kernel(
    tok_in, tgt_in, gain_in, wq_in, wo_in, seed_in, block_in, tab_t_in, tab_b_in,
    oq_out, oo_out,
    seed, block, oq, oo, gain, tab_t, tab_b, tok, tgt, wq, nrm, acc,
    stat, few, nb, gkv,
    wt, ww, pp, wpt, ga, gb,
    qq, qk, gg, score, prob, prob_tan, rnd, slope, cv_acc, ck_acc,
    mix_acc, mix_out, mix_in, back_acc, grad, resid,
    sab, ra1, rb1, sa2, sb2, ra2, rb2,
    ha, hb, ca, cb, xa, xb, ya, yb, fa, fb, oa, ob,
    cv, cvr, cvs, cvf, ck, ckr, cks, ckf, cot, sgn, acc_q, out_acc,
    send, recv, local,
):
    fs = lax.axis_index("fsdp")
    s = lax.axis_index("seq")
    x = fs // 8
    yl = (fs // 4) % 2
    z = fs % 4
    yh = s // 2
    c = s % 2
    s_sib = yh * 2 + (1 - c)
    s_crs = (1 - yh) * 2 + c
    s_crd = (1 - yh) * 2 + (1 - c)
    own_cols = (x * 4 + z) * PART

    def device(px, py, pz, ps):
        return ((px * 2 + py) * 4 + pz, ps)

    def xp(d):
        return device((x + d) % 4, yl, z, s)

    def zp(d):
        return device(x, yl, (z + d) % 4, s)

    kept = (s + 2 * (x % 2)) % 4
    alone = (x == s) & (x % 2 == 0)

    def fin(d):
        return device(kept, yl, (z + d) % 4, x)

    def fin_from(d):
        return device(s, yl, (z + d) % 4, (x + 2 * (s % 2)) % 4)

    partner = device(x, 1 - yl, z, s)
    sib = device(x, yl, z, s_sib)
    crs = device(x, yl, z, s_crs)
    crd = device(x, yl, z, s_crd)

    count = [0]
    sent = []

    def group(size):
        i = count[0]
        count[0] += 1
        sent.append(Group(size, send.at[i], recv.at[i]))
        return sent[-1]

    def remote(src, dst, to, within=None, begin=True):
        held = within or group(dst)
        copy = pltpu.make_async_remote_copy(
            src_ref=src, dst_ref=dst, send_sem=held.send, recv_sem=held.recv,
            device_id=to, device_id_type=MESH,
        )
        if begin:
            copy.start()
        return copy if not begin else held

    local_count = [0]

    def stay(src, dst):
        i = local_count[0]
        local_count[0] += 1
        copy = pltpu.make_async_copy(src, dst, local.at[i])
        copy.start()
        return copy

    def nearby(src, dst):
        i = local_count[0]
        local_count[0] += 1
        return pltpu.make_async_copy(src, dst, local.at[i])

    def arrived(copies):
        for copy in copies:
            copy.wait_recv()

    def lanes(start, size):
        return pl.ds(pl.multiple_of(start, 128), size)

    def rows(start, size):
        return pl.ds(pl.multiple_of(start, 16), size)

    tok_loads = [stay(tok_in.at[pl.ds(k * 64, 64)], tok.at[pl.ds(k * 64, 64)]) for k in range(4)]
    tab_loads = [stay(seed_in, seed), stay(block_in, block), stay(gain_in, gain), stay(tab_t_in, tab_t), stay(tab_b_in, tab_b)]
    tgt_load = stay(tgt_in.at[:, lanes(own_cols, PART)], tgt)
    first, second = jnp.where(c == 0, x, z), jnp.where(c == 0, z, x)

    def column(a, k):
        return jnp.where(c == 0, a * 4 + k, k * 4 + a) * PART

    own_w = [
        stay(wo_in.at[rows(c * HALF, HALF), lanes(column(first, k), PART)], wt.at[first, k])
        for k in range(4)
    ]

    barrier = pltpu.get_barrier_semaphore()

    def greet(to):
        pl.semaphore_signal(barrier, inc=1, device_id=to, device_id_type=MESH)

    for d in (1, 2, 3):
        greet(xp(d))
        greet(zp(d))
    for to in (partner, sib, crs, crd):
        greet(to)

    for d in (1, 2, 3):
        greet(fin_from(d))

    @pl.when(jnp.logical_not(alone))
    def _():
        greet(fin_from(0))


    def norm_sums(i, carry):
        at = rows(i * 16, 16)
        middle = stat[0, at, :]
        totals = [jnp.zeros((16, 128), F32) for _ in range(4)]
        for k in range(D // 128):
            moved = tok[at, k * 128 : (k + 1) * 128].astype(F32) - middle
            totals[k % 2] += moved
            totals[2 + k % 2] += moved * moved
        stat[1, at, :] = totals[0] + totals[1]
        stat[2, at, :] = totals[2] + totals[3]
        return carry

    for k in range(4):
        tok_loads[k].wait()
        at = pl.ds(k * 64, 64)
        pivot = jnp.mean(tok[at, 0:128].astype(F32), axis=-1, keepdims=True)
        stat[0, at] = jnp.broadcast_to(pivot, (64, 128))
        lax.fori_loop(k * 4, (k + 1) * 4, norm_sums, 0, unroll=2)
    wq_load = stay(wq_in, wq)
    drift = jnp.sum(stat[1], axis=-1, keepdims=True) * (1 / D)
    spread = jnp.sum(stat[2], axis=-1, keepdims=True) * (1 / D) - drift * drift
    stat[0] += jnp.broadcast_to(drift, (TOK, 128))
    stat[1] = jnp.broadcast_to(lax.rsqrt(jnp.maximum(spread, 0.0) + 1e-05), (TOK, 128))

    pl.semaphore_wait(barrier, jnp.where(alone, 13, 14))

    def along_first(d):
        return device(
            jnp.where(c == 0, (x + d) % 4, x), yl, jnp.where(c == 0, z, (z + d) % 4), s
        )

    def along_second(d):
        return device(
            jnp.where(c == 0, x, (x + d) % 4), yl, jnp.where(c == 0, (z + d) % 4, z), s
        )

    w_one = group(wt.at[pl.ds(0, 3)])
    for d in (1, 2, 3):
        for k in range(4):
            remote(
                wo_in.at[rows(c * HALF, HALF), lanes(column((first + d) % 4, k), PART)],
                wt.at[first, k], along_first(d), w_one,
            )

    for copy in tab_loads:
        copy.wait()

    def norm_into(to, start, at):
        middle, factor = stat[0, at, :], stat[1, at, :]
        for k in range(D // 128):
            cols = slice(k * 128, (k + 1) * 128)
            to[start, cols] = ((tok[at, cols].astype(F32) - middle) * factor * gain[:, cols]).astype(BF)

    def norm_rows(i, carry):
        norm_into(nrm, rows(i * 16, 16), rows(i * 16, 16))
        return carry

    piece = jnp.where(c == 0, z * 4 + x, x * 4 + z) * 16
    norm_into(few, slice(0, 16), rows(piece, 16))
    n_far = group(nb.at[0, pl.ds(0, 32)])
    remote(
        few.at[:, lanes(s_crs * SHARE, SHARE)], nb.at[s, rows(piece, 16)], crs, n_far
    )
    remote(
        few.at[:, lanes(s_crd * SHARE, SHARE)], nb.at[s, rows(piece, 16)], crd, n_far
    )


    lax.fori_loop(0, TOK // 16, norm_rows, 0)

    n_sib = remote(nrm.at[:, lanes(s_sib * SHARE, SHARE)], nb.at[s], sib)

    wq_load.wait()
    acc[...] = jnp.zeros_like(acc)
    seeded = seed[0]
    q_probe = float(np.float32(1 / math.sqrt(D)).astype(jnp.bfloat16))
    o_probe = float(np.float32(1 / math.sqrt(INNER)).astype(jnp.bfloat16))

    def project(start, size, steps=(0, D // STEP)):
        q_rows = lax.broadcasted_iota(jnp.int32, (size, STEP), 1)
        q_cols = lax.broadcasted_iota(jnp.int32, (size, STEP), 0)
        q_base = (q_rows * WIDE + q_cols + (fs * COLS + start)) * jnp.int32(MIX[0]) + seeded
        to = pl.ds(start, size)

        def step(i, carry):
            at = pl.ds(pl.multiple_of(i * STEP, STEP), STEP)
            bit = sign_bit(q_base + i * jnp.int32(wrap(STEP * WIDE * MIX[0])))
            probe = jnp.where(bit == 0, F32(q_probe), F32(-q_probe)).astype(BF)
            both = dot(jnp.concatenate([wq[to, at], probe], axis=0), nrm[:, at], NT)
            acc[0, to] += both[:size]
            acc[1, to] += both[size:]
            return carry

        lax.fori_loop(*steps, step, 0)

    project(HS, 2 * HS)

    number = block[0]
    low = lax.broadcasted_iota(jnp.int32, (ROT, TOK), 0) < ROT // 2

    def trig(here):
        cos_b = jnp.zeros((ROT, TOK), F32)
        sin_b = jnp.zeros((ROT, TOK), F32)
        for k in range(4):
            cos_b = jnp.where(here == k, tab_b[k, 0], cos_b)
            sin_b = jnp.where(here == k, tab_b[k, 1], sin_b)
        cos = cos_b * tab_t[0] - sin_b * tab_t[1]
        sin = sin_b * tab_t[0] + cos_b * tab_t[1]
        return cos, jnp.where(low, -sin, sin)

    own_trig = trig(jnp.full((ROT, TOK), number, jnp.int32))

    def rotate(field, turns, sign=1.0, cols=slice(0, TOK)):
        cos, sin = turns[0][:, cols], turns[1][:, cols]
        head = field[:ROT]
        swapped = pltpu.roll(head, ROT // 2, 0)
        return jnp.concatenate([head * cos + swapped * (sin * sign), field[ROT:]], axis=0)

    for k in range(2):
        gkv[s, k * HS : (k + 1) * HS] = rotate(acc[k, HS : 2 * HS], own_trig).astype(BF)
    gkv[s, KEYS - 16 : KEYS] = jnp.full((16, TOK), number, jnp.int32).astype(F32).astype(BF)
    k_part, v_part = pl.ds(0, KEYS), pl.ds(KEYS, 2 * HS)

    def spread_kv(slot, part, to):
        return remote(gkv.at[slot, part], gkv.at[slot, part], to)

    k_crs = spread_kv(s, k_part, crs)
    k_sib = spread_kv(s, k_part, sib)
    for k in range(2):
        gkv[s, KEYS + k * HS : KEYS + (k + 1) * HS] = acc[k, 2 * HS : 3 * HS].astype(BF)
    v_crs = spread_kv(s, v_part, crs)
    v_sib = spread_kv(s, v_part, sib)

    b0 = (1 - yh) * 2
    b1 = b0 + 1
    arrived([n_far])
    n_one = group(nb.at[0, pl.ds(0, 96)])
    for d in (1, 2, 3):
        at0 = nb.at[b0, rows((z * 4 + x) * 16, 16)]
        at1 = nb.at[b1, rows((x * 4 + z) * 16, 16)]
        remote(at0, at0, xp(d), n_one)
        remote(at1, at1, zp(d), n_one)

    def span(h):
        return slice(h * SPAN, (h + 1) * SPAN)

    tgt_load.wait()
    project(0, HS, (0, 4))

    for copy in own_w:
        copy.wait()
    arrived([w_one])
    w_two = group(ww.at[0, pl.ds(0, 3)])
    for d in (1, 2, 3):
        remote(wt.at[:, (second + d) % 4], ww.at[c, second], along_second(d), w_two)
    own_ww = stay(wt.at[:, second], ww.at[c, second])

    project(0, HS, (4, D // STEP))

    q = rotate(acc[0, :HS], own_trig).astype(BF)
    q_tan = rotate(acc[1, :HS], own_trig).astype(BF)
    for h in range(2):
        one, two = q[:, span(h)], q_tan[:, span(h)]
        qq[h] = jnp.concatenate(
            [jnp.concatenate([one, two], axis=1), jnp.concatenate([jnp.zeros_like(one), one], axis=1)],
            axis=0,
        ).astype(F32).T.astype(BF)
        qk[h] = jnp.concatenate([one, two], axis=1)
    resid[...] = (tok[:, lanes(own_cols, PART)].astype(F32) - tgt[...].astype(F32)).T

    o_rows = lax.broadcasted_iota(jnp.int32, (HALF, PART), 0)
    o_lanes = lax.broadcasted_iota(jnp.int32, (HALF, PART), 1)
    o_base = (o_rows * D + o_lanes + (D * WIDE + own_cols)) * jnp.int32(MIX[0]) + seeded

    def probe_piece(i, carry):
        for k in range(4):
            first = ((k * 2 + yl) * 4 + i) * HS
            second = ((i * 2 + yl) * 4 + k) * HS + HALF
            bit = sign_bit(o_base + first * jnp.int32(wrap(D * MIX[0])))
            pp[0, i, k] = jnp.where(bit == 0, F32(o_probe), F32(-o_probe)).astype(BF)
            bit = sign_bit(o_base + second * jnp.int32(wrap(D * MIX[0])))
            pp[1, i, k] = jnp.where(bit == 0, F32(o_probe), F32(-o_probe)).astype(BF)
        return carry

    lax.fori_loop(0, 4, probe_piece, 0)

    def turned(source, start):
        def turn(i, carry):
            for a in range(2):
                value = source[a, pl.ds(2 * i, 2)].reshape(8 * HALF, PART).astype(F32)
                wpt[a, start : start + PART, lanes(i * 8 * HALF, 8 * HALF)] = value.T.astype(BF)
            return carry

        lax.fori_loop(0, 2, turn, 0)

    turned(pp, PART)

    def spread_normed(cols):
        held = group(nb.at[pl.ds(0, 2), pl.ds(0, 192), cols])
        for d in (1, 2, 3):
            at0 = nb.at[b0, rows(z * 64, 64), cols]
            at1 = nb.at[b1, rows(x * 64, 64), cols]
            remote(at0, at0, zp(d), held)
            remote(at1, at1, xp(d), held)
        return held

    arrived([k_crs])
    k_rel = spread_kv(s_crs, k_part, sib)

    root = 1 / math.sqrt(HS)

    def keys_of(b):
        return lanes(b * TOK, TOK)

    def pulls(left, part, h, blocks=range(4)):
        for b in blocks:
            score[h, :, keys_of(b)] = dot(left[h], gkv[b, part], NN)

    along = lax.broadcasted_iota(jnp.int32, (1, TOK), 1).astype(F32)
    number_f = jnp.full((32, 1), number, jnp.int32).astype(F32)
    down = lax.broadcasted_iota(jnp.int32, (32, 1), 0)

    def soft(h):
        def soft_rows(i, carry):
            at = pl.ds(pl.multiple_of(h * SPAN + i * 32, 32), 32)
            low, high = pl.ds(pl.multiple_of(i * 32, 32), 32), pl.ds(pl.multiple_of(SPAN + i * 32, 32), 32)
            query_pos = number_f * float(TOK) + (down + (h * SPAN + i * 32)).astype(F32)
            allowed = key_pos <= query_pos
            values = jnp.where(allowed, score[h, low, :] * root, -1e30)
            highest = jnp.max(values, axis=-1, keepdims=True)
            weights = jnp.exp(values - highest)
            weights = weights * (1.0 / jnp.sum(weights, axis=-1, keepdims=True))
            moved = weights * (score[h, high, :] * root)
            moved = moved - weights * jnp.sum(moved, axis=-1, keepdims=True)
            prob[at, :] = weights
            prob_tan[at, :] = moved
            rnd[h, high, :] = weights.astype(BF)
            rnd[h, low, :] = moved.astype(BF)
            return carry

        lax.fori_loop(0, SPAN // 32, soft_rows, 0, unroll=2)

    def joint(part, ref, h):
        def term(b, held):
            return held + dot(gkv[b, part], ref[h, :, keys_of(b)], NT)

        return lax.fori_loop(0, 4, term, jnp.zeros((2 * HS, 2 * SPAN), F32))

    def attn_products(h):
        terms = joint(v_part, rnd, h)
        both = jnp.concatenate([terms[:HS, SPAN:], terms[:HS, :SPAN] + terms[HS:, SPAN:]], axis=1)
        both = both.astype(BF)
        ga[h, z, x] = both[:HALF]
        gb[h, x, z] = both[HALF:]
        held = group(ra1.at[0, pl.ds(0, 3), pl.ds(0, 2)])
        for d in (1, 2, 3):
            remote(ga.at[h, z, x], ga.at[h, z, x], xp(d), held)
            remote(gb.at[h, x, z], gb.at[h, x, z], zp(d), held)
        return held

    def side(t):
        return pl.ds(t * SPAN, SPAN)

    def gather_two(h):
        groups = []
        for t in range(2):
            held = group(ra1.at[:, :, :, :, side(t)])
            for d in (1, 2, 3):
                at0, at1 = ga.at[h, z, :, :, side(t)], gb.at[h, x, :, :, side(t)]
                remote(at0, at0, zp(d), held)
                remote(at1, at1, xp(d), held)
            groups.append(held)
        return groups

    pulls(qq, pl.ds(0, 2 * HS), 0, (s, s_crs))
    pulls(qq, pl.ds(0, 2 * HS), 1, (s, s_crs))
    arrived([k_sib, k_rel])
    key_pos = jnp.concatenate(
        [gkv[b, KEYS - 16 : KEYS].astype(F32)[0:1] * float(TOK) + along for b in range(4)], axis=1
    )
    pulls(qq, pl.ds(0, 2 * HS), 0, (s_sib, s_crd))
    pulls(qq, pl.ds(0, 2 * HS), 1, (s_sib, s_crd))
    arrived([n_one])
    n_two = [spread_normed(pl.ds(0, SHARE // 4))]
    arrived([v_crs])
    v_rel = spread_kv(s_crs, v_part, sib)
    soft(0)
    arrived([v_sib, v_rel])
    g_one = [attn_products(0)]
    own_ww.wait()
    arrived([w_two])
    w_sib = remote(ww.at[c], ww.at[c], sib)
    soft(1)

    g_one.append(attn_products(1))

    arrived([g_one[0]])
    g_two = [gather_two(0)]
    arrived([w_sib])
    turned(ww, 0)
    arrived([g_one[1]])
    g_two.append(gather_two(1))
    n_two.append(spread_normed(pl.ds(SHARE // 4, SHARE // 4)))

    s_base = (
        (lax.broadcasted_iota(jnp.int32, (COLS, TOK), 1) + s * SHARE) * WIDE
        + lax.broadcasted_iota(jnp.int32, (COLS, TOK), 0)
        + fs * COLS
    ) * jnp.int32(MIX[0]) + seeded

    def sign_cols(i, carry):
        bit = sign_bit(s_base + i * jnp.int32(wrap(TOK * WIDE * MIX[0])))
        sgn[:, lanes(i * TOK, TOK)] = jnp.where(bit == 0, F32(math.sqrt(D)), F32(-math.sqrt(D)))
        return carry

    lax.fori_loop(0, SHARE // TOK, sign_cols, 0)

    def products(h, t, tall):
        right = [
            ref[h, :, :, :, t * SPAN : (t + 1) * SPAN].reshape(16 * HALF, SPAN) for ref in (ga, gb)
        ]
        return dot(wpt[0, 0:tall], right[0], NN) + dot(wpt[1, 0:tall], right[1], NN)

    def trade(h, t):
        part = side(t)
        mix_out[h, :, part] = mix_acc[h, :, part].astype(BF)
        return remote(mix_out.at[h, :, part], mix_in.at[h, :, part], partner)

    def mix(h, t):
        arrived([g_two[h][t]])
        if t == 0:
            total = products(h, 0, 2 * PART)
            mix_acc[h, :, side(0)] = total[:PART]
            mix_acc[h, :, side(1)] = total[PART:]
        else:
            mix_acc[h, :, side(1)] += products(h, 1, PART)
        return trade(h, t)

    m_part = {}
    m_part[0, 0] = mix(0, 0)
    m_part[0, 1] = mix(0, 1)
    m_part[1, 0] = mix(1, 0)

    def back(h, t):
        arrived([m_part[h, t]])
        part = side(t)
        total = mix_acc[h, :, part] + mix_in[h, :, part].astype(F32)
        if t == 0:
            total = total + resid[:, span(h)]
        grad[h, :, part] = (total * (1 / 1024)).astype(BF)

        right = grad[h, :, part]
        for a in range(2):
            first = dot(ww[a].reshape(16 * HALF, PART), right, NN)
            if t == 1:
                first = first + back_acc[h, a]
            sab[h, a, :, :, :, part] = first.astype(BF).reshape(4, 4, HALF, SPAN)
        held = group(ra1.at[:, :, :, :, part])
        for d in (1, 2, 3):
            remote(
                sab.at[h, 0, (z + d) % 4, :, :, part], ra1.at[h, d - 1, :, :, part], zp(d), held
            )
            remote(
                sab.at[h, 1, (x + d) % 4, :, :, part], rb1.at[h, d - 1, :, :, part], xp(d), held
            )
        if t == 0:
            for a in range(2):
                back_acc[h, a] = dot(pp[a].reshape(16 * HALF, PART), right, NN)
        return held

    def total_of(own, others):
        total = own.astype(F32)
        for other in others:
            total = total + other.astype(F32)
        return total

    def scatter_two(h):
        arrived(r_one[h])
        sa2[h] = total_of(sab[h, 0, z], [ra1[h, k] for k in range(3)]).astype(BF)
        sb2[h] = total_of(sab[h, 1, x], [rb1[h, k] for k in range(3)]).astype(BF)
        held = group(ra2)
        for d in (1, 2, 3):
            remote(sa2.at[h, (x + d) % 4], ra2.at[h, d - 1], xp(d), held)
            remote(sb2.at[h, (z + d) % 4], rb2.at[h, d - 1], zp(d), held)
        return held

    def scattered(h):
        arrived([r_two[h]])
        first = total_of(sa2[h, x], [ra2[h, k] for k in range(3)])
        second = total_of(sb2[h, z], [rb2[h, k] for k in range(3)])
        return jnp.concatenate([first.astype(BF), second.astype(BF)], axis=0)

    def out_terms(h, t):
        right = grad[h, :, side(t)].astype(F32).T.astype(BF)
        for a, (ref, to) in enumerate(((ga, ha), (gb, hb))):
            left = ref[h, :, :, :, (1 - t) * SPAN : (2 - t) * SPAN].reshape(16 * HALF, SPAN)
            total = dot(left, right, NN)
            if (h, t) == (0, 0):
                out_acc[a] = total
            elif (h, t) == (1, 1):
                to[...] = (out_acc[a] + total).astype(BF).reshape(4, 4, HALF, PART)
                half, come = ((ha, ca), (hb, cb))[a]
                held = group(come)
                for k in range(2):
                    from_one = half.at[:, 2 * k + 1 - c] if a == 0 else half.at[2 * k + 1 - c]
                    remote(from_one, come.at[k], sib, held)
                o_core.append(held)
            else:
                out_acc[a] += total

    o_core = []
    r_one = [[back(0, 0)], []]
    m_part[1, 1] = mix(1, 1)
    r_one[0].append(back(0, 1))
    out_terms(0, 0)
    out_terms(0, 1)
    r_one[1].append(back(1, 0))
    out_terms(1, 0)
    r_one[1].append(back(1, 1))
    out_terms(1, 1)


    near, far = kept // 2, 1 - kept // 2
    arrived([o_core[0]])
    xa[...] = total_of(ha[:, 2 * far + c], [ca[far]]).astype(BF)
    o_crs = [remote(xa, ya, crs)]
    r_two = [scatter_two(0)]
    arrived([o_core[1]])
    xb[...] = total_of(hb[2 * far + c], [cb[far]]).astype(BF)
    o_crs.append(remote(xb, yb, crs))

    cv_acc[...] = jnp.zeros_like(cv_acc)
    ck_acc[...] = jnp.zeros_like(ck_acc)

    def soft_back(h):
        def rows_back(i, carry):
            at = pl.ds(pl.multiple_of(h * SPAN + i * 32, 32), 32)
            low, high = pl.ds(pl.multiple_of(i * 32, 32), 32), pl.ds(pl.multiple_of(SPAN + i * 32, 32), 32)
            weights, moved = prob[at, :], prob_tan[at, :]
            pulled, pulled_tan = score[h, low, :], score[h, high, :]
            base = jnp.sum(weights * pulled, axis=-1, keepdims=True)
            base_tan = jnp.sum(moved * pulled + weights * pulled_tan, axis=-1, keepdims=True)
            less = pulled - base
            slope[h, high, :] = (weights * less).astype(BF)
            slope[h, low, :] = (moved * less + weights * (pulled_tan - base_tan)).astype(BF)
            return carry

        lax.fori_loop(0, SPAN // 32, rows_back, 0, unroll=2)

    def value_terms(h, g):
        def step(b, carry):
            cv_acc[b] += dot(g, rnd[h, :, keys_of(b)], NN)
            return carry

        lax.fori_loop(0, 4, step, 0, unroll=2)

    def slopes(h, g):
        one, two = g[:, :SPAN], g[:, SPAN:]
        gg[h] = jnp.concatenate(
            [jnp.concatenate([one, two], axis=1), jnp.concatenate([jnp.zeros_like(one), one], axis=1)],
            axis=0,
        ).astype(F32).T.astype(BF)
        pulls(gg, v_part, h)
        soft_back(h)

    def key_terms(h):
        def step(b, carry):
            ck_acc[b] += dot(qk[h], slope[h, :, keys_of(b)], NN)
            return carry

        lax.fori_loop(0, 4, step, 0, unroll=2)

    def query_terms(h):
        terms = joint(pl.ds(0, 2 * HS), slope, h)
        total = (terms[:HS, :SPAN] + terms[HS:, SPAN:]) * root
        turned_back = rotate(total.astype(BF).astype(F32), own_trig, -1.0, span(h))
        cot[s, 0:HS, span(h)] = turned_back.astype(BF)

    def send_query(h, within):
        at = cot.at[s, pl.ds(0, HS), pl.ds(h * SPAN, SPAN)]
        return remote(at, at, crs, within)

    def chip_sums(own, other, kept):
        for k in range(2):
            kept[k] = total_of(own[2 * k + c], [other[k]]).astype(BF)

    r_two.append(scatter_two(1))
    g_first = scattered(0)
    value_terms(0, g_first)
    slopes(0, g_first)
    key_terms(0)
    query_terms(0)
    q_far = group(cot.at[0, pl.ds(0, HS)])
    send_query(0, q_far)

    def hand_out(k, source, to):
        held = group(ca.at[0, pl.ds(0, 3)])
        for d in (1, 2, 3):
            remote(source.at[(z + d) % 4], to.at[z], fin(d), held)
        lone = Group(source.at[z], send.at[count[0]], recv.at[count[0]])
        count[0] += 1
        there = remote(source.at[z], to.at[z], fin(0), lone, begin=False)
        here = nearby(source.at[z], to.at[z])

        @pl.when(jnp.logical_not(alone))
        def _():
            there.start()

        @pl.when(alone)
        def _():
            here.start()

        return held, there, here

    arrived([o_crs[0]])
    fa[...] = total_of(ha[:, kept], [ca[near], ya[...]]).astype(BF)
    o_fin = [hand_out(0, fa, oa)]

    g_second = scattered(1)
    n_two.append(spread_normed(pl.ds(SHARE // 2, SHARE // 2)))
    value_terms(1, g_second)
    cv[...] = cv_acc[...].astype(BF)
    v_core = group(cvr)
    for k in range(2):
        remote(cv.at[2 * k + 1 - c], cvr.at[k], sib, v_core)
    slopes(1, g_second)

    arrived([v_core])
    chip_sums(cv, cvr, cvs)
    v_far = remote(cvs, cvf, crs)
    key_terms(1)
    ck[...] = (ck_acc[...] * root).astype(BF)

    k_core = group(ckr)
    for k in range(2):
        remote(ck.at[2 * k + 1 - c], ckr.at[k], sib, k_core)
    query_terms(1)
    k_rows, head_part = pl.ds(HS, HS), pl.ds(0, 2 * HS)
    tail_part = pl.ds(2 * HS, HS)
    arrived([k_core])
    chip_sums(ck, ckr, cks)
    k_far = remote(cks, ckf, crs)
    send_query(1, q_far)

    e_base = (
        lax.broadcasted_iota(jnp.int32, (HALF, PART), 0) * D
        + lax.broadcasted_iota(jnp.int32, (HALF, PART), 1)
        + (D * WIDE + fs * HS * D + s * SHARE)
    ) * jnp.int32(MIX[0]) + seeded
    scale = math.sqrt(INNER)
    leaving = []

    def result(half):
        held, there, here = o_fin[half]
        arrived([held])

        @pl.when(jnp.logical_not(alone))
        def _():
            there.wait_recv()
            there.wait_send()

        @pl.when(alone)
        def _():
            here.wait()

        at = pl.ds(half * HALF, HALF)
        for k in range(4):
            bit = sign_bit(e_base + jnp.int32(wrap((half * HALF * D + k * PART) * MIX[0])))
            signed = (oa, ob)[half][k].astype(F32) * jnp.where(bit == 0, F32(scale), F32(-scale))
            oo[at, k * PART : (k + 1) * PART] = signed.astype(BF)
        leaving.append(stay(oo.at[at], oo_out.at[at]))


    arrived([v_far])
    for k in range(2):
        cot[2 * k + c, tail_part] = total_of(cvs[k], [cvf[k]]).astype(BF)
    t_tail = group(cvr)
    for k in range(2):
        remote(cot.at[2 * k + c, tail_part], cot.at[2 * k + c, tail_part], sib, t_tail)
    arrived([o_crs[1]])
    fb[...] = total_of(hb[kept], [cb[near], yb[...]]).astype(BF)
    o_fin.append(hand_out(1, fb, ob))


    turns = [
        trig(jnp.broadcast_to(gkv[2 * k + c, KEYS - 16 : KEYS].astype(F32)[0:1], (ROT, TOK)))
        for k in range(2)
    ]
    arrived([n_sib] + n_two)

    def first_terms(part):
        def term(i, carry):
            at = lanes(i * TOK, TOK)
            acc_q[part, at] = dot(cot[s, part], nrm[:, lanes(s * SHARE + i * TOK, TOK)], NN) + dot(
                cot[s_crs, part], nb[s_crs, :, at], NN
            )
            return carry

        lax.fori_loop(0, SHARE // TOK, term, 0, unroll=2)

    def last_terms(part, start, stop):
        def term(i, carry):
            at = lanes(i * TOK, TOK)
            total = acc_q[part, at] + (
                dot(cot[s_sib, part], nb[s_sib, :, at], NN) + dot(cot[s_crd, part], nb[s_crd, :, at], NN)
            )
            oq[part, at] = (total * sgn[part, at]).astype(BF)
            return carry

        lax.fori_loop(start, stop, term, 0, unroll=3)

    first_terms(tail_part)
    arrived([t_tail])
    last_terms(tail_part, 0, 6)
    leaving.append(stay(oq.at[tail_part], oq_out.at[tail_part]))

    arrived([k_far])
    for k in range(2):
        both = total_of(cks[k], [ckf[k]]).astype(BF).astype(F32)
        cot[2 * k + c, k_rows] = rotate(both, turns[k], -1.0).astype(BF)
    arrived([q_far])
    t_head = group(cot.at[pl.ds(0, 2), head_part])
    for k in range(2):
        remote(cot.at[2 * k + c, head_part], cot.at[2 * k + c, head_part], sib, t_head)
    first_terms(head_part)

    result(0)

    arrived([t_head])
    for k in range(2):
        last_terms(head_part, k * 3, k * 3 + 3)
        cols = pl.ds(k * SHARE // 2, SHARE // 2)
        leaving.append(stay(oq.at[head_part, cols], oq_out.at[head_part, cols]))
    result(1)
    for copy in leaving:
        copy.wait()

    for copy in sent:
        copy.wait_send()


def widen(product_in, out_in, product, out, narrow, narrow_out, wide, wide_out, loads, stores):
    pieces = [pl.ds(k * SHARE // 6, SHARE // 6) for k in range(6)]
    parts = [(product_in.at[:, at], narrow.at[k], wide.at[k], product.at[:, at]) for k, at in enumerate(pieces)]
    parts.append((out_in, narrow_out, wide_out, out))
    arrive = [pltpu.make_async_copy(part[0], part[1], loads.at[k]) for k, part in enumerate(parts)]
    leave = [pltpu.make_async_copy(part[2], part[3], stores.at[k]) for k, part in enumerate(parts)]
    for copy in arrive:
        copy.start()
    for k, part in enumerate(parts):
        arrive[k].wait()
        part[2][...] = part[1][...].astype(F32)
        leave[k].start()
    for copy in leave:
        copy.wait()


def tables():
    rate = 10000.0 ** (-2.0 * np.arange(ROT // 2) / ROT)
    rate = np.concatenate([rate, rate])[:, None]
    within = np.arange(TOK)[None, :] * rate
    blocks = np.arange(4)[:, None, None] * float(TOK) * rate[None] + np.zeros((1, 1, TOK))
    tab_t = np.stack([np.cos(within), np.sin(within)]).astype(np.float32)
    tab_b = np.stack([np.cos(blocks), np.sin(blocks)], axis=1).astype(np.float32)
    return tab_t, tab_b


def per_device(tokens, target, norm_gain, qkv_weight, out_weight, probe_seed, block_order):
    tab_t, tab_b = tables()
    anywhere = pl.BlockSpec(memory_space=pl.ANY)
    v = pltpu.VMEM
    scratch = [
        pltpu.SMEM((1,), jnp.int32), pltpu.SMEM((1,), jnp.int32),
        v((COLS, SHARE), BF), v((HS, SHARE), BF), v((1, D), F32), v((2, ROT, TOK), F32), v((4, 2, ROT, TOK), F32),
        v((TOK, D), BF), v((TOK, PART), BF), v((COLS, D), BF), v((TOK, D), BF), v((2, COLS, TOK), F32),
        v((3, TOK, 128), F32), v((16, D), BF), v((4, TOK, SHARE), BF), v((4, 4 * HS + 16, TOK), BF),
        v((4, 4, HALF, PART), BF), v((2, 4, 4, HALF, PART), BF), v((2, 4, 4, HALF, PART), BF),
        v((2, 2 * PART, 16 * HALF), BF),
        v((2, 4, 4, HALF, 2 * SPAN), BF), v((2, 4, 4, HALF, 2 * SPAN), BF),
        v((2, 2 * SPAN, 2 * HS), BF), v((2, HS, 2 * SPAN), BF), v((2, 2 * SPAN, 2 * HS), BF),
        v((2, 2 * SPAN, 1024), F32), v((TOK, 1024), F32), v((TOK, 1024), F32),
        v((2, 2 * SPAN, 1024), BF), v((2, 2 * SPAN, 1024), BF),
        v((4, HS, TOK), F32), v((4, HS, TOK), F32),
        v((2, PART, 2 * SPAN), F32), v((2, PART, 2 * SPAN), BF), v((2, PART, 2 * SPAN), BF),
        v((2, 2, 16 * HALF, SPAN), F32), v((2, PART, 2 * SPAN), BF), v((PART, TOK), F32),
        v((2, 2, 4, 4, HALF, 2 * SPAN), BF),
        v((2, 3, 4, HALF, 2 * SPAN), BF), v((2, 3, 4, HALF, 2 * SPAN), BF),
        v((2, 4, HALF, 2 * SPAN), BF), v((2, 4, HALF, 2 * SPAN), BF),
        v((2, 3, HALF, 2 * SPAN), BF), v((2, 3, HALF, 2 * SPAN), BF),
        v((4, 4, HALF, PART), BF), v((4, 4, HALF, PART), BF),
        v((2, 4, HALF, PART), BF), v((2, 4, HALF, PART), BF),
        v((4, HALF, PART), BF), v((4, HALF, PART), BF), v((4, HALF, PART), BF), v((4, HALF, PART), BF),
        v((4, HALF, PART), BF), v((4, HALF, PART), BF), v((4, HALF, PART), BF), v((4, HALF, PART), BF),
        v((4, HS, TOK), BF), v((2, HS, TOK), BF), v((2, HS, TOK), BF), v((2, HS, TOK), BF),
        v((4, HS, TOK), BF), v((2, HS, TOK), BF), v((2, HS, TOK), BF), v((2, HS, TOK), BF),
        v((4, 3 * HS, TOK), BF), v((COLS, SHARE), F32), v((COLS, SHARE), F32), v((2, 16 * HALF, PART), F32),
        pltpu.SemaphoreType.DMA((N_REMOTE,)), pltpu.SemaphoreType.DMA((N_REMOTE,)),
        pltpu.SemaphoreType.DMA((N_LOCAL,)),
    ]
    product, out_curv = pl.pallas_call(
        kernel,
        out_shape=(
            jax.ShapeDtypeStruct((COLS, SHARE), BF),
            jax.ShapeDtypeStruct((HS, SHARE), BF),
        ),
        in_specs=[anywhere] * 9,
        out_specs=(anywhere, anywhere),
        scratch_shapes=scratch,
        compiler_params=pltpu.CompilerParams(
            collective_id=0, has_side_effects=True, vmem_limit_bytes=60 * 2**20
        ),
    )(
        tokens, target, norm_gain.reshape(1, D), qkv_weight.T, out_weight, probe_seed, block_order,
        jnp.asarray(tab_t), jnp.asarray(tab_b),
    )
    product, out_curv = pl.pallas_call(
        widen,
        out_shape=(
            jax.ShapeDtypeStruct((COLS, SHARE), F32),
            jax.ShapeDtypeStruct((HS, SHARE), F32),
        ),
        in_specs=[anywhere, anywhere],
        out_specs=(anywhere, anywhere),
        scratch_shapes=[
            v((6, COLS, SHARE // 6), BF), v((HS, SHARE), BF),
            v((6, COLS, SHARE // 6), F32), v((HS, SHARE), F32),
            pltpu.SemaphoreType.DMA((7,)), pltpu.SemaphoreType.DMA((7,)),
        ],
    )(product, out_curv)
    return product.T, out_curv


def solution(mesh):
    placed = (P("seq", None), P("seq", None), P(), P(None, "fsdp"), P("fsdp", None), P(), P("seq"))
    return jax.shard_map(
        per_device,
        mesh=mesh,
        in_specs=placed,
        out_specs=(P("seq", "fsdp"), P("fsdp", "seq")),
        check_vma=False,
    )
```

```python
import functools
import math

import jax
import jax.numpy as jnp
import numpy as np
from jax import lax
from jax.experimental import pallas as pl
from jax.experimental.pallas import tpu as pltpu
from jax.sharding import PartitionSpec as P

MESH = pl.DeviceIdType.MESH
BF = jnp.bfloat16
F32 = jnp.float32
D = 6144
HS = 96
ROT = 24
TOK = 256
COLS = 288
WIDE = 9216
INNER = 3072
SHARE = 1536
PART = 384
HALF = 48
SPAN = 128
KEYS = 2 * HS + 16
STEP = 768
MIX = (-1640531535, -2048144789, -1028477387)
N_REMOTE = 52
N_LOCAL = 25


def wrap(value):
    return ((value + 2**31) % 2**32) - 2**31


def shifted(state, places):
    return lax.shift_right_logical(state, jnp.full(state.shape, places, jnp.int32))


def sign_word(state):
    state = state ^ shifted(state, 16)
    state = state * jnp.int32(MIX[1])
    state = state ^ shifted(state, 13)
    state = state * jnp.int32(wrap(MIX[2] * 256))
    return state ^ lax.shift_left(state, jnp.full(state.shape, 16, jnp.int32))


def dot(a, b, contract):
    return lax.dot_general(a, b, (contract, ((), ())), preferred_element_type=F32)


NN = ((1,), (0,))
NT = ((1,), (1,))
TN = ((0,), (0,))


class Group:
    def __init__(self, size, send, recv):
        self.size, self.send, self.recv = size, send, recv

    def wait_recv(self):
        pltpu.make_async_copy(self.size, self.size, self.recv).wait()

    def wait_send(self):
        pltpu.make_async_copy(self.size, self.size, self.send).wait()


def kernel(
    tok_in, tgt_in, gain_in, wq_in, wo_in, seed_in, block_in, tab_t_in, tab_b_in,
    oq_out, oo_out,
    seed, block, oq, oo, gain, tab_t, tab_b, tok, tgt, wq, nrm, acc,
    stat, few, nb, gkv,
    wt, ww, pp, wpt, ga, gb,
    qq, qk, gg, score, prob, prob_tan, rnd, slope, cv_acc, ck_acc,
    mix_acc, mix_out, mix_in, back_acc, grad, resid,
    sab, ra1, rb1, sa2, sb2, ra2, rb2,
    ha, hb, ca, cb, xa, xb, ya, yb, fa, fb, oa, ob,
    cv, cvr, cvs, cvf, ck, ckr, cks, ckf, cot, sgn, acc_q, out_acc,
    send, recv, local,
):
    fs = lax.axis_index("fsdp")
    s = lax.axis_index("seq")
    x = fs // 8
    yl = (fs // 4) % 2
    z = fs % 4
    yh = s // 2
    c = s % 2
    s_sib = yh * 2 + (1 - c)
    s_crs = (1 - yh) * 2 + c
    s_crd = (1 - yh) * 2 + (1 - c)
    own_cols = (x * 4 + z) * PART

    def device(px, py, pz, ps):
        return ((px * 2 + py) * 4 + pz, ps)

    def xp(d):
        return device((x + d) % 4, yl, z, s)

    def zp(d):
        return device(x, yl, (z + d) % 4, s)

    kept = (s + 2 * (x % 2)) % 4
    alone = (x == s) & (x % 2 == 0)

    def fin(d):
        return device(kept, yl, (z + d) % 4, x)

    def fin_from(d):
        return device(s, yl, (z + d) % 4, (x + 2 * (s % 2)) % 4)

    partner = device(x, 1 - yl, z, s)
    sib = device(x, yl, z, s_sib)
    crs = device(x, yl, z, s_crs)
    crd = device(x, yl, z, s_crd)

    count = [0]
    sent = []

    def group(size):
        i = count[0]
        count[0] += 1
        sent.append(Group(size, send.at[i], recv.at[i]))
        return sent[-1]

    def remote(src, dst, to, within=None, begin=True):
        held = within or group(dst)
        copy = pltpu.make_async_remote_copy(
            src_ref=src, dst_ref=dst, send_sem=held.send, recv_sem=held.recv,
            device_id=to, device_id_type=MESH,
        )
        if begin:
            copy.start()
        return copy if not begin else held

    local_count = [0]

    def stay(src, dst):
        i = local_count[0]
        local_count[0] += 1
        copy = pltpu.make_async_copy(src, dst, local.at[i])
        copy.start()
        return copy

    def nearby(src, dst):
        i = local_count[0]
        local_count[0] += 1
        return pltpu.make_async_copy(src, dst, local.at[i])

    def arrived(copies):
        for copy in copies:
            copy.wait_recv()

    def lanes(start, size):
        return pl.ds(pl.multiple_of(start, 128), size)

    def rows(start, size):
        return pl.ds(pl.multiple_of(start, 16), size)

    tok_loads = [stay(tok_in.at[pl.ds(k * 64, 64)], tok.at[pl.ds(k * 64, 64)]) for k in range(4)]
    tab_loads = [stay(seed_in, seed), stay(block_in, block), stay(gain_in, gain), stay(tab_t_in, tab_t), stay(tab_b_in, tab_b)]
    tgt_load = stay(tgt_in.at[:, lanes(own_cols, PART)], tgt)
    first, second = jnp.where(c == 0, x, z), jnp.where(c == 0, z, x)

    def column(a, k):
        return jnp.where(c == 0, a * 4 + k, k * 4 + a) * PART

    own_w = [
        stay(wo_in.at[rows(c * HALF, HALF), lanes(column(first, k), PART)], wt.at[first, k])
        for k in range(4)
    ]

    barrier = pltpu.get_barrier_semaphore()

    def greet(to):
        pl.semaphore_signal(barrier, inc=1, device_id=to, device_id_type=MESH)

    for d in (1, 2, 3):
        greet(xp(d))
        greet(zp(d))
    for to in (partner, sib, crs, crd):
        greet(to)

    for d in (1, 2, 3):
        greet(fin_from(d))

    @pl.when(jnp.logical_not(alone))
    def _():
        greet(fin_from(0))


    def norm_sums(i, carry):
        at = rows(i * 16, 16)
        middle = stat[0, at, :]
        totals = [jnp.zeros((16, 128), F32) for _ in range(4)]
        for k in range(D // 128):
            moved = tok[at, k * 128 : (k + 1) * 128].astype(F32) - middle
            totals[k % 2] += moved
            totals[2 + k % 2] += moved * moved
        stat[1, at, :] = totals[0] + totals[1]
        stat[2, at, :] = totals[2] + totals[3]
        return carry

    for k in range(4):
        tok_loads[k].wait()
        at = pl.ds(k * 64, 64)
        pivot = jnp.mean(tok[at, 0:128].astype(F32), axis=-1, keepdims=True)
        stat[0, at] = jnp.broadcast_to(pivot, (64, 128))
        lax.fori_loop(k * 4, (k + 1) * 4, norm_sums, 0, unroll=2)
    wq_load = stay(wq_in, wq)
    drift = jnp.sum(stat[1], axis=-1, keepdims=True) * (1 / D)
    spread = jnp.sum(stat[2], axis=-1, keepdims=True) * (1 / D) - drift * drift
    stat[0] += jnp.broadcast_to(drift, (TOK, 128))
    stat[1] = jnp.broadcast_to(lax.rsqrt(jnp.maximum(spread, 0.0) + 1e-05), (TOK, 128))

    pl.semaphore_wait(barrier, jnp.where(alone, 13, 14))

    def along_first(d):
        return device(
            jnp.where(c == 0, (x + d) % 4, x), yl, jnp.where(c == 0, z, (z + d) % 4), s
        )

    def along_second(d):
        return device(
            jnp.where(c == 0, x, (x + d) % 4), yl, jnp.where(c == 0, (z + d) % 4, z), s
        )

    w_one = group(wt.at[pl.ds(0, 3)])
    for d in (1, 2, 3):
        for k in range(4):
            remote(
                wo_in.at[rows(c * HALF, HALF), lanes(column((first + d) % 4, k), PART)],
                wt.at[first, k], along_first(d), w_one,
            )

    for copy in tab_loads:
        copy.wait()

    def norm_into(to, start, at):
        middle, factor = stat[0, at, :], stat[1, at, :]
        for k in range(D // 128):
            cols = slice(k * 128, (k + 1) * 128)
            to[start, cols] = ((tok[at, cols].astype(F32) - middle) * factor * gain[:, cols]).astype(BF)

    def norm_rows(i, carry):
        norm_into(nrm, rows(i * 16, 16), rows(i * 16, 16))
        return carry

    piece = jnp.where(c == 0, z * 4 + x, x * 4 + z) * 16
    norm_into(few, slice(0, 16), rows(piece, 16))
    n_far = group(nb.at[0, pl.ds(0, 32)])
    remote(
        few.at[:, lanes(s_crs * SHARE, SHARE)], nb.at[s, rows(piece, 16)], crs, n_far
    )
    remote(
        few.at[:, lanes(s_crd * SHARE, SHARE)], nb.at[s, rows(piece, 16)], crd, n_far
    )


    lax.fori_loop(0, TOK // 16, norm_rows, 0)

    n_sib = remote(nrm.at[:, lanes(s_sib * SHARE, SHARE)], nb.at[s], sib)

    wq_load.wait()
    acc[...] = jnp.zeros_like(acc)
    seeded = seed[0]
    q_probe = float(np.float32(1 / math.sqrt(D)).astype(jnp.bfloat16))
    o_probe = float(np.float32(1 / math.sqrt(INNER)).astype(jnp.bfloat16))

    def project(start, size, steps=(0, D // STEP)):
        q_rows = lax.broadcasted_iota(jnp.int32, (size, STEP), 1)
        q_cols = lax.broadcasted_iota(jnp.int32, (size, STEP), 0)
        q_base = (q_rows * WIDE + q_cols + (fs * COLS + start)) * jnp.int32(MIX[0]) + seeded
        to = pl.ds(start, size)

        def step(i, carry):
            at = pl.ds(pl.multiple_of(i * STEP, STEP), STEP)
            word = sign_word(q_base + i * jnp.int32(wrap(STEP * WIDE * MIX[0])))
            probe = jnp.where(word >= 0, F32(q_probe), F32(-q_probe)).astype(BF)
            both = dot(jnp.concatenate([wq[to, at], probe], axis=0), nrm[:, at], NT)
            acc[0, to] += both[:size]
            acc[1, to] += both[size:]
            return carry

        lax.fori_loop(*steps, step, 0)

    project(HS, 2 * HS)

    number = block[0]
    low = lax.broadcasted_iota(jnp.int32, (ROT, TOK), 0) < ROT // 2

    def trig(here):
        cos_b = jnp.zeros((ROT, TOK), F32)
        sin_b = jnp.zeros((ROT, TOK), F32)
        for k in range(4):
            cos_b = jnp.where(here == k, tab_b[k, 0], cos_b)
            sin_b = jnp.where(here == k, tab_b[k, 1], sin_b)
        cos = cos_b * tab_t[0] - sin_b * tab_t[1]
        sin = sin_b * tab_t[0] + cos_b * tab_t[1]
        return cos, jnp.where(low, -sin, sin)

    own_trig = trig(jnp.full((ROT, TOK), number, jnp.int32))

    def rotate(field, turns, sign=1.0, cols=slice(0, TOK)):
        cos, sin = turns[0][:, cols], turns[1][:, cols]
        head = field[:ROT]
        swapped = pltpu.roll(head, ROT // 2, 0)
        return jnp.concatenate([head * cos + swapped * (sin * sign), field[ROT:]], axis=0)

    for k in range(2):
        gkv[s, k * HS : (k + 1) * HS] = rotate(acc[k, HS : 2 * HS], own_trig).astype(BF)
    gkv[s, KEYS - 16 : KEYS] = jnp.full((16, TOK), number, jnp.int32).astype(F32).astype(BF)
    k_part, v_part = pl.ds(0, KEYS), pl.ds(KEYS, 2 * HS)

    def spread_kv(slot, part, to):
        return remote(gkv.at[slot, part], gkv.at[slot, part], to)

    k_crs = spread_kv(s, k_part, crs)
    k_sib = spread_kv(s, k_part, sib)
    for k in range(2):
        gkv[s, KEYS + k * HS : KEYS + (k + 1) * HS] = acc[k, 2 * HS : 3 * HS].astype(BF)
    v_crs = spread_kv(s, v_part, crs)
    v_sib = spread_kv(s, v_part, sib)

    b0 = (1 - yh) * 2
    b1 = b0 + 1
    arrived([n_far])
    n_one = group(nb.at[0, pl.ds(0, 96)])
    for d in (1, 2, 3):
        at0 = nb.at[b0, rows((z * 4 + x) * 16, 16)]
        at1 = nb.at[b1, rows((x * 4 + z) * 16, 16)]
        remote(at0, at0, xp(d), n_one)
        remote(at1, at1, zp(d), n_one)

    def span(h):
        return slice(h * SPAN, (h + 1) * SPAN)

    tgt_load.wait()
    project(0, HS, (0, 4))

    for copy in own_w:
        copy.wait()
    arrived([w_one])
    w_two = group(ww.at[0, pl.ds(0, 3)])
    for d in (1, 2, 3):
        remote(wt.at[:, (second + d) % 4], ww.at[c, second], along_second(d), w_two)
    own_ww = stay(wt.at[:, second], ww.at[c, second])

    project(0, HS, (4, D // STEP))

    q = rotate(acc[0, :HS], own_trig).astype(BF)
    q_tan = rotate(acc[1, :HS], own_trig).astype(BF)
    for h in range(2):
        one, two = q[:, span(h)], q_tan[:, span(h)]
        qq[h] = jnp.concatenate(
            [jnp.concatenate([one, two], axis=1), jnp.concatenate([jnp.zeros_like(one), one], axis=1)],
            axis=0,
        ).astype(F32).T.astype(BF)
        qk[h] = jnp.concatenate([one, two], axis=1)
    resid[...] = (tok[:, lanes(own_cols, PART)].astype(F32) - tgt[...].astype(F32)).T

    def spread_normed(cols):
        held = group(nb.at[pl.ds(0, 2), pl.ds(0, 192), cols])
        for d in (1, 2, 3):
            at0 = nb.at[b0, rows(z * 64, 64), cols]
            at1 = nb.at[b1, rows(x * 64, 64), cols]
            remote(at0, at0, zp(d), held)
            remote(at1, at1, xp(d), held)
        return held

    arrived([k_crs])
    k_rel = spread_kv(s_crs, k_part, sib)

    root = 1 / math.sqrt(HS)

    def keys_of(b):
        return lanes(b * TOK, TOK)

    def pulls(left, part, h, blocks=range(4)):
        for b in blocks:
            score[h, :, keys_of(b)] = dot(left[h], gkv[b, part], NN)

    along = lax.broadcasted_iota(jnp.int32, (1, TOK), 1).astype(F32)
    number_f = jnp.full((32, 1), number, jnp.int32).astype(F32)
    down = lax.broadcasted_iota(jnp.int32, (32, 1), 0)

    def soft(h):
        def soft_rows(i, carry):
            at = pl.ds(pl.multiple_of(h * SPAN + i * 32, 32), 32)
            low, high = pl.ds(pl.multiple_of(i * 32, 32), 32), pl.ds(pl.multiple_of(SPAN + i * 32, 32), 32)
            query_pos = number_f * float(TOK) + (down + (h * SPAN + i * 32)).astype(F32)
            allowed = key_pos <= query_pos
            values = jnp.where(allowed, score[h, low, :] * root, -1e30)
            highest = jnp.max(values, axis=-1, keepdims=True)
            weights = jnp.exp(values - highest)
            weights = weights * (1.0 / jnp.sum(weights, axis=-1, keepdims=True))
            moved = weights * (score[h, high, :] * root)
            moved = moved - weights * jnp.sum(moved, axis=-1, keepdims=True)
            prob[at, :] = weights
            prob_tan[at, :] = moved
            rnd[h, high, :] = weights.astype(BF)
            rnd[h, low, :] = moved.astype(BF)
            return carry

        lax.fori_loop(0, SPAN // 32, soft_rows, 0, unroll=2)

    def joint(part, ref, h):
        def term(b, held):
            return held + dot(gkv[b, part], ref[h, :, keys_of(b)], NT)

        return lax.fori_loop(0, 4, term, jnp.zeros((2 * HS, 2 * SPAN), F32))

    def attn_products(h):
        terms = joint(v_part, rnd, h)
        both = jnp.concatenate([terms[:HS, SPAN:], terms[:HS, :SPAN] + terms[HS:, SPAN:]], axis=1)
        both = both.astype(BF)
        ga[h, z, x] = both[:HALF]
        gb[h, x, z] = both[HALF:]
        held = group(ra1.at[0, pl.ds(0, 3), pl.ds(0, 2)])
        for d in (1, 2, 3):
            remote(ga.at[h, z, x], ga.at[h, z, x], xp(d), held)
            remote(gb.at[h, x, z], gb.at[h, x, z], zp(d), held)
        return held

    def side(t):
        return pl.ds(t * SPAN, SPAN)

    def gather_two(h):
        groups = []
        for t in range(2):
            held = group(ra1.at[:, :, :, :, side(t)])
            for d in (1, 2, 3):
                at0, at1 = ga.at[h, z, :, :, side(t)], gb.at[h, x, :, :, side(t)]
                remote(at0, at0, zp(d), held)
                remote(at1, at1, xp(d), held)
            groups.append(held)
        return groups

    pulls(qq, pl.ds(0, 2 * HS), 0, (s, s_crs))
    pulls(qq, pl.ds(0, 2 * HS), 1, (s, s_crs))
    arrived([k_sib, k_rel])
    key_pos = jnp.concatenate(
        [gkv[b, KEYS - 16 : KEYS].astype(F32)[0:1] * float(TOK) + along for b in range(4)], axis=1
    )
    pulls(qq, pl.ds(0, 2 * HS), 0, (s_sib, s_crd))
    pulls(qq, pl.ds(0, 2 * HS), 1, (s_sib, s_crd))
    arrived([n_one])
    n_two = [spread_normed(pl.ds(0, SHARE // 4))]
    arrived([v_crs])
    v_rel = spread_kv(s_crs, v_part, sib)
    soft(0)
    arrived([v_sib, v_rel])
    g_one = [attn_products(0)]
    own_ww.wait()
    arrived([w_two])
    w_sib = remote(ww.at[c], ww.at[c], sib)
    soft(1)

    g_one.append(attn_products(1))

    o_rows = lax.broadcasted_iota(jnp.int32, (HALF, PART), 0)
    o_lanes = lax.broadcasted_iota(jnp.int32, (HALF, PART), 1)
    o_base = (o_rows * D + o_lanes + (D * WIDE + own_cols)) * jnp.int32(MIX[0]) + seeded

    def probe_piece(i, carry):
        for k in range(4):
            first = ((k * 2 + yl) * 4 + i) * HS
            second = ((i * 2 + yl) * 4 + k) * HS + HALF
            word = sign_word(o_base + first * jnp.int32(wrap(D * MIX[0])))
            pp[0, i, k] = jnp.where(word >= 0, F32(o_probe), F32(-o_probe)).astype(BF)
            word = sign_word(o_base + second * jnp.int32(wrap(D * MIX[0])))
            pp[1, i, k] = jnp.where(word >= 0, F32(o_probe), F32(-o_probe)).astype(BF)
        return carry

    lax.fori_loop(0, 4, probe_piece, 0)

    def turned(source, start):
        def turn(i, carry):
            for a in range(2):
                value = source[a, pl.ds(2 * i, 2)].reshape(8 * HALF, PART).astype(F32)
                wpt[a, start : start + PART, lanes(i * 8 * HALF, 8 * HALF)] = value.T.astype(BF)
            return carry

        lax.fori_loop(0, 2, turn, 0)

    turned(pp, PART)

    arrived([g_one[0]])
    g_two = [gather_two(0)]
    arrived([w_sib])
    turned(ww, 0)
    arrived([g_one[1]])
    g_two.append(gather_two(1))
    n_two.append(spread_normed(pl.ds(SHARE // 4, SHARE // 4)))

    s_base = (
        (lax.broadcasted_iota(jnp.int32, (COLS, TOK), 1) + s * SHARE) * WIDE
        + lax.broadcasted_iota(jnp.int32, (COLS, TOK), 0)
        + fs * COLS
    ) * jnp.int32(MIX[0]) + seeded

    def sign_cols(i, carry):
        word = sign_word(s_base + i * jnp.int32(wrap(TOK * WIDE * MIX[0])))
        sgn[:, lanes(i * TOK, TOK)] = jnp.where(word >= 0, F32(math.sqrt(D)), F32(-math.sqrt(D)))
        return carry

    lax.fori_loop(0, SHARE // TOK, sign_cols, 0)

    def products(h, t, tall):
        right = [
            ref[h, :, :, :, t * SPAN : (t + 1) * SPAN].reshape(16 * HALF, SPAN) for ref in (ga, gb)
        ]
        return dot(wpt[0, 0:tall], right[0], NN) + dot(wpt[1, 0:tall], right[1], NN)

    def trade(h, t):
        part = side(t)
        mix_out[h, :, part] = mix_acc[h, :, part].astype(BF)
        return remote(mix_out.at[h, :, part], mix_in.at[h, :, part], partner)

    def mix(h, t):
        arrived([g_two[h][t]])
        if t == 0:
            total = products(h, 0, 2 * PART)
            mix_acc[h, :, side(0)] = total[:PART]
            mix_acc[h, :, side(1)] = total[PART:]
        else:
            mix_acc[h, :, side(1)] += products(h, 1, PART)
        return trade(h, t)

    m_part = {}
    m_part[0, 0] = mix(0, 0)
    m_part[0, 1] = mix(0, 1)
    m_part[1, 0] = mix(1, 0)

    def back(h, t):
        arrived([m_part[h, t]])
        part = side(t)
        total = mix_acc[h, :, part] + mix_in[h, :, part].astype(F32)
        if t == 0:
            total = total + resid[:, span(h)]
        grad[h, :, part] = (total * (1 / 1024)).astype(BF)

        right = grad[h, :, part]
        for a in range(2):
            first = dot(ww[a].reshape(16 * HALF, PART), right, NN)
            if t == 1:
                first = first + back_acc[h, a]
            sab[h, a, :, :, :, part] = first.astype(BF).reshape(4, 4, HALF, SPAN)
        held = group(ra1.at[:, :, :, :, part])
        for d in (1, 2, 3):
            remote(
                sab.at[h, 0, (z + d) % 4, :, :, part], ra1.at[h, d - 1, :, :, part], zp(d), held
            )
            remote(
                sab.at[h, 1, (x + d) % 4, :, :, part], rb1.at[h, d - 1, :, :, part], xp(d), held
            )
        if t == 0:
            for a in range(2):
                back_acc[h, a] = dot(pp[a].reshape(16 * HALF, PART), right, NN)
        return held

    def total_of(own, others):
        total = own.astype(F32)
        for other in others:
            total = total + other.astype(F32)
        return total

    def scatter_two(h):
        arrived(r_one[h])
        sa2[h] = total_of(sab[h, 0, z], [ra1[h, k] for k in range(3)]).astype(BF)
        sb2[h] = total_of(sab[h, 1, x], [rb1[h, k] for k in range(3)]).astype(BF)
        held = group(ra2)
        for d in (1, 2, 3):
            remote(sa2.at[h, (x + d) % 4], ra2.at[h, d - 1], xp(d), held)
            remote(sb2.at[h, (z + d) % 4], rb2.at[h, d - 1], zp(d), held)
        return held

    def scattered(h):
        arrived([r_two[h]])
        first = total_of(sa2[h, x], [ra2[h, k] for k in range(3)])
        second = total_of(sb2[h, z], [rb2[h, k] for k in range(3)])
        return jnp.concatenate([first.astype(BF), second.astype(BF)], axis=0)

    def out_terms(h, t):
        right = grad[h, :, side(t)].astype(F32).T.astype(BF)
        for a, (ref, to) in enumerate(((ga, ha), (gb, hb))):
            left = ref[h, :, :, :, (1 - t) * SPAN : (2 - t) * SPAN].reshape(16 * HALF, SPAN)
            total = dot(left, right, NN)
            if (h, t) == (0, 0):
                out_acc[a] = total
            elif (h, t) == (1, 1):
                to[...] = (out_acc[a] + total).astype(BF).reshape(4, 4, HALF, PART)
                half, come = ((ha, ca), (hb, cb))[a]
                held = group(come)
                for k in range(2):
                    from_one = half.at[:, 2 * k + 1 - c] if a == 0 else half.at[2 * k + 1 - c]
                    remote(from_one, come.at[k], sib, held)
                o_core.append(held)
            else:
                out_acc[a] += total

    o_core = []
    r_one = [[back(0, 0)], []]
    m_part[1, 1] = mix(1, 1)
    r_one[0].append(back(0, 1))
    out_terms(0, 0)
    out_terms(0, 1)
    r_one[1].append(back(1, 0))
    out_terms(1, 0)
    r_one[1].append(back(1, 1))
    out_terms(1, 1)


    near, far = kept // 2, 1 - kept // 2
    arrived([o_core[0]])
    xa[...] = total_of(ha[:, 2 * far + c], [ca[far]]).astype(BF)
    o_crs = [remote(xa, ya, crs)]
    r_two = [scatter_two(0)]
    arrived([o_core[1]])
    xb[...] = total_of(hb[2 * far + c], [cb[far]]).astype(BF)
    o_crs.append(remote(xb, yb, crs))

    cv_acc[...] = jnp.zeros_like(cv_acc)
    ck_acc[...] = jnp.zeros_like(ck_acc)

    def soft_back(h):
        def rows_back(i, carry):
            at = pl.ds(pl.multiple_of(h * SPAN + i * 32, 32), 32)
            low, high = pl.ds(pl.multiple_of(i * 32, 32), 32), pl.ds(pl.multiple_of(SPAN + i * 32, 32), 32)
            weights, moved = prob[at, :], prob_tan[at, :]
            pulled, pulled_tan = score[h, low, :], score[h, high, :]
            base = jnp.sum(weights * pulled, axis=-1, keepdims=True)
            base_tan = jnp.sum(moved * pulled + weights * pulled_tan, axis=-1, keepdims=True)
            less = pulled - base
            slope[h, high, :] = (weights * less).astype(BF)
            slope[h, low, :] = (moved * less + weights * (pulled_tan - base_tan)).astype(BF)
            return carry

        lax.fori_loop(0, SPAN // 32, rows_back, 0, unroll=2)

    def value_terms(h, g):
        def step(b, carry):
            cv_acc[b] += dot(g, rnd[h, :, keys_of(b)], NN)
            return carry

        lax.fori_loop(0, 4, step, 0, unroll=2)

    def slopes(h, g):
        one, two = g[:, :SPAN], g[:, SPAN:]
        gg[h] = jnp.concatenate(
            [jnp.concatenate([one, two], axis=1), jnp.concatenate([jnp.zeros_like(one), one], axis=1)],
            axis=0,
        ).astype(F32).T.astype(BF)
        pulls(gg, v_part, h)
        soft_back(h)

    def key_terms(h):
        def step(b, carry):
            ck_acc[b] += dot(qk[h], slope[h, :, keys_of(b)], NN)
            return carry

        lax.fori_loop(0, 4, step, 0, unroll=2)

    def query_terms(h):
        terms = joint(pl.ds(0, 2 * HS), slope, h)
        total = (terms[:HS, :SPAN] + terms[HS:, SPAN:]) * root
        turned_back = rotate(total.astype(BF).astype(F32), own_trig, -1.0, span(h))
        cot[s, 0:HS, span(h)] = turned_back.astype(BF)

    def send_query(h, within):
        at = cot.at[s, pl.ds(0, HS), pl.ds(h * SPAN, SPAN)]
        return remote(at, at, crs, within)

    def chip_sums(own, other, kept):
        for k in range(2):
            kept[k] = total_of(own[2 * k + c], [other[k]]).astype(BF)

    r_two.append(scatter_two(1))
    g_first = scattered(0)
    value_terms(0, g_first)
    slopes(0, g_first)
    key_terms(0)
    query_terms(0)
    q_far = group(cot.at[0, pl.ds(0, HS)])
    send_query(0, q_far)

    def hand_out(k, source, to):
        held = group(ca.at[0, pl.ds(0, 3)])
        for d in (1, 2, 3):
            remote(source.at[(z + d) % 4], to.at[z], fin(d), held)
        lone = Group(source.at[z], send.at[count[0]], recv.at[count[0]])
        count[0] += 1
        there = remote(source.at[z], to.at[z], fin(0), lone, begin=False)
        here = nearby(source.at[z], to.at[z])

        @pl.when(jnp.logical_not(alone))
        def _():
            there.start()

        @pl.when(alone)
        def _():
            here.start()

        return held, there, here

    arrived([o_crs[0]])
    fa[...] = total_of(ha[:, kept], [ca[near], ya[...]]).astype(BF)
    o_fin = [hand_out(0, fa, oa)]

    g_second = scattered(1)
    n_two.append(spread_normed(pl.ds(SHARE // 2, SHARE // 2)))
    value_terms(1, g_second)
    cv[...] = cv_acc[...].astype(BF)
    v_core = group(cvr)
    for k in range(2):
        remote(cv.at[2 * k + 1 - c], cvr.at[k], sib, v_core)
    slopes(1, g_second)

    arrived([v_core])
    chip_sums(cv, cvr, cvs)
    v_far = remote(cvs, cvf, crs)
    key_terms(1)
    ck[...] = (ck_acc[...] * root).astype(BF)

    k_core = group(ckr)
    for k in range(2):
        remote(ck.at[2 * k + 1 - c], ckr.at[k], sib, k_core)
    query_terms(1)
    k_rows, head_part = pl.ds(HS, HS), pl.ds(0, 2 * HS)
    tail_part = pl.ds(2 * HS, HS)
    arrived([k_core])
    chip_sums(ck, ckr, cks)
    k_far = remote(cks, ckf, crs)
    send_query(1, q_far)

    e_base = (
        lax.broadcasted_iota(jnp.int32, (HALF, PART), 0) * D
        + lax.broadcasted_iota(jnp.int32, (HALF, PART), 1)
        + (D * WIDE + fs * HS * D + s * SHARE)
    ) * jnp.int32(MIX[0]) + seeded
    scale = math.sqrt(INNER)
    leaving = []

    def result(half):
        held, there, here = o_fin[half]
        arrived([held])

        @pl.when(jnp.logical_not(alone))
        def _():
            there.wait_recv()
            there.wait_send()

        @pl.when(alone)
        def _():
            here.wait()

        at = pl.ds(half * HALF, HALF)
        for k in range(4):
            word = sign_word(e_base + jnp.int32(wrap((half * HALF * D + k * PART) * MIX[0])))
            signed = (oa, ob)[half][k].astype(F32) * jnp.where(word >= 0, F32(scale), F32(-scale))
            oo[at, k * PART : (k + 1) * PART] = signed.astype(BF)
        leaving.append(stay(oo.at[at], oo_out.at[at]))


    result(0)

    arrived([o_crs[1]])
    fb[...] = total_of(hb[kept], [cb[near], yb[...]]).astype(BF)
    o_fin.append(hand_out(1, fb, ob))


    arrived([v_far])
    for k in range(2):
        cot[2 * k + c, tail_part] = total_of(cvs[k], [cvf[k]]).astype(BF)
    t_tail = group(cvr)
    for k in range(2):
        remote(cot.at[2 * k + c, tail_part], cot.at[2 * k + c, tail_part], sib, t_tail)
    turns = [
        trig(jnp.broadcast_to(gkv[2 * k + c, KEYS - 16 : KEYS].astype(F32)[0:1], (ROT, TOK)))
        for k in range(2)
    ]
    arrived([n_sib] + n_two)

    def first_terms(part):
        def term(i, carry):
            at = lanes(i * TOK, TOK)
            acc_q[part, at] = dot(cot[s, part], nrm[:, lanes(s * SHARE + i * TOK, TOK)], NN) + dot(
                cot[s_crs, part], nb[s_crs, :, at], NN
            )
            return carry

        lax.fori_loop(0, SHARE // TOK, term, 0, unroll=2)

    def last_terms(part, start, stop):
        def term(i, carry):
            at = lanes(i * TOK, TOK)
            total = acc_q[part, at] + (
                dot(cot[s_sib, part], nb[s_sib, :, at], NN) + dot(cot[s_crd, part], nb[s_crd, :, at], NN)
            )
            oq[part, at] = (total * sgn[part, at]).astype(BF)
            return carry

        lax.fori_loop(start, stop, term, 0, unroll=3)

    first_terms(tail_part)
    arrived([k_far])
    for k in range(2):
        both = total_of(cks[k], [ckf[k]]).astype(BF).astype(F32)
        cot[2 * k + c, k_rows] = rotate(both, turns[k], -1.0).astype(BF)
    arrived([q_far])
    t_head = group(cot.at[pl.ds(0, 2), head_part])
    for k in range(2):
        remote(cot.at[2 * k + c, head_part], cot.at[2 * k + c, head_part], sib, t_head)
    arrived([t_tail])
    last_terms(tail_part, 0, 6)
    leaving.append(stay(oq.at[tail_part], oq_out.at[tail_part]))

    first_terms(head_part)

    arrived([t_head])
    for k in range(2):
        last_terms(head_part, k * 3, k * 3 + 3)
        cols = pl.ds(k * SHARE // 2, SHARE // 2)
        leaving.append(stay(oq.at[head_part, cols], oq_out.at[head_part, cols]))
    result(1)
    for copy in leaving:
        copy.wait()

    for copy in sent:
        copy.wait_send()


def widen(product_in, out_in, product, out, narrow, narrow_out, wide, wide_out, loads, stores):
    pieces = [pl.ds(k * SHARE // 6, SHARE // 6) for k in range(6)]
    parts = [(product_in.at[:, at], narrow.at[k], wide.at[k], product.at[:, at]) for k, at in enumerate(pieces)]
    parts.append((out_in, narrow_out, wide_out, out))
    arrive = [pltpu.make_async_copy(part[0], part[1], loads.at[k]) for k, part in enumerate(parts)]
    leave = [pltpu.make_async_copy(part[2], part[3], stores.at[k]) for k, part in enumerate(parts)]
    for copy in arrive:
        copy.start()
    for k, part in enumerate(parts):
        arrive[k].wait()
        part[2][...] = part[1][...].astype(F32)
        leave[k].start()
    for copy in leave:
        copy.wait()


def tables():
    rate = 10000.0 ** (-2.0 * np.arange(ROT // 2) / ROT)
    rate = np.concatenate([rate, rate])[:, None]
    within = np.arange(TOK)[None, :] * rate
    blocks = np.arange(4)[:, None, None] * float(TOK) * rate[None] + np.zeros((1, 1, TOK))
    tab_t = np.stack([np.cos(within), np.sin(within)]).astype(np.float32)
    tab_b = np.stack([np.cos(blocks), np.sin(blocks)], axis=1).astype(np.float32)
    return tab_t, tab_b


def per_device(tokens, target, norm_gain, qkv_weight, out_weight, probe_seed, block_order):
    tab_t, tab_b = tables()
    anywhere = pl.BlockSpec(memory_space=pl.ANY)
    v = pltpu.VMEM
    scratch = [
        pltpu.SMEM((1,), jnp.int32), pltpu.SMEM((1,), jnp.int32),
        v((COLS, SHARE), BF), v((HS, SHARE), BF), v((1, D), F32), v((2, ROT, TOK), F32), v((4, 2, ROT, TOK), F32),
        v((TOK, D), BF), v((TOK, PART), BF), v((COLS, D), BF), v((TOK, D), BF), v((2, COLS, TOK), F32),
        v((3, TOK, 128), F32), v((16, D), BF), v((4, TOK, SHARE), BF), v((4, 4 * HS + 16, TOK), BF),
        v((4, 4, HALF, PART), BF), v((2, 4, 4, HALF, PART), BF), v((2, 4, 4, HALF, PART), BF),
        v((2, 2 * PART, 16 * HALF), BF),
        v((2, 4, 4, HALF, 2 * SPAN), BF), v((2, 4, 4, HALF, 2 * SPAN), BF),
        v((2, 2 * SPAN, 2 * HS), BF), v((2, HS, 2 * SPAN), BF), v((2, 2 * SPAN, 2 * HS), BF),
        v((2, 2 * SPAN, 1024), F32), v((TOK, 1024), F32), v((TOK, 1024), F32),
        v((2, 2 * SPAN, 1024), BF), v((2, 2 * SPAN, 1024), BF),
        v((4, HS, TOK), F32), v((4, HS, TOK), F32),
        v((2, PART, 2 * SPAN), F32), v((2, PART, 2 * SPAN), BF), v((2, PART, 2 * SPAN), BF),
        v((2, 2, 16 * HALF, SPAN), F32), v((2, PART, 2 * SPAN), BF), v((PART, TOK), F32),
        v((2, 2, 4, 4, HALF, 2 * SPAN), BF),
        v((2, 3, 4, HALF, 2 * SPAN), BF), v((2, 3, 4, HALF, 2 * SPAN), BF),
        v((2, 4, HALF, 2 * SPAN), BF), v((2, 4, HALF, 2 * SPAN), BF),
        v((2, 3, HALF, 2 * SPAN), BF), v((2, 3, HALF, 2 * SPAN), BF),
        v((4, 4, HALF, PART), BF), v((4, 4, HALF, PART), BF),
        v((2, 4, HALF, PART), BF), v((2, 4, HALF, PART), BF),
        v((4, HALF, PART), BF), v((4, HALF, PART), BF), v((4, HALF, PART), BF), v((4, HALF, PART), BF),
        v((4, HALF, PART), BF), v((4, HALF, PART), BF), v((4, HALF, PART), BF), v((4, HALF, PART), BF),
        v((4, HS, TOK), BF), v((2, HS, TOK), BF), v((2, HS, TOK), BF), v((2, HS, TOK), BF),
        v((4, HS, TOK), BF), v((2, HS, TOK), BF), v((2, HS, TOK), BF), v((2, HS, TOK), BF),
        v((4, 3 * HS, TOK), BF), v((COLS, SHARE), F32), v((COLS, SHARE), F32), v((2, 16 * HALF, PART), F32),
        pltpu.SemaphoreType.DMA((N_REMOTE,)), pltpu.SemaphoreType.DMA((N_REMOTE,)),
        pltpu.SemaphoreType.DMA((N_LOCAL,)),
    ]
    product, out_curv = pl.pallas_call(
        kernel,
        out_shape=(
            jax.ShapeDtypeStruct((COLS, SHARE), BF),
            jax.ShapeDtypeStruct((HS, SHARE), BF),
        ),
        in_specs=[anywhere] * 9,
        out_specs=(anywhere, anywhere),
        scratch_shapes=scratch,
        compiler_params=pltpu.CompilerParams(
            collective_id=0, has_side_effects=True, vmem_limit_bytes=60 * 2**20
        ),
    )(
        tokens, target, norm_gain.reshape(1, D), qkv_weight.T, out_weight, probe_seed, block_order,
        jnp.asarray(tab_t), jnp.asarray(tab_b),
    )
    product, out_curv = pl.pallas_call(
        widen,
        out_shape=(
            jax.ShapeDtypeStruct((COLS, SHARE), F32),
            jax.ShapeDtypeStruct((HS, SHARE), F32),
        ),
        in_specs=[anywhere, anywhere],
        out_specs=(anywhere, anywhere),
        scratch_shapes=[
            v((6, COLS, SHARE // 6), BF), v((HS, SHARE), BF),
            v((6, COLS, SHARE // 6), F32), v((HS, SHARE), F32),
            pltpu.SemaphoreType.DMA((7,)), pltpu.SemaphoreType.DMA((7,)),
        ],
    )(product, out_curv)
    return product.T, out_curv


def solution(mesh):
    placed = (P("seq", None), P("seq", None), P(), P(None, "fsdp"), P("fsdp", None), P(), P("seq"))
    return jax.shard_map(
        per_device,
        mesh=mesh,
        in_specs=placed,
        out_specs=(P("seq", "fsdp"), P("fsdp", "seq")),
        check_vma=False,
    )
```
